32 devices in a mesh: dp: 8 (over z, y), tok: 4 (over x, core).
Axes of the slice: x: 2, y: 2, z: 4, core: 2. Of those that a mesh axis runs over, the one named last changes fastest.
Arguments:
- images: bfloat16 [196, 128, 768], P('tok', 'dp'), may hold values from -6 to 6
- partner: int32 [128], replicated, may hold values from 0 to 127, as said below
- lam: float32 [128], replicated, may hold values from 0.2 to 0.8
- labels: int32 [128], replicated, may hold values from 0 to 999
- counts: int32 [8, 2], replicated, may hold values from 1 to 8
- class_weights: float32 [1000], replicated, may hold values from 0.5 to 2
- stem_w: float32 [768, 768], P(None, 'dp'), may hold values from -0.21875 to 0.21875
- stem_m: float32 [768, 768], P(None, 'dp'), may hold values from -0.00015258789 to 0.00015258789
- stem_v: float32 [768, 768], P(None, 'dp'), may hold values from 2.5950322e-11 to 4.1520515e-10
- tok_w: float32 [2, 2, 196, 384], P(None, None, None, 'tok'), may hold values from -0.4375 to 0.4375
- tok_m: float32 [2, 2, 196, 384], P(None, None, None, 'tok'), may hold values from -0.00021362305 to 0.00021362305
- tok_v: float32 [2, 2, 196, 384], P(None, None, None, 'tok'), may hold values from 5.1900644e-11 to 8.304103e-10
- chan_w: float32 [2, 2, 768, 3072], P(None, None, 'dp'), may hold values from -0.21875 to 0.21875
- chan_m: float32 [2, 2, 768, 3072], P(None, None, 'dp'), may hold values from -0.00015258789 to 0.00015258789
- chan_v: float32 [2, 2, 768, 3072], P(None, None, 'dp'), may hold values from 2.5950322e-11 to 4.1520515e-10
- head_w: float32 [768, 1000], P('dp'), may hold values from -0.21875 to 0.21875
- head_m: float32 [768, 1000], P('dp'), may hold values from -0.0024414062 to 0.0024414062
- head_v: float32 [768, 1000], P('dp'), may hold values from 7.8125e-09 to 1.25e-07
- vec_w: float32 [11, 768], replicated, may hold values from -1 to 2.3
- vec_m: float32 [11, 768], replicated, may hold values from -0.00061035156 to 0.00061035156
- vec_v: float32 [11, 768], replicated, may hold values from 4.1520515e-10 to 6.6432824e-09
- hb_w: float32 [1000], replicated, may hold values from -1.75 to 1.75
- hb_m: float32 [1000], replicated, may hold values from -0.0024414062 to 0.0024414062
- hb_v: float32 [1000], replicated, may hold values from 7.8125e-09 to 1.25e-07
Outputs:
- stem_new: float32 [768, 768], P(None, 'dp')
- stem_m_new: float32 [768, 768], P(None, 'dp')
- stem_v_new: float32 [768, 768], P(None, 'dp')
- tok_new: float32 [2, 2, 196, 384], P(None, None, None, 'tok')
- tok_m_new: float32 [2, 2, 196, 384], P(None, None, None, 'tok')
- tok_v_new: float32 [2, 2, 196, 384], P(None, None, None, 'tok')
- chan_new: float32 [2, 2, 768, 3072], P(None, None, 'dp')
- chan_m_new: float32 [2, 2, 768, 3072], P(None, None, 'dp')
- chan_v_new: float32 [2, 2, 768, 3072], P(None, None, 'dp')
- head_new: float32 [768, 1000], P('dp')
- head_m_new: float32 [768, 1000], P('dp')
- head_v_new: float32 [768, 1000], P('dp')
- vec_new: float32 [11, 768], replicated
- vec_m_new: float32 [11, 768], replicated
- vec_v_new: float32 [11, 768], replicated
- hb_new: float32 [1000], replicated
- hb_m_new: float32 [1000], replicated
- hb_v_new: float32 [1000], replicated
- stem_low: bfloat16 [768, 768], P(None, 'dp')
- tok_low: bfloat16 [2, 2, 196, 384], P(None, None, None, 'tok')
- chan_low: bfloat16 [2, 2, 768, 3072], P(None, None, 'dp')
- head_low: bfloat16 [768, 1000], P('dp')
- norms: float32 [22, 2], replicated
- loss_parts: float32 [2], replicated
The draws below stay inside these ranges and needn't reach their ends.
Inputs may be any that keep to these rules, and one draw needn't show every extreme that they name: `partner`: with d = i // 16 the data index of image i and b = (i // 8) mod 2 its micro-batch, partner_i is an image of micro-batch b of data index (d + 8 / 2) mod 8, where 8 is the number of data indices; the partners of the 8 images of one micro-batch of one data index are all different.
All inputs are finite; a program needn't handle non-finite values.
Results may differ from the reference program's by a relative error of at most 0.023.
Values may be sent and summed in bfloat16 or wider, within the bound.
No kernel may reach another device: no remote copies, remote signals or barrier semaphores. Data moves between devices by JAX's collectives and lax.ppermute only.
A program may use at most 384 MiB of HBM per device.

```python
import math
import jax
import jax.numpy as jnp
from jax import lax

C = 768
DS = 384
DC = 3072
S = 196
P_SIZE = 768
K = 1000
LAYERS = 2
MB = 2
STEP = 5
IMG_MB = 8
IMAGES = 128
NV = 11
N_DP = 8


def draw_partner(key, part):
    key = jax.random.fold_in(key, 7)
    blocks = N_DP * MB
    keys = jax.random.split(key, blocks)
    orders = jax.vmap(lambda single: jax.random.permutation(single, IMG_MB))(keys)
    block_index = jnp.arange(blocks)
    source = (block_index // MB + N_DP // 2) % N_DP
    batch_index = block_index % MB
    base = source * (MB * IMG_MB) + batch_index * IMG_MB
    return (base[:, None] + orders).reshape(-1).astype(jnp.int32)


def draw_counts(key, part):
    key = jax.random.fold_in(key, 5)
    position = jnp.arange(N_DP)[:, None]
    base = IMG_MB * (N_DP - 1 + 2 * position) // (3 * (N_DP - 1))
    extra = jax.random.randint(key, (N_DP, MB), 0, 2)
    values = jnp.clip(base + extra, 1, IMG_MB)
    return values.at[N_DP - 1, 0].set(IMG_MB).astype(jnp.int32)


def draw_vec_w(key, part):
    key = jax.random.fold_in(key, 11)
    rows = jnp.arange(NV)[:, None]
    is_gain = (rows > 0) & ((rows - 1) % 2 == 0)
    position = jnp.arange(C)[None, :].astype(jnp.float32) / C
    ramp = 0.5 + position
    factor = jax.random.uniform(key, (NV, C), jnp.float32, 0.8, 1.25)
    noise = 0.3 * jax.random.truncated_normal(jax.random.fold_in(key, 2), -3.0, 3.0, (NV, C), jnp.float32)
    return jnp.where(is_gain, ramp * factor, noise)


def place_ends(entries, rng, low, high):
    longest = entries.shape.index(max(entries.shape))
    spots = []
    for shift in (0, 1):
        where = [jax.random.randint(jax.random.fold_in(rng, axis), (), 0, length) for axis, length in enumerate(entries.shape)]
        where[longest] = (where[longest] + shift) % entries.shape[longest]
        spots.append(tuple(where))
    return entries.at[spots[0]].set(low).at[spots[1]].set(high)


def block_levels(rng, dims, pieces, least, largest):
    def one(dim, blocks):
        steps = jax.random.uniform(jax.random.fold_in(jax.random.fold_in(rng, 6), dim), (blocks,), jnp.float32, least / len(pieces), largest / len(pieces))
        return jnp.repeat(jnp.exp(steps), dims[dim] // blocks).reshape((-1,) + (1,) * (len(dims) - dim - 1))

    loudness = one(*pieces[0])
    for cut in pieces[1:]:
        loudness = loudness * one(*cut)
    return loudness


def gaussian(rng, shape, scale, limit, pieces=(), held_as=jnp.bfloat16):
    drawn = scale * jax.random.normal(rng, shape, jnp.float32)
    if pieces:
        drawn = drawn * block_levels(rng, shape, pieces, -0.22, 0.18)
    return jnp.clip(drawn, -limit, limit).astype(held_as)


def setup_inputs(seed: int = 0) -> dict:
    key_of = jax.random.split(jax.random.key(seed), 25)
    return {
        "images": gaussian(key_of[0], (S, IMAGES, P_SIZE), 1.0, 6.0, ((0, 4), (1, 8))),
        "partner": draw_partner(jax.random.fold_in(key_of[24], 71), 0),
        "lam": jnp.clip(jax.random.uniform(key_of[2], (IMAGES,), jnp.float32, 0.2, 0.8), 0.2, 0.8),
        "labels": place_ends(jax.random.randint(key_of[3], (IMAGES,), 0, K), jax.random.fold_in(key_of[3], 1), 0, K - 1).astype(jnp.int32),
        "counts": draw_counts(jax.random.fold_in(key_of[24], 71), 0),
        "class_weights": jnp.clip(jnp.exp(jax.random.uniform(key_of[5], (K,), jnp.float32, math.log(0.5), math.log(2.0))), 0.5, 2.0),
        "stem_w": gaussian(key_of[6], (P_SIZE, C), P_SIZE ** -0.5, 0.21875, ((1, 8),), jnp.float32),
        "stem_m": gaussian(key_of[7], (P_SIZE, C), (0.11 * (IMAGES * S * C) ** -0.5), 0.00015258789, ((1, 8),), jnp.float32),
        "stem_v": jnp.clip(jnp.exp(math.log(4.1520514804105346e-10) - 2.7725887 * jax.random.uniform(key_of[8], (P_SIZE, C), jnp.float32) ** block_levels(key_of[8], (P_SIZE, C), ((1, 8),), -0.2, 0.2)), 2.595032175256584e-11, 4.1520514804105346e-10),
        "tok_w": gaussian(key_of[9], (LAYERS, 2, S, DS), S ** -0.5, 0.4375, ((3, 4),), jnp.float32),
        "tok_m": gaussian(key_of[10], (LAYERS, 2, S, DS), (0.11 * (IMAGES * S * DS) ** -0.5), 0.00021362305, ((3, 4),), jnp.float32),
        "tok_v": jnp.clip(jnp.exp(math.log(8.304102960821069e-10) - 2.7725887 * jax.random.uniform(key_of[11], (LAYERS, 2, S, DS), jnp.float32) ** block_levels(key_of[11], (LAYERS, 2, S, DS), ((3, 4),), -0.2, 0.2)), 5.190064350513168e-11, 8.304102960821069e-10),
        "chan_w": gaussian(key_of[12], (LAYERS, 2, C, DC), C ** -0.5, 0.21875, ((2, 8),), jnp.float32),
        "chan_m": gaussian(key_of[13], (LAYERS, 2, C, DC), (0.11 * (IMAGES * S * C) ** -0.5), 0.00015258789, ((2, 8),), jnp.float32),
        "chan_v": jnp.clip(jnp.exp(math.log(4.1520514804105346e-10) - 2.7725887 * jax.random.uniform(key_of[14], (LAYERS, 2, C, DC), jnp.float32) ** block_levels(key_of[14], (LAYERS, 2, C, DC), ((2, 8),), -0.2, 0.2)), 2.595032175256584e-11, 4.1520514804105346e-10),
        "head_w": gaussian(key_of[15], (C, K), C ** -0.5, 0.21875, ((0, 8),), jnp.float32),
        "head_m": gaussian(key_of[16], (C, K), (0.15 * (IMAGES * K) ** -0.5), 0.0024414062, ((0, 8),), jnp.float32),
        "head_v": jnp.clip(jnp.exp(math.log(1.2499999968440534e-07) - 2.7725887 * jax.random.uniform(key_of[17], (C, K), jnp.float32) ** block_levels(key_of[17], (C, K), ((0, 8),), -0.2, 0.2)), 7.812499980275334e-09, 1.2499999968440534e-07),
        "vec_w": draw_vec_w(jax.random.fold_in(key_of[24], 71), 0),
        "vec_m": gaussian(key_of[19], (NV, C), (0.44 * (IMAGES * S * C) ** -0.5), 0.00061035156, (), jnp.float32),
        "vec_v": jnp.clip(jnp.exp(jax.random.uniform(key_of[20], (NV, C), jnp.float32, math.log(4.1520514804105346e-10), math.log(6.643282368656855e-09))), 4.1520514804105346e-10, 6.643282368656855e-09),
        "hb_w": gaussian(key_of[21], (K,), 0.3, 1.75, (), jnp.float32),
        "hb_m": gaussian(key_of[22], (K,), (0.15 * (IMAGES * K) ** -0.5), 0.0024414062, (), jnp.float32),
        "hb_v": jnp.clip(jnp.exp(jax.random.uniform(key_of[23], (K,), jnp.float32, math.log(7.812499980275334e-09), math.log(1.2499999968440534e-07))), 7.812499980275334e-09, 1.2499999968440534e-07),
    }


@jax.custom_vjp
def low(v):
    return lax.optimization_barrier(v.astype(jnp.bfloat16)).astype(jnp.float32)

@jax.custom_vjp
def low_back(v):
    return v

def low_keep(v):
    return (low(v), None)

def low_pass(kept, grad):
    return (grad,)

def back_keep(v):
    return (v, None)

def back_low(kept, grad):
    return (low(grad),)
low.defvjp(low_keep, low_pass)
low_back.defvjp(back_keep, back_low)
highest = lax.Precision.HIGHEST
beta_one = 0.9
beta_two = 0.999
epsilon = 1e-06
weight_decay = 0.01
learn_rate = 0.3

def layer_norm(values, gain, shift):
    centre = values - lax.optimization_barrier(jnp.mean(values, -1, keepdims=True))
    spread = lax.optimization_barrier(jnp.mean(centre * centre, -1, keepdims=True))
    return centre * lax.rsqrt(spread + 1e-06) * gain + shift

def block_loss(params, mixed, targets, weights, total):
    stem, tokens, channel, head, vectors, head_bias = params
    stem_low = low(stem)
    token_low = low(tokens)
    channel_low = low(channel)
    head_low = low(head)
    state = low_back(jnp.einsum('sbp,pc->sbc', mixed, stem_low, precision=highest) + vectors[0])
    for layer in range(LAYERS):
        base = 1 + 4 * layer
        normed = low(layer_norm(state, vectors[base], vectors[base + 1]))
        before = low_back(jnp.einsum('sj,sbc->jbc', token_low[layer, 0], normed, precision=highest))
        hidden = low(jax.nn.gelu(before))
        state = state + low_back(jnp.einsum('sj,jbc->sbc', token_low[layer, 1], hidden, precision=highest))
        normed = low(layer_norm(state, vectors[base + 2], vectors[base + 3]))
        inner = low_back(jnp.einsum('sbc,cf->sbf', normed, channel_low[layer, 0], precision=highest))
        active = low(jax.nn.gelu(inner))
        state = state + low_back(jnp.einsum('sbf,cf->sbc', active, channel_low[layer, 1], precision=highest))
    pooled = low(lax.optimization_barrier(jnp.mean(layer_norm(state, vectors[NV - 2], vectors[NV - 1]), 0)))
    logits = jnp.dot(pooled, head_low, precision=highest) + head_bias
    losses = -lax.optimization_barrier(jnp.sum(targets * jax.nn.log_softmax(logits, -1), -1))
    raw = jnp.sum(weights * losses)
    return (raw / total, raw)

def lamb(weight, gradient, first, second, groups, decay_rate):
    first_new = beta_one * first + (1 - beta_one) * gradient
    second_new = beta_two * second + (1 - beta_two) * gradient * gradient
    update = first_new / (1 - beta_one ** STEP) / (jnp.sqrt(second_new / (1 - beta_two ** STEP)) + epsilon) + decay_rate * weight
    flat = update.reshape(groups, -1)
    weight_flat = weight.reshape(groups, -1)
    weight_norm = jnp.sqrt(lax.optimization_barrier(jnp.sum(weight_flat * weight_flat, 1)))
    update_norm = jnp.sqrt(lax.optimization_barrier(jnp.sum(flat * flat, 1)))
    trust = weight_norm / (update_norm + epsilon)
    fresh = weight - learn_rate * (trust[:, None] * flat).reshape(weight.shape)
    return (fresh, first_new, second_new, jnp.stack([weight_norm, update_norm], 1))

def reference(images, partner, lam, labels, counts, class_weights, stem_w, stem_m, stem_v, tok_w, tok_m, tok_v, chan_w, chan_m, chan_v, head_w, head_m, head_v, vec_w, vec_m, vec_v, hb_w, hb_m, hb_v):
    classes = jnp.arange(K, dtype=jnp.int32)
    own_hot = (labels[:, None] == classes[None, :]).astype(jnp.float32)
    other_hot = (labels[partner][:, None] == classes[None, :]).astype(jnp.float32)
    live = (jnp.arange(IMG_MB, dtype=jnp.int32)[None, :] < counts.reshape(-1)[:, None]).astype(jnp.float32).reshape(-1)
    mixing = lam[:, None]
    targets = mixing * own_hot + (1 - mixing) * other_hot
    weights = live * lax.optimization_barrier(jnp.sum(targets * class_weights[None, :], 1))
    total = jnp.sum(weights)
    params = (stem_w, tok_w, chan_w, head_w, vec_w, hb_w)

    def block_step(carry, block):
        sums, loss_sum = carry
        start = block * IMG_MB
        own = lax.dynamic_slice_in_dim(images, start, IMG_MB, 1).astype(jnp.float32)
        picks = lax.dynamic_slice_in_dim(partner, start, IMG_MB, 0)
        other = jnp.take(images, picks, axis=1).astype(jnp.float32)
        share = lax.dynamic_slice_in_dim(lam, start, IMG_MB, 0)[None, :, None]
        mixed = low(share * own + (1 - share) * other)
        target_block = lax.dynamic_slice_in_dim(targets, start, IMG_MB, 0)
        weight_block = lax.dynamic_slice_in_dim(weights, start, IMG_MB, 0)
        _, backward, raw = jax.vjp(lambda values: block_loss(values, mixed, target_block, weight_block, total), params, has_aux=True)
        gradients = backward(jnp.ones((), jnp.float32))[0]
        return ((jax.tree.map(jnp.add, sums, gradients), loss_sum + raw), None)
    zeros = jax.tree.map(jnp.zeros_like, params)
    (grads, loss_sum), _ = lax.scan(block_step, (zeros, jnp.zeros((), jnp.float32)), jnp.arange(N_DP * MB, dtype=jnp.int32))
    stem_up = lamb(stem_w, grads[0], stem_m, stem_v, 1, weight_decay)
    tok_up = lamb(tok_w, grads[1], tok_m, tok_v, 2 * LAYERS, weight_decay)
    chan_up = lamb(chan_w, grads[2], chan_m, chan_v, 2 * LAYERS, weight_decay)
    head_up = lamb(head_w, grads[3], head_m, head_v, 1, weight_decay)
    vec_up = lamb(vec_w, grads[4], vec_m, vec_v, NV, 0.0)
    hb_up = lamb(hb_w, grads[5], hb_m, hb_v, 1, 0.0)
    norms = jnp.concatenate([stem_up[3], tok_up[3], chan_up[3], head_up[3], vec_up[3], hb_up[3]], 0)
    loss_parts = jnp.stack([loss_sum, total])
    return (stem_up[0], stem_up[1], stem_up[2], tok_up[0], tok_up[1], tok_up[2], chan_up[0], chan_up[1], chan_up[2], head_up[0], head_up[1], head_up[2], vec_up[0], vec_up[1], vec_up[2], hb_up[0], hb_up[1], hb_up[2], stem_up[0].astype(jnp.bfloat16), tok_up[0].astype(jnp.bfloat16), chan_up[0].astype(jnp.bfloat16), head_up[0].astype(jnp.bfloat16), norms, loss_parts)
```

```python
import jax
import jax.numpy as jnp
from jax import lax
from jax.sharding import PartitionSpec as P

LAYERS = 2
STEP = 5
IMG_MB = 8
NV = 11
LANES = 128

highest = lax.Precision.HIGHEST
low = jnp.bfloat16
beta_one = 0.9
beta_two = 0.999
epsilon = 1e-06
weight_decay = 0.01
learn_rate = 0.3


def swap(array, axis, mask):
    count = lax.axis_size(axis)
    return lax.ppermute(array, axis, [(i, i ^ mask) for i in range(count)])


def dp_masks():
    masks = []
    mask = lax.axis_size("dp") // 2
    while mask > 1:
        masks.append(mask)
        mask //= 2
    return masks


def row_order():
    order = [0]
    for mask in dp_masks() + [1]:
        order = order + [r ^ mask for r in order]
    return order


def spread(piece, tok_first):
    for mask in dp_masks():
        piece = jnp.concatenate([piece, swap(piece, "dp", mask)], 0)
    if tok_first:
        second = swap(piece, "tok", 2)
        low_row, low_second = swap(piece, "dp", 1), swap(second, "dp", 1)
    else:
        low_row = swap(piece, "dp", 1)
        second, low_second = swap(piece, "tok", 2), swap(low_row, "tok", 2)
    near = [[piece, second], [low_row, low_second]]
    return [row + [swap(block, "tok", 1) for block in row] for row in near]


def joined(blocks):
    return jnp.concatenate([jnp.concatenate(row, 1) for row in blocks], 0)


def halves(array, axis):
    middle = array.shape[axis] // 2
    return (
        lax.slice_in_dim(array, 0, middle, axis=axis),
        lax.slice_in_dim(array, middle, 2 * middle, axis=axis),
    )


def fold(array, dimension, axis, mask):
    keep, send = halves(array, dimension)
    return keep.astype(jnp.float32) + swap(send.astype(low), axis, mask).astype(jnp.float32)


def collect(grad, tok_first):
    grad = fold(grad, 1, "tok", 1)
    if tok_first:
        grad = fold(fold(grad, 0, "dp", 1), 1, "tok", 2)
    else:
        grad = fold(fold(grad, 1, "tok", 2), 0, "dp", 1)
    for mask in reversed(dp_masks()):
        grad = fold(grad, 0, "dp", mask)
    own = grad.astype(low)
    far = swap(own, "tok", 2)
    return jnp.concatenate([own, far, swap(own, "tok", 1), swap(far, "tok", 1)], 1)


def ordered(array, axis, bits):
    row = lax.axis_index("tok")
    blocks = jnp.split(array, 4, axis)
    rel = [blocks[0], blocks[2], blocks[1], blocks[3]] if bits else blocks
    rel = [jnp.where((row & 1) == 1, rel[k ^ 1], rel[k]) for k in range(4)]
    rel = [jnp.where((row & 2) == 2, rel[k ^ 2], rel[k]) for k in range(4)]
    return jnp.concatenate(rel, axis)


def relative(array, axis):
    row = lax.axis_index("tok")
    rel = jnp.split(array, 4, axis)
    rel = [jnp.where((row & 1) == 1, rel[k ^ 1], rel[k]) for k in range(4)]
    rel = [jnp.where((row & 2) == 2, rel[k ^ 2], rel[k]) for k in range(4)]
    return jnp.concatenate([rel[0], rel[2], rel[1], rel[3]], axis)


def quarter(array, axis):
    size = array.shape[axis] // lax.axis_size("tok")
    return lax.dynamic_slice_in_dim(array, lax.axis_index("tok") * size, size, axis)


def layer_norm(values, gain, shift):
    centre = values - jnp.mean(values, -1, keepdims=True)
    spread_of = jnp.mean(centre * centre, -1, keepdims=True)
    return centre * lax.rsqrt(spread_of + 1e-06) * gain + shift


def gelu_back(inputs, upstream):
    return jax.vjp(jax.nn.gelu, inputs)[1](upstream)[0]


def moments(weight, gradient, first, second, decay_rate):
    first_new = beta_one * first + (1 - beta_one) * gradient
    second_new = beta_two * second + (1 - beta_two) * gradient * gradient
    update = (
        first_new / (1 - beta_one**STEP) / (jnp.sqrt(second_new / (1 - beta_two**STEP)) + epsilon)
        + decay_rate * weight
    )
    return (first_new, second_new, update)


def row_squares(array, groups):
    flat = array.reshape(groups, -1)
    return jnp.sum(flat * flat, 1)


def renew(weight, update, weight_norm, update_norm, groups):
    trust = weight_norm / (update_norm + epsilon)
    return weight - learn_rate * (trust[:, None] * update.reshape(groups, -1)).reshape(weight.shape)


def layer_forward(state, token_in, token_out, channel_in, channel_out, gains):
    normed_one = layer_norm(state, gains[0], gains[1]).astype(low)
    before = jnp.einsum("sj,bsc->bjc", token_in, normed_one, preferred_element_type=jnp.float32)
    hidden = jax.nn.gelu(before).astype(low)
    middle = state + jnp.einsum("sj,bjc->bsc", token_out, hidden, preferred_element_type=jnp.float32)
    normed_two = layer_norm(middle, gains[2], gains[3]).astype(low)
    inner = jnp.einsum("bsc,cf->bsf", normed_two, channel_in, preferred_element_type=jnp.float32)
    active = jax.nn.gelu(inner).astype(low)
    result = middle + jnp.einsum("bsf,cf->bsc", active, channel_out, preferred_element_type=jnp.float32)
    return (result, (state, normed_one, before, hidden, middle, normed_two, inner, active))


def layer_backward(gradient, saved, token_in, token_out, channel_in, channel_out, gains):
    state, normed_one, before, hidden, middle, normed_two, inner, active = saved
    grad_out = gradient.astype(low)
    grad_channel_out = jnp.einsum("bsf,bsc->cf", active, grad_out, preferred_element_type=jnp.float32)
    grad_active = jnp.einsum("bsc,cf->bsf", grad_out, channel_out, preferred_element_type=jnp.float32)
    grad_inner = gelu_back(inner, grad_active).astype(low)
    grad_channel_in = jnp.einsum("bsc,bsf->cf", normed_two, grad_inner, preferred_element_type=jnp.float32)
    grad_normed_two = jnp.einsum("bsf,cf->bsc", grad_inner, channel_in, preferred_element_type=jnp.float32)
    second_back = jax.vjp(layer_norm, middle, gains[2], gains[3])[1]
    grad_middle_norm, grad_gain_two, grad_shift_two = second_back(grad_normed_two)
    grad_middle = gradient + grad_middle_norm
    grad_token = grad_middle.astype(low)
    hidden_sum = jnp.einsum("sj,bsc->bjc", token_out, grad_token, preferred_element_type=jnp.float32)
    grad_token_out = jnp.einsum("bsc,bjc->sj", grad_token, hidden, preferred_element_type=jnp.float32)
    grad_before = gelu_back(before, hidden_sum).astype(low)
    grad_token_in = jnp.einsum("bsc,bjc->sj", normed_one, grad_before, preferred_element_type=jnp.float32)
    grad_normed_one = jnp.einsum("sj,bjc->bsc", token_in, grad_before, preferred_element_type=jnp.float32)
    first_back = jax.vjp(layer_norm, state, gains[0], gains[1])[1]
    grad_state_norm, grad_gain_one, grad_shift_one = first_back(grad_normed_one)
    token_grads = jnp.stack([grad_token_in, grad_token_out])
    vector_grads = jnp.stack([grad_gain_one, grad_shift_one, grad_gain_two, grad_shift_two])
    return (grad_middle + grad_state_norm, token_grads, grad_channel_in, grad_channel_out, vector_grads)


def body(
    images,
    partner,
    lam,
    labels,
    counts,
    class_weights,
    stem_w,
    stem_m,
    stem_v,
    tok_w,
    tok_m,
    tok_v,
    chan_w,
    chan_m,
    chan_v,
    head_w,
    head_m,
    head_v,
    vec_w,
    vec_m,
    vec_v,
    hb_w,
    hb_m,
    hb_v,
):
    count_dp = lax.axis_size("dp")
    count_tok = lax.axis_size("tok")
    device_row = lax.axis_index("dp")
    token_row = lax.axis_index("tok")
    patches = images.shape[0]
    all_patches = patches * count_tok
    per_device = images.shape[1]
    per_tok = per_device // count_tok
    classes_all = hb_w.shape[0]
    class_pad = -classes_all % (count_tok * LANES)
    width = vec_w.shape[1]

    incoming = swap(images, "dp", count_dp // 2)
    stem_piece = quarter(stem_w.astype(low).T, 1)
    stem_blocks = spread(stem_piece, False)
    chan_low = quarter(chan_w.astype(low), 3)
    chan_blocks = [
        [spread(chan_low[layer, way], way == 1) for way in range(2)] for layer in range(LAYERS)
    ]
    head_piece = quarter(jnp.pad(head_w.astype(low), ((0, 0), (0, class_pad))), 1)
    head_blocks = spread(head_piece, True)
    tok_low = tok_w.astype(low)
    tok_far = swap(tok_low, "tok", 2)
    tok_all = jnp.concatenate([tok_low, tok_far, swap(tok_low, "tok", 1), swap(tok_far, "tok", 1)], 3)

    start = device_row * per_device
    picks = lax.dynamic_slice_in_dim(partner, start, per_device, 0)
    share = lax.dynamic_slice_in_dim(lam, start, per_device, 0)
    place = picks % per_device
    pick = (place[:, None] == jnp.arange(per_device, dtype=jnp.int32)[None, :]).astype(low)
    other = jnp.einsum("kx,sxp->ksp", pick, incoming, preferred_element_type=jnp.float32)
    own = jnp.swapaxes(images, 0, 1).astype(jnp.float32)
    mixed_all = (share[:, None, None] * own + (1 - share)[:, None, None] * other).astype(low)
    groups = mixed_all.reshape(count_tok, per_tok, patches, -1)
    shares = [
        lax.dynamic_index_in_dim(groups, token_row ^ q, 0, keepdims=False) for q in range(count_tok)
    ]
    arrived = [shares[0]] + [swap(shares[q], "tok", q) for q in range(1, count_tok)]
    mixed = jnp.concatenate(arrived, 1)
    mixed = ordered(mixed, 1, False)

    order = row_order()
    rows = jnp.asarray(order, jnp.int32) ^ device_row
    vectors = vec_w.reshape(NV, count_dp, -1)[:, rows].reshape(NV, width)
    stem_all = ordered(joined(stem_blocks), 1, True)
    chan_all = [[joined(blocks) for blocks in pair] for pair in chan_blocks]
    head_all = joined(head_blocks)
    token_low = tok_all

    padded = classes_all + class_pad
    numbers = relative(jnp.arange(padded, dtype=jnp.int32), 0)
    bias = relative(jnp.pad(hb_w, (0, class_pad)), 0)
    own_hot = (labels[:, None] == jnp.arange(classes_all, dtype=jnp.int32)[None, :]).astype(jnp.float32)
    other_labels = jnp.take(labels, partner)
    own_weight = jnp.sum(own_hot * class_weights[None, :], 1)
    other_weight = jnp.take(own_weight, partner)
    live = (
        (jnp.arange(IMG_MB, dtype=jnp.int32)[None, :] < counts.reshape(-1)[:, None])
        .astype(jnp.float32)
        .reshape(-1)
    )
    weights = live * (lam * own_weight + (1 - lam) * other_weight)
    total = jnp.sum(weights)
    first_row = start + token_row * per_tok
    row_of = lambda array: lax.dynamic_slice_in_dim(array, first_row, per_tok, 0)
    lam_rows = row_of(lam)[:, None]
    targets = lam_rows * (row_of(labels)[:, None] == numbers[None, :]).astype(jnp.float32) + (
        1 - lam_rows
    ) * (row_of(other_labels)[:, None] == numbers[None, :]).astype(jnp.float32)
    weight_rows = row_of(weights)

    state = jnp.einsum("bsp,cp->bsc", mixed, stem_all, preferred_element_type=jnp.float32) + vectors[0]
    saved_layers = []
    for layer in range(LAYERS):
        state, saved = layer_forward(
            state,
            token_low[layer, 0],
            token_low[layer, 1],
            chan_all[layer][0],
            chan_all[layer][1],
            vectors[1 + 4 * layer : 5 + 4 * layer],
        )
        saved_layers.append(saved)
    final, final_back = jax.vjp(layer_norm, state, vectors[NV - 2], vectors[NV - 1])
    pooled_low = (jnp.sum(final, 1) / all_patches).astype(low)
    logits = jnp.dot(pooled_low, head_all, preferred_element_type=jnp.float32) + bias
    logits = jnp.where(numbers[None, :] < classes_all, logits, -jnp.inf)
    peak = jnp.max(logits, -1, keepdims=True)
    powers = jnp.exp(logits - peak)
    mass = jnp.sum(powers, -1, keepdims=True)
    log_probs = jnp.where(numbers[None, :] < classes_all, logits - peak - jnp.log(mass), 0.0)
    loss_local = jnp.sum(weight_rows * -jnp.sum(targets * log_probs, -1))
    grad_logits = (weight_rows / total)[:, None] * (
        powers / mass * jnp.sum(targets, -1, keepdims=True) - targets
    )
    head_grad = jnp.dot(pooled_low.astype(jnp.float32).T, grad_logits, precision=highest)
    grad_pooled = jnp.dot(grad_logits, head_all.astype(jnp.float32).T, precision=highest) / all_patches
    head_sum = collect(head_grad, True)
    grad_state, grad_gain_last, grad_shift_last = final_back(
        jnp.broadcast_to(grad_pooled[:, None], final.shape)
    )
    token_list = [None] * LAYERS
    channel_list = [None] * LAYERS
    vector_list = [None] * LAYERS
    for layer in reversed(range(LAYERS)):
        grad_state, token_list[layer], grad_in, grad_out, vector_list[layer] = layer_backward(
            grad_state,
            saved_layers[layer],
            token_low[layer, 0],
            token_low[layer, 1],
            chan_all[layer][0],
            chan_all[layer][1],
            vectors[1 + 4 * layer : 5 + 4 * layer],
        )
        channel_list[layer] = jnp.stack([collect(grad_in, False), collect(grad_out, True)])
    grad_low = grad_state.astype(low)
    stem_grad = jnp.einsum("bsc,bsp->cp", grad_low, mixed, preferred_element_type=jnp.float32)
    stem_bias = jnp.sum(grad_low.astype(jnp.float32), (0, 1))
    stem_sum = ordered(collect(relative(stem_grad, 1), False), 1, True).astype(jnp.float32).T
    vector_part = jnp.concatenate(
        [stem_bias[None]] + vector_list + [grad_gain_last[None], grad_shift_last[None]], 0
    )
    back_rows = jnp.argsort(rows)
    vector_part = vector_part.reshape(NV, count_dp, -1)[:, back_rows].reshape(NV, width)
    bias_part = ordered(jnp.sum(grad_logits, 0), 0, True)[:classes_all]
    token_part = fold(fold(jnp.stack(token_list), 3, "tok", 1), 3, "tok", 2)
    token_grad = lax.psum(token_part, "dp")
    vector_grad, bias_grad, loss_total = lax.psum((vector_part, bias_part, loss_local), ("dp", "tok"))
    chan_grad = ordered(jnp.stack(channel_list), 3, True).astype(jnp.float32)
    head_grad = ordered(head_sum, 1, True)[:, :classes_all].astype(jnp.float32)
    stem_grad = stem_sum
    stem_first, stem_second, stem_update = moments(stem_w, stem_grad, stem_m, stem_v, weight_decay)
    tok_first, tok_second, tok_update = moments(tok_w, token_grad, tok_m, tok_v, weight_decay)
    chan_first, chan_second, chan_update = moments(chan_w, chan_grad, chan_m, chan_v, weight_decay)
    head_first, head_second, head_update = moments(head_w, head_grad, head_m, head_v, weight_decay)
    vec_first, vec_second, vec_update = moments(vec_w, vector_grad, vec_m, vec_v, 0.0)
    hb_first, hb_second, hb_update = moments(hb_w, bias_grad, hb_m, hb_v, 0.0)
    matrix_groups = 2 * LAYERS
    weight_squares = jnp.concatenate(
        [
            row_squares(stem_w, 1) / count_tok,
            row_squares(tok_w, matrix_groups) / count_dp,
            row_squares(chan_w, matrix_groups) / count_tok,
            row_squares(head_w, 1) / count_tok,
        ]
    )
    update_squares = jnp.concatenate(
        [
            row_squares(stem_update, 1) / count_tok,
            row_squares(tok_update, matrix_groups) / count_dp,
            row_squares(chan_update, matrix_groups) / count_tok,
            row_squares(head_update, 1) / count_tok,
        ]
    )
    weight_total, update_total = lax.psum((weight_squares, update_squares), ("dp", "tok"))
    weight_norms = jnp.sqrt(weight_total)
    update_norms = jnp.sqrt(update_total)
    stem_end = 1
    tok_end = 1 + matrix_groups
    chan_end = 1 + 2 * matrix_groups
    stem_new = renew(stem_w, stem_update, weight_norms[0:stem_end], update_norms[0:stem_end], 1)
    tok_new = renew(
        tok_w,
        tok_update,
        weight_norms[stem_end:tok_end],
        update_norms[stem_end:tok_end],
        matrix_groups,
    )
    chan_new = renew(
        chan_w,
        chan_update,
        weight_norms[tok_end:chan_end],
        update_norms[tok_end:chan_end],
        matrix_groups,
    )
    head_new = renew(head_w, head_update, weight_norms[chan_end:], update_norms[chan_end:], 1)
    vec_weight_norm = jnp.sqrt(row_squares(vec_w, NV))
    vec_update_norm = jnp.sqrt(row_squares(vec_update, NV))
    hb_weight_norm = jnp.sqrt(row_squares(hb_w, 1))
    hb_update_norm = jnp.sqrt(row_squares(hb_update, 1))
    vec_new = renew(vec_w, vec_update, vec_weight_norm, vec_update_norm, NV)
    hb_new = renew(hb_w, hb_update, hb_weight_norm, hb_update_norm, 1)
    norms = jnp.stack(
        [
            jnp.concatenate([weight_norms, vec_weight_norm, hb_weight_norm]),
            jnp.concatenate([update_norms, vec_update_norm, hb_update_norm]),
        ],
        1,
    )
    loss_parts = jnp.stack([loss_total, total])
    return (
        stem_new,
        stem_first,
        stem_second,
        tok_new,
        tok_first,
        tok_second,
        chan_new,
        chan_first,
        chan_second,
        head_new,
        head_first,
        head_second,
        vec_new,
        vec_first,
        vec_second,
        hb_new,
        hb_first,
        hb_second,
        stem_new.astype(jnp.bfloat16),
        tok_new.astype(jnp.bfloat16),
        chan_new.astype(jnp.bfloat16),
        head_new.astype(jnp.bfloat16),
        norms,
        loss_parts,
    )


def solution(mesh):
    in_specs = (
        P("tok", "dp", None),
        P(),
        P(),
        P(),
        P(),
        P(),
        P(None, "dp"),
        P(None, "dp"),
        P(None, "dp"),
        P(None, None, None, "tok"),
        P(None, None, None, "tok"),
        P(None, None, None, "tok"),
        P(None, None, "dp", None),
        P(None, None, "dp", None),
        P(None, None, "dp", None),
        P("dp", None),
        P("dp", None),
        P("dp", None),
        P(),
        P(),
        P(),
        P(),
        P(),
        P(),
    )
    out_specs = (
        P(None, "dp"),
        P(None, "dp"),
        P(None, "dp"),
        P(None, None, None, "tok"),
        P(None, None, None, "tok"),
        P(None, None, None, "tok"),
        P(None, None, "dp", None),
        P(None, None, "dp", None),
        P(None, None, "dp", None),
        P("dp", None),
        P("dp", None),
        P("dp", None),
        P(),
        P(),
        P(),
        P(),
        P(),
        P(),
        P(None, "dp"),
        P(None, None, None, "tok"),
        P(None, None, "dp", None),
        P("dp", None),
        P(),
        P(),
    )
    return jax.shard_map(body, mesh=mesh, in_specs=in_specs, out_specs=out_specs, check_vma=False)
```

```python
import functools

import jax
import jax.numpy as jnp
from jax import lax
from jax.experimental import pallas as pl
from jax.experimental.pallas import tpu as pltpu
from jax.sharding import PartitionSpec as P

LAYERS = 2
STEP = 5
IMG_MB = 8
NV = 11
LANES = 128
SUBLANES = 8
FOLD_MAX = 1200000

low = jnp.bfloat16
beta_one = 0.9
beta_two = 0.999
epsilon = 1e-06
weight_decay = 0.01
learn_rate = 0.3
root = 0.7978845608028654
cubic = 0.044715
room = pltpu.CompilerParams(vmem_limit_bytes=44 * 1024 * 1024)
places = (0, 2, 1, 3)


def dot(left, right, contract=(1, 0)):
    return lax.dot_general(
        left, right, (((contract[0],), (contract[1],)), ((), ())), preferred_element_type=jnp.float32
    )


def gelu(values):
    return 0.5 * values * (1 + jnp.tanh(root * values * (1 + cubic * values * values)))


def gelu_both(values):
    square = values * values
    bend = jnp.tanh(root * values * (1 + cubic * square))
    half = 0.5 * (1 + bend)
    slope = half + 0.5 * values * (1 - bend * bend) * (root * (1 + 3 * cubic * square))
    return values * half, slope


def centred(values):
    centre = values - jnp.mean(values, -1, keepdims=True)
    inverse = lax.rsqrt(jnp.mean(centre * centre, -1, keepdims=True) + 1e-06)
    return centre * inverse, inverse


def centred_back(scaled, hat, inverse):
    return inverse * (
        scaled - jnp.mean(scaled, -1, keepdims=True) - hat * jnp.mean(scaled * hat, -1, keepdims=True)
    )


def whole(array):
    zeros = (0,) * array.ndim
    return pl.BlockSpec(array.shape, lambda *_: zeros)


def cost(flops, bytes_accessed, powers=0):
    return pl.CostEstimate(flops=flops, bytes_accessed=bytes_accessed, transcendentals=powers)


def token_forward_kernel(state, gains, token_in, token_out, middle, before):
    hat, _ = centred(state[...])
    normed = (hat * gains[0:1] + gains[1:2]).astype(low)
    pre = dot(token_in[...], normed)
    before[0] = pre.astype(low)
    middle[...] = state[...] + dot(token_out[...], gelu(pre).astype(low))


def token_forward(state, gains, token_in, token_out):
    hidden, rows = token_in.shape
    count, width = state.shape[0] // rows, state.shape[1]
    one = pl.BlockSpec((rows, width), lambda i: (i, 0))
    return pl.pallas_call(
        token_forward_kernel,
        grid=(count,),
        in_specs=[one, whole(gains), whole(token_in), whole(token_out)],
        out_specs=[one, pl.BlockSpec((1, hidden, width), lambda i: (i, 0, 0))],
        out_shape=[
            jax.ShapeDtypeStruct(state.shape, jnp.float32),
            jax.ShapeDtypeStruct((count, hidden, width), low),
        ],
        compiler_params=room,
        cost_estimate=cost(4 * count * rows * hidden * width, 10 * state.size, 0),
        name="token_forward",
    )(state, gains, token_in, token_out)


def hbm(arrays):
    return [pl.BlockSpec(memory_space=pl.ANY)] * len(arrays)


scalars = pl.BlockSpec(memory_space=pltpu.SMEM)


class Pieces:
    def __init__(self, first, second):
        self.arrays = [*first, *second]
        self.specs = hbm(self.arrays)
        self.width = 2 * second[0].shape[1]
        self.size = second[0].shape[2]
        self.sems = 4

    def copies(self, refs, held_in, held_out, sems, slot, place):
        half = self.width // 2
        out = []
        for side in range(2):
            rows = pl.ds(side * half, half)
            first = refs[place].at[side, pl.ds(0, half)]
            second = refs[4 + place // 2 * 2 + side].at[place % 2]
            out.append(pltpu.make_async_copy(first, held_in.at[slot, rows], sems.at[slot, side]))
            out.append(pltpu.make_async_copy(second, held_out.at[slot, rows], sems.at[slot, 2 + side]))
        return out


class Gathered:
    def __init__(self, array, shards, device):
        self.arrays = [shards, device, array]
        self.specs = [scalars, scalars] + hbm([array])
        self.blocks, self.rows, self.size = array.shape[0], array.shape[2] // 2, array.shape[3]
        self.width = self.blocks * self.rows
        self.sems = 2 * self.blocks

    def copies(self, refs, held_in, held_out, sems, slot, place):
        shards, device, array = refs
        quarter_at = device[0] ^ places[place]
        out = []
        for block in range(self.blocks):
            rows = pl.ds(block * self.rows, self.rows)
            for way, held in enumerate((held_in, held_out)):
                out.append(
                    pltpu.make_async_copy(
                        array.at[shards[block], quarter_at, pl.ds(way * self.rows, self.rows)],
                        held.at[slot, rows],
                        sems.at[slot, 2 * block + way],
                    )
                )
        return out


def channel_forward_kernel(source, middle, gains, *rest):
    refs = rest[: len(source.arrays)]
    result, inner, normed, held_in, held_out, sems = rest[-6:]
    step = pl.program_id(0)

    @pl.when(step == 0)
    def _():
        for q in range(4):
            for copy in source.copies(refs, held_in, held_out, sems, q, q):
                copy.start()
        hat, _ = centred(middle[...])
        normed[...] = (hat * gains[2:3] + gains[3:4]).astype(low)
        result[...] = middle[...]

    for q in range(4):

        @pl.when(step == q)
        def _(q=q):
            for copy in source.copies(refs, held_in, held_out, sems, q, q):
                copy.wait()
            product = dot(normed[...], held_in[q])
            inner[...] = product.astype(low)
            result[...] += dot(gelu(product).astype(low), held_out[q], (1, 1))


def channel_forward(middle, gains, source):
    rows, width = middle.shape
    size = source.size
    total = 4 * size
    return pl.pallas_call(
        functools.partial(channel_forward_kernel, source),
        grid=(4,),
        in_specs=[whole(middle), whole(gains)] + source.specs,
        out_specs=[whole(middle), pl.BlockSpec((rows, size), lambda i: (0, i))],
        out_shape=[
            jax.ShapeDtypeStruct(middle.shape, jnp.float32),
            jax.ShapeDtypeStruct((rows, total), low),
        ],
        scratch_shapes=[
            pltpu.VMEM(middle.shape, low),
            pltpu.VMEM((4, width, size), low),
            pltpu.VMEM((4, width, size), low),
            pltpu.SemaphoreType.DMA((4, source.sems)),
        ],
        compiler_params=room,
        cost_estimate=cost(4 * rows * width * total, 4 * width * total + 2 * rows * total),
        name="channel_forward",
    )(middle, gains, *source.arrays)


def channel_backward_kernel(source, last, gradient, middle, gains, inner, *rest):
    if last:
        before, rest = rest[0], rest[1:]
    refs = rest[: len(source.arrays)]
    grads, total, grad_vectors, grad_low, grad_turn, normed_turn, held_in, held_out, sems = rest[-9:]
    step = pl.program_id(0)
    first = 0 if last else 2

    @pl.when(step == 0)
    def _():
        for q in range(2):
            for copy in source.copies(refs, held_in, held_out, sems, q, first + q):
                copy.start()
        grad_low[...] = gradient[...].astype(low)
        grad_turn[...] = gradient[...].T.astype(low)
        hat, _ = centred(middle[...])
        normed_turn[...] = (hat * gains[2:3] + gains[3:4]).T.astype(low)
        total[...] = before[...] if last else jnp.zeros_like(total)

    for q in range(2):

        @pl.when(step == q)
        def _(q=q):
            for copy in source.copies(refs, held_in, held_out, sems, q, first + q):
                copy.wait()
            active, slope = gelu_both(inner[...].astype(jnp.float32))
            grads[1, 0] = dot(grad_turn[...], active.astype(low)).astype(low)
            grad_inner = (slope * dot(grad_low[...], held_out[q])).astype(low)
            grads[0, 0] = dot(normed_turn[...], grad_inner).astype(low)
            total[...] += dot(grad_inner, held_in[q], (1, 1))

    if last:

        @pl.when(step == 1)
        def _():
            hat, inverse = centred(middle[...])
            upstream = total[...]
            grad_vectors[0:1] = jnp.sum(upstream * hat, 0, keepdims=True)
            grad_vectors[1:2] = jnp.sum(upstream, 0, keepdims=True)
            total[...] = gradient[...] + centred_back(upstream * gains[2:3], hat, inverse)


def channel_backward(gradient, middle, gains, inner, source, before=None):
    rows, width = middle.shape
    size = source.size
    last = before is not None
    shift = 0 if last else 2
    carried = [before] if last else []
    total = 2 * size
    return pl.pallas_call(
        functools.partial(channel_backward_kernel, source, last),
        grid=(2,),
        in_specs=[whole(middle), whole(middle), whole(gains), pl.BlockSpec((rows, size), lambda i: (0, i + shift))]
        + [whole(array) for array in carried]
        + source.specs,
        out_specs=[
            pl.BlockSpec((2, 1, width, size), lambda i: (0, i, 0, 0)),
            whole(middle),
            pl.BlockSpec((2, width), lambda i: (0, 0)),
        ],
        out_shape=[
            jax.ShapeDtypeStruct((2, 2, width, size), low),
            jax.ShapeDtypeStruct(middle.shape, jnp.float32),
            jax.ShapeDtypeStruct((2, width), jnp.float32),
        ],
        scratch_shapes=[
            pltpu.VMEM((rows, width), low),
            pltpu.VMEM((width, rows), low),
            pltpu.VMEM((width, rows), low),
            pltpu.VMEM((2, width, size), low),
            pltpu.VMEM((2, width, size), low),
            pltpu.SemaphoreType.DMA((2, source.sems)),
        ],
        compiler_params=room,
        cost_estimate=cost(8 * rows * width * total, 8 * width * total + 2 * rows * total),
        name="channel_backward",
    )(gradient, middle, gains, inner, *carried, *source.arrays)


def step_kernel(device, weight, mean, power, near, far, *rest):
    apart, (mean_new, power_new, update, sums) = rest[:4], rest[-4:]
    way = pl.program_id(0)
    size = near.shape[2]
    weight_part, update_part = 0.0, 0.0
    for a in range(4):
        rel = device[0] ^ a
        lanes = slice(a * size, (a + 1) * size)
        values = [
            jnp.where(way == 0, one.astype(jnp.float32), two[...].astype(jnp.float32))
            for one, two in zip((near[0], far[0], near[1], far[1]), apart, strict=True)
        ]
        grad = jnp.where(
            rel < 2, jnp.where(rel == 0, values[0], values[1]), jnp.where(rel == 2, values[2], values[3])
        )
        value = weight[0, 0, :, lanes]
        mean_next, power_next, change = moments(
            value, grad, mean[0, 0, :, lanes], power[0, 0, :, lanes], weight_decay
        )
        mean_new[0, 0, :, lanes] = mean_next
        power_new[0, 0, :, lanes] = power_next
        update[0, 0, :, lanes] = change
        weight_part += jnp.sum(value * value)
        update_part += jnp.sum(change * change)
    sums[way, 0] = weight_part
    sums[way, 1] = update_part


def channel_step(layer, device, weight, mean, power, chain_in, chain_out, earlier):
    near, far = chain_in
    rows = near.shape[1]
    columns = weight.shape[3]
    block = pl.BlockSpec((1, 1, rows, columns), lambda w: (layer, w, 0, 0))
    shape = jax.ShapeDtypeStruct(weight.shape, jnp.float32)
    return pl.pallas_call(
        step_kernel,
        grid=(2,),
        in_specs=[scalars, block, block, block]
        + [whole(array) for array in (near, far, *chain_out)]
        + hbm(earlier),
        out_specs=[block, block, block, scalars],
        out_shape=[shape, shape, shape, jax.ShapeDtypeStruct((2, 2), jnp.float32)],
        input_output_aliases={10 + i: i for i in range(len(earlier))},
        compiler_params=room,
        cost_estimate=cost(40 * near.size, 104 * near.size),
        name="channel_step",
    )(device, weight, mean, power, near, far, *chain_out, *earlier)


def renew_kernel(trust, weight, update, fresh, fresh_low):
    value = weight[...] - learn_rate * (trust[pl.program_id(0), pl.program_id(1)] * update[...])
    fresh[...] = value
    fresh_low[...] = value.astype(low)


def channel_renew(trust, weight, update):
    layers, ways, rows, columns = weight.shape
    block = pl.BlockSpec((1, 1, rows, columns), lambda i, j: (i, j, 0, 0))
    return pl.pallas_call(
        renew_kernel,
        grid=(layers, ways),
        in_specs=[pl.BlockSpec(memory_space=pltpu.SMEM), block, block],
        out_specs=[block, block],
        out_shape=[jax.ShapeDtypeStruct(weight.shape, jnp.float32), jax.ShapeDtypeStruct(weight.shape, low)],
        compiler_params=room,
        cost_estimate=cost(3 * weight.size, 14 * weight.size),
        name="channel_renew",
    )(trust, weight, update)


def token_backward_kernel(gradient, state, gains, before, token_in, token_out_turn, *rest):
    grad_state, grad_vectors, grad_in, grad_out = rest[-4:]
    step = pl.program_id(0)
    token_grad = gradient[...].astype(low)
    hat, inverse = centred(state[...])
    normed = (hat * gains[0:1] + gains[1:2]).astype(low)
    hidden, slope = gelu_both(before[0].astype(jnp.float32))
    grad_before = (slope * dot(token_out_turn[...], token_grad)).astype(low)
    part_out = dot(token_grad, hidden.astype(low), (1, 1))
    part_in = dot(normed, grad_before, (1, 1))
    upstream = dot(token_in[...], grad_before)
    grad_state[...] = gradient[...] + centred_back(upstream * gains[0:1], hat, inverse)
    part_gain = jnp.sum(upstream * hat, 0, keepdims=True)
    part_shift = jnp.sum(upstream, 0, keepdims=True)

    @pl.when(step == 0)
    def _():
        grad_out[...] = part_out
        grad_in[...] = part_in
        grad_vectors[0:1] = part_gain
        grad_vectors[1:2] = part_shift

    @pl.when(step > 0)
    def _():
        grad_out[...] += part_out
        grad_in[...] += part_in
        grad_vectors[0:1] += part_gain
        grad_vectors[1:2] += part_shift


def token_backward(gradient, state, gains, before, token_in, token_out_turn, after=()):
    rows, hidden = token_in.shape
    count, width = state.shape[0] // rows, state.shape[1]
    one = pl.BlockSpec((rows, width), lambda i: (i, 0))
    still = lambda shape: pl.BlockSpec(shape, lambda i: (0, 0))
    return pl.pallas_call(
        token_backward_kernel,
        grid=(count,),
        in_specs=[
            one, one, whole(gains), pl.BlockSpec((1, hidden, width), lambda i: (i, 0, 0)),
            whole(token_in), whole(token_out_turn),
        ] + [pl.BlockSpec(memory_space=pl.ANY)] * len(after),
        out_specs=[one, still((2, width)), still((rows, hidden)), still((rows, hidden))],
        out_shape=[
            jax.ShapeDtypeStruct(state.shape, jnp.float32),
            jax.ShapeDtypeStruct((2, width), jnp.float32),
            jax.ShapeDtypeStruct((rows, hidden), jnp.float32),
            jax.ShapeDtypeStruct((rows, hidden), jnp.float32),
        ],
        compiler_params=room,
        cost_estimate=cost(8 * count * rows * hidden * width, 16 * state.size, 0),
        name="token_backward",
    )(gradient, state, gains, before, token_in, token_out_turn, *after)


def mix_kernel(place, share, device, own, incoming, *rest):
    outs, (own_wide, incoming_wide, joint) = rest[:-3], rest[-3:]
    patches, images, width = own.shape
    group = images // len(outs)
    for at in range(0, width, LANES):
        lanes = slice(at, at + LANES)
        own_wide[...] = own[:, :, lanes].astype(jnp.float32).reshape(own_wide.shape)
        incoming_wide[...] = incoming[:, :, lanes].astype(jnp.float32).reshape(own_wide.shape)
        for q, out in enumerate(outs):
            for i in range(group):
                image = (device[0] ^ q) * group + i
                first = own_wide[pl.ds(image, patches, stride=images), :]
                second = incoming_wide[pl.ds(place[image], patches, stride=images), :]
                joint[i * patches : (i + 1) * patches, :] = (
                    share[image] * first + (1 - share[image]) * second
                )
            out[:, lanes] = joint[...].astype(low)


def mix(place, share, device, own, incoming, groups):
    patches, images, width = own.shape
    rows = images // groups * patches
    scalar = pl.BlockSpec(memory_space=pltpu.SMEM)
    return pl.pallas_call(
        mix_kernel,
        in_specs=[scalar, scalar, scalar, pl.BlockSpec(), pl.BlockSpec()],
        out_shape=[jax.ShapeDtypeStruct((rows, width), low)] * groups,
        scratch_shapes=[
            pltpu.VMEM((patches * images, LANES), jnp.float32),
            pltpu.VMEM((patches * images, LANES), jnp.float32),
            pltpu.VMEM((rows, LANES), jnp.float32),
        ],
        compiler_params=room,
        cost_estimate=cost(4 * own.size, 6 * own.size),
        name="mix",
    )(place, share, device, own, incoming)


def stem_kernel(device, *rest):
    pieces, (weights, gains, mixed, state, joint, spare) = rest[:-6], rest[-6:]
    count = len(pieces) // 2
    odd, upper = (device[0] & 1) == 1, (device[0] & 2) == 2
    patches = pieces[0].shape[0] // 2
    rows = joint.shape[0] // (2 * 2)
    joint[...] = jnp.zeros_like(joint)
    for side in range(2):
        arrived = [ref[...].astype(jnp.float32) for ref in pieces[side * count : (side + 1) * count]]
        arrived = [jnp.where(odd, arrived[k ^ 1], arrived[k]) for k in range(count)]
        for k in range(count):
            spare[...] = jnp.where(upper, arrived[k ^ 2], arrived[k])
            for i in range(2):
                at = (side * 2 + i) * rows + k * patches
                joint[at : at + patches, :] = spare[i * patches : (i + 1) * patches, :]
    mixed[...] = joint[...].astype(low)
    state[...] = dot(mixed[...], weights[...], (1, 1)) + gains[0:1]


def stem(device, pieces, weights, gains, rows, after=()):
    width, pixels = weights.shape
    scalar = pl.BlockSpec(memory_space=pltpu.SMEM)
    return pl.pallas_call(
        stem_kernel,
        in_specs=[scalar] + [pl.BlockSpec()] * (len(pieces) + 2),
        out_shape=[
            jax.ShapeDtypeStruct((rows, pixels), low),
            jax.ShapeDtypeStruct((rows, width), jnp.float32),
        ],
        scratch_shapes=[
            pltpu.VMEM((rows, pixels), jnp.float32),
            pltpu.VMEM(pieces[0].shape, jnp.float32),
        ],
        compiler_params=room,
        cost_estimate=cost(2 * rows * width * pixels, 12 * rows * width),
        name="stem",
    )(device, *pieces, weights, gains)


def head_kernel(
    patches, device, state, gains, head, bias, numbers, labels, others, lam, weight, scale,
    gradient, grad_vectors, grads, grad_bias, loss, pooled, upstream,
):
    rows, width = state.shape
    count = lam.shape[0]
    each = rows // count
    live = lax.broadcasted_iota(jnp.int32, (each, 1), 0) < patches
    hat, inverse = centred(state[...])
    pooled[...] = jnp.zeros_like(pooled)
    sums = []
    for i in range(count):
        sums.append(jnp.sum(jnp.where(live, hat[i * each : (i + 1) * each], 0.0), 0, keepdims=True))
        pooled[i : i + 1] = sums[i] / patches * gains[0:1] + gains[1:2]
    pooled_low = pooled[...].astype(low)
    logits = dot(pooled_low, head[...])[:count] + bias[...]
    logits = jnp.where(numbers[...] >= 0, logits, -jnp.inf)
    peak = jnp.max(logits, -1, keepdims=True)
    powers = jnp.exp(logits - peak)
    mass = jnp.sum(powers, -1, keepdims=True)
    targets = jnp.where(numbers[...] == labels[...], lam[...], 0.0) + jnp.where(
        numbers[...] == others[...], 1 - lam[...], 0.0
    )
    log_probs = jnp.where(numbers[...] >= 0, logits - peak - jnp.log(mass), 0.0)
    losses = -jnp.sum(targets * log_probs, -1, keepdims=True)
    loss[...] = jnp.sum(weight[...] * losses, 0, keepdims=True)
    grad_logits = scale[...] * (powers / mass * jnp.sum(targets, -1, keepdims=True) - targets)
    grad_bias[...] = jnp.sum(grad_logits, 0, keepdims=True)
    pad = jnp.zeros((pooled.shape[0] - count, grad_logits.shape[1]), jnp.float32)
    grad_logits = jnp.concatenate([grad_logits, pad], 0)
    main = grad_logits.astype(low)
    rest = (grad_logits - main.astype(jnp.float32)).astype(low)
    size = main.shape[1] // 4
    for a in range(4):
        lanes = slice(a * size, (a + 1) * size)
        part = dot(pooled_low, main[:, lanes], (0, 0)) + dot(pooled_low, rest[:, lanes], (0, 0))
        rel = device[0] ^ a
        grads[(rel & 1) * 2 + (rel >> 1)] = part.astype(low)
    spread_back = (dot(main, head[...], (1, 1)) + dot(rest, head[...], (1, 1))) / patches
    upstream[...] = jnp.zeros_like(upstream)
    grad_gain = jnp.zeros((1, width), jnp.float32)
    for i in range(count):
        one = spread_back[i : i + 1]
        grad_gain = grad_gain + one * sums[i]
        upstream[i * each : (i + 1) * each] = jnp.where(live, one, 0.0)
    grad_vectors[0:1] = grad_gain
    grad_vectors[1:2] = jnp.sum(spread_back[:count], 0, keepdims=True) * patches
    gradient[...] = centred_back(upstream[...] * gains[0:1], hat, inverse)


def head_step(device, state, gains, weights, bias, numbers, labels, others, lam, weight, scale, patches):
    rows, width = state.shape
    columns = weights.shape[1]
    return pl.pallas_call(
        functools.partial(head_kernel, patches),
        in_specs=[scalars] + [pl.BlockSpec()] * 10,
        out_shape=[
            jax.ShapeDtypeStruct(state.shape, jnp.float32),
            jax.ShapeDtypeStruct((2, width), jnp.float32),
            jax.ShapeDtypeStruct((4, width, columns // 4), low),
            jax.ShapeDtypeStruct((1, columns), jnp.float32),
            jax.ShapeDtypeStruct((1, 1), jnp.float32),
        ],
        scratch_shapes=[
            pltpu.VMEM((16, width), jnp.float32),
            pltpu.VMEM(state.shape, jnp.float32),
        ],
        compiler_params=room,
        cost_estimate=cost(64 * width * columns, 8 * rows * width),
        name="head_step",
    )(device, state, gains, weights, bias, numbers, labels, others, lam, weight, scale)


def stem_backward_kernel(device, gradient, mixed, grads, shift):
    rounded = gradient[...].astype(low)
    shift[...] = jnp.sum(rounded.astype(jnp.float32), 0, keepdims=True)
    whole_grad = dot(gradient[...].T.astype(low), mixed[...]).astype(low)
    size = whole_grad.shape[1] // 4
    for a in range(4):
        rel = device[0] ^ a
        grads[(rel & 1) * 2 + (rel >> 1)] = whole_grad[:, a * size : (a + 1) * size]


def stem_backward(device, gradient, mixed):
    width, pixels = gradient.shape[1], mixed.shape[1]
    return pl.pallas_call(
        stem_backward_kernel,
        in_specs=[scalars] + [pl.BlockSpec()] * 2,
        out_shape=[
            jax.ShapeDtypeStruct((4, width, pixels // 4), low),
            jax.ShapeDtypeStruct((1, width), jnp.float32),
        ],
        compiler_params=room,
        cost_estimate=cost(2 * gradient.size * pixels, 8 * gradient.size),
        name="stem_backward",
    )(device, gradient, mixed)


def moved(values, source, way):
    spots = (lax.broadcasted_iota(jnp.int32, (values.shape[1],) * 2, 0) == source).astype(low)
    main = values.astype(low)
    rest = values - main.astype(jnp.float32)
    middle = rest.astype(low)
    rest = (rest - middle.astype(jnp.float32)).astype(low)
    return sum(dot(part, spots, (1, way)) for part in (main, middle, rest))


def vectors_kernel(vectors, source, out):
    out[...] = moved(vectors[...], source[...], 0)


def relative_vectors(vectors, source):
    return pl.pallas_call(
        vectors_kernel,
        out_shape=jax.ShapeDtypeStruct(vectors.shape, jnp.float32),
        compiler_params=room,
        name="relative_vectors",
    )(vectors, source)


def gather_small_kernel(source, *rest):
    parts, (bias, loss, out, joint) = rest[:-4], rest[-4:]
    joint[...] = jnp.zeros_like(joint)
    at = 0
    for part in parts:
        joint[at : at + part.shape[0]] = part[...]
        at += part.shape[0]
    out[...] = jnp.zeros_like(out)
    out[:, : joint.shape[1]] = moved(joint[...], source[...], 1)
    out[at : at + 1] = bias[...]
    out[at + 1 : at + 2, 0:1] = loss[...]


def gather_small(source, parts, bias, loss):
    return pl.pallas_call(
        gather_small_kernel,
        out_shape=jax.ShapeDtypeStruct((16, bias.shape[1]), jnp.float32),
        scratch_shapes=[pltpu.VMEM((16, parts[0].shape[1]), jnp.float32)],
        compiler_params=room,
        name="gather_small",
    )(source, *parts, bias, loss)


def swap(array, axis, mask):
    count = lax.axis_size(axis)
    return lax.ppermute(array, axis, [(i, i ^ mask) for i in range(count)])


def fence(*trees):
    return lax.optimization_barrier(trees)


def dp_masks():
    masks = []
    mask = lax.axis_size("dp") // 2
    while mask > 1:
        masks.append(mask)
        mask //= 2
    return masks


def row_order():
    order = [0]
    for mask in dp_masks() + [1]:
        order = order + [r ^ mask for r in order]
    return order


def packed(blocks):
    return jnp.concatenate(blocks, 0)


def unpacked(array, blocks):
    out = []
    at = 0
    for block in blocks:
        out.append(lax.slice_in_dim(array, at, at + block.shape[0], axis=0))
        at += block.shape[0]
    return out


def doubled(blocks, got):
    return [jnp.concatenate(pair, 0) for pair in zip(blocks, unpacked(got, blocks), strict=True)]


def added(keep, got):
    return (keep.astype(jnp.float32) + got.astype(jnp.float32)).astype(keep.dtype)


def cut_rows(array, half):
    middle = array.shape[-2] // 2
    return array[..., half * middle : (half + 1) * middle, :]


def folded(keep, got, kind):
    if kind == "rows":
        return [added(cut_rows(keep, half), cut_rows(got, half)) for half in range(2)]
    if kind == "blocks":
        return [added(keep[0], got[0]), added(keep[1], got[1])]
    if kind == "turned":
        return [jnp.stack([added(keep[0], got[1]), added(keep[1], got[0])])]
    return [added(keep, got)]


def fold_kernel(kinds, *refs):
    outs = list(refs[2 * len(kinds) :])
    for i, kind in enumerate(kinds):
        for value in folded(refs[2 * i][...], refs[2 * i + 1][...], kind):
            outs.pop(0)[...] = value


def fold_all(jobs):
    kinds = [kind for _, _, kind in jobs]
    arrays = [array for keep, got, _ in jobs for array in (keep, got)]
    shapes = [jax.eval_shape(functools.partial(folded, kind=kind), keep, got) for keep, got, kind in jobs]
    flat = [shape for group in shapes for shape in group]
    outs = pl.pallas_call(
        functools.partial(fold_kernel, kinds),
        out_shape=flat,
        compiler_params=room,
        cost_estimate=cost(sum(a.size for a in arrays), sum(4 * a.size for a in arrays)),
        name="fold_all",
    )(*arrays)
    out = []
    for group in shapes:
        out.append(outs[: len(group)])
        outs = outs[len(group) :]
    return out


def reduce_rows(keep, got):
    keep, send = yield keep, got, "rows"
    steps = [1] + dp_masks()[::-1]
    for mask in steps[:-1]:
        keep, send = yield keep, swap(send, "dp", mask), "rows"
    (keep,) = yield keep, swap(send, "dp", steps[-1]), "sum"
    (keep,) = yield keep, swap(keep, "tok", 2), "turned"
    near, far = yield keep, swap(keep, "tok", 1), "none"
    return near, far


def reduce_columns(keep, got):
    keep, send = yield keep, got, "blocks"
    keep, send = yield keep, swap(send, "tok", 2), "rows"
    steps = [1] + dp_masks()[::-1]
    for mask in steps[:-1]:
        keep, send = yield keep, swap(send, "dp", mask), "rows"
    (keep,) = yield keep, swap(send, "dp", steps[-1]), "sum"
    keep, others = yield keep, [swap(keep, "tok", q) for q in range(1, 4)], "none"
    return [keep, *others]


def reduce_cores(grads):
    keep, got = grads[:2], swap(grads[2:], "tok", 1)
    return (yield from reduce_columns(keep, got))


def reduce_tokens(array):
    axis = array.ndim - 1
    for mask in (1, 2):
        middle = array.shape[axis] // 2
        keep = lax.slice_in_dim(array, 0, middle, axis=axis)
        send = lax.slice_in_dim(array, middle, 2 * middle, axis=axis)
        (array,) = yield keep, swap(send, "tok", mask), "sum"
    for mask in [1] + dp_masks()[::-1]:
        (array,) = yield array, swap(array, "dp", mask), "sum"
    return array


def sum_over(array, steps):
    for axis, mask in steps:
        (array,) = yield array, swap(array, axis, mask), "sum"
    return array


class Chain:
    def __init__(self, moves):
        self.moves, self.result = moves, None
        self.state = next(moves)

    def push(self, state):
        try:
            self.state = self.moves.send(state)
        except StopIteration as end:
            self.state, self.result = None, end.value


def advance(chains, *others):
    chains = [chain for chain in chains if chain.state is not None]
    states, others = fence([chain.state[:2] for chain in chains], others)
    jobs = []
    for chain, (keep, got) in zip(chains, states, strict=True):
        kind = chain.state[2]
        small = keep.size <= FOLD_MAX if kind != "none" else False
        if kind in ("rows",) and keep.shape[-2] % 32:
            small = False
        if small:
            jobs.append((chain, keep, got, kind))
    results = dict(
        zip([id(job[0]) for job in jobs], fold_all([job[1:] for job in jobs]) if jobs else [], strict=True)
    )
    for chain, (keep, got) in zip(chains, states, strict=True):
        kind = chain.state[2]
        if id(chain) in results:
            chain.push(results[id(chain)])
        elif kind == "none":
            chain.push((keep, got))
        else:
            chain.push(folded(keep, got, kind))
    return others


def exchanged(blocks):
    row = lax.axis_index("tok")
    blocks = [jnp.where((row & 1) == 1, blocks[k ^ 1], blocks[k]) for k in range(4)]
    return [jnp.where((row & 2) == 2, blocks[k ^ 2], blocks[k]) for k in range(4)]


def ordered(blocks, axis):
    return jnp.concatenate(exchanged([blocks[0], blocks[2], blocks[1], blocks[3]]), axis)


def quarter(array, axis):
    size = array.shape[axis] // lax.axis_size("tok")
    return lax.dynamic_slice_in_dim(array, lax.axis_index("tok") * size, size, axis)


def moments(weight, gradient, first, second, decay_rate):
    first_new = beta_one * first + (1 - beta_one) * gradient
    second_new = beta_two * second + (1 - beta_two) * gradient * gradient
    update = (
        first_new / (1 - beta_one**STEP) / (jnp.sqrt(second_new / (1 - beta_two**STEP)) + epsilon)
        + decay_rate * weight
    )
    return (first_new, second_new, update)


def row_squares(array, groups):
    flat = array.reshape(groups, -1)
    return jnp.sum(flat * flat, 1)


def renew(weight, update, weight_norm, update_norm, groups):
    trust = weight_norm / (update_norm + epsilon)
    return weight - learn_rate * (trust[:, None] * update.reshape(groups, -1)).reshape(weight.shape)


def body(
    images,
    partner,
    lam,
    labels,
    counts,
    class_weights,
    stem_w,
    stem_m,
    stem_v,
    tok_w,
    tok_m,
    tok_v,
    chan_w,
    chan_m,
    chan_v,
    head_w,
    head_m,
    head_v,
    vec_w,
    vec_m,
    vec_v,
    hb_w,
    hb_m,
    hb_v,
):
    count_dp = lax.axis_size("dp")
    count_tok = lax.axis_size("tok")
    device_row = lax.axis_index("dp")
    token_row = lax.axis_index("tok")
    patches = images.shape[0]
    all_patches = patches * count_tok
    per_device = images.shape[1]
    per_tok = per_device // count_tok
    classes_all = hb_w.shape[0]
    class_pad = -classes_all % (count_tok * LANES)
    width = vec_w.shape[1]
    each = all_patches + -all_patches % SUBLANES

    masks = dp_masks()
    batches = per_device // IMG_MB
    start = device_row * per_device
    own_parts, owners, shares = [], [], []
    for batch in range(batches):
        at = start + batch * IMG_MB
        own_parts.append(images[:, batch * IMG_MB : (batch + 1) * IMG_MB])
        owners.append(lax.dynamic_slice_in_dim(partner, at, IMG_MB, 0) % IMG_MB)
        shares.append(lax.dynamic_slice_in_dim(lam, at, IMG_MB, 0))
    device = token_row.astype(jnp.int32)[None]

    def mixed_pieces(batch, incoming):
        sends = mix(owners[batch], shares[batch], device, own_parts[batch], incoming, count_tok)
        return [sends[0]] + [swap(sends[q], "tok", q) for q in range(1, count_tok)]

    chan_low = quarter(chan_w.astype(low), 3)
    shard, size = chan_low.shape[2:]
    order = row_order()
    rows = jnp.asarray(order, jnp.int32) ^ device_row
    column_source = (rows[:, None] * shard + jnp.arange(shard, dtype=jnp.int32)[None, :]).reshape(1, width)
    ends = jnp.concatenate([stem_w.astype(low).T, jnp.pad(head_w.astype(low), ((0, 0), (0, class_pad)))], 1)
    ends = lax.all_gather(ends, "dp")
    later = lax.all_gather(chan_low[1].reshape(2 * shard, size), ("dp", "tok"))
    later = later.reshape(count_dp, count_tok, 2 * shard, size)

    vectors = relative_vectors(vec_w, column_source)
    numbers = jnp.arange(classes_all + class_pad, dtype=jnp.int32)
    numbers = jnp.where(numbers < classes_all, numbers, -1)[None]
    bias = jnp.pad(hb_w, (0, class_pad))[None]
    own_hot = (labels[:, None] == jnp.arange(classes_all, dtype=jnp.int32)[None, :]).astype(jnp.float32)
    other_labels = jnp.take(labels, partner)
    own_weight = jnp.sum(own_hot * class_weights[None, :], 1)
    other_weight = jnp.take(own_weight, partner)
    live = (
        (jnp.arange(IMG_MB, dtype=jnp.int32)[None, :] < counts.reshape(-1)[:, None])
        .astype(jnp.float32)
        .reshape(-1)
    )
    weights = live * (lam * own_weight + (1 - lam) * other_weight)
    total = jnp.sum(weights)
    group = IMG_MB // count_tok

    def row_of(array):
        return jnp.concatenate(
            [
                lax.dynamic_slice_in_dim(array, start + batch * IMG_MB + token_row * group, group, 0)
                for batch in range(batches)
            ]
        )[:, None]

    image_rows = [row_of(array) for array in (labels, other_labels, lam, weights, weights / total)]

    blocks = [chan_low[0, 0], chan_low[0, 1]]
    tok_low = tok_w.astype(low)
    partner_mask = count_dp // 2
    incoming_one = swap(own_parts[0], "dp", partner_mask)
    for step, mask in enumerate(masks):
        got = swap(packed(blocks), "dp", mask)
        if step == 0:
            blocks, got, tok_far, own_parts[1] = fence(blocks, got, swap(tok_low, "tok", 2), own_parts[1])
            tok_half = jnp.concatenate([tok_low, tok_far], 3)
            tok_near = swap(tok_half, "tok", 1)
        elif step == 1:
            blocks, got, tok_near, incoming_one, own_parts[1], vectors, image_rows = fence(
                blocks, got, tok_near, incoming_one, own_parts[1], vectors, image_rows
            )
        else:
            blocks, got = fence(blocks, got)
        blocks = doubled(blocks, got)
    tok_all = jnp.concatenate([tok_half, tok_near], 3)
    tok_all = jnp.pad(tok_all, ((0, 0), (0, 0), (0, each - all_patches), (0, 0)))
    tok_turn = jnp.swapaxes(tok_all, 2, 3)

    incoming_two = swap(own_parts[1], "dp", partner_mask)
    first, second = blocks
    first_low, second_far = swap(first, "dp", 1), swap(second, "tok", 2)
    first, second, first_low, second_far, incoming_one = fence(first, second, first_low, second_far, incoming_one)
    pieces = mixed_pieces(0, incoming_one)
    firsts, seconds = jnp.stack([first, first_low]), jnp.stack([second, second_far])
    firsts_far, seconds_low = swap(firsts, "tok", 2), swap(seconds, "dp", 1)
    firsts, seconds, firsts_far, seconds_low, incoming_two, pieces, tok_all, tok_turn = fence(
        firsts, seconds, firsts_far, seconds_low, incoming_two, pieces, tok_all, tok_turn
    )
    more = mixed_pieces(1, incoming_two)
    source_zero = Pieces(
        [firsts, firsts_far, swap(firsts, "tok", 1), swap(firsts_far, "tok", 1)],
        [seconds, seconds_low, swap(seconds, "tok", 1), swap(seconds_low, "tok", 1)],
    )
    ends = jnp.take(ends, rows, axis=0).reshape(width, -1)
    stem_all, head_all = ends[:, : stem_w.shape[0]], ends[:, stem_w.shape[0] :]
    if shard % 16:
        later = jnp.take(later, rows, axis=0).reshape(width // 96, 96 // shard, count_tok, 2, shard, size)
        later = later.transpose(0, 2, 3, 1, 4, 5).reshape(width // 96, count_tok, 2 * 96, size)
        source_one = Gathered(later, jnp.arange(width // 96, dtype=jnp.int32), device)
    else:
        source_one = Gathered(later, rows, device)

    gains = [vectors[1 + 4 * layer : 5 + 4 * layer] for layer in range(LAYERS)]
    mixed, stem_state = stem(device, pieces + more, stem_all, vectors, each * per_tok)
    middle_zero, before_zero = token_forward(stem_state, gains[0], tok_turn[0, 0], tok_all[0, 1])
    first_state, inner_zero = channel_forward(middle_zero, gains[0], source_zero)
    middle_one, before_one = token_forward(first_state, gains[1], tok_turn[1, 0], tok_all[1, 1])
    second_state, inner_one = channel_forward(middle_one, gains[1], source_one)
    gradient, last_part, head_grads, bias_part, loss_local = head_step(
        device, second_state, vectors[NV - 2 :], head_all, bias, numbers, *image_rows, all_patches
    )

    head_chain = Chain(reduce_cores(head_grads))
    send, partial, _ = channel_backward(gradient, middle_one, gains[1], inner_one, source_one)
    got = swap(send, "tok", 1)
    keep, gradient, second_one = channel_backward(gradient, middle_one, gains[1], inner_one, source_one, partial)
    chains_one = [Chain(reduce_rows(keep[0], got[0])), Chain(reduce_columns(keep[1], got[1]))]
    (gradient,) = advance([head_chain] + chains_one, gradient)
    gradient, first_one, *token_one = token_backward(
        gradient, first_state, gains[1], before_one, tok_all[1, 0], tok_turn[1, 1]
    )
    send, partial, _ = channel_backward(gradient, middle_zero, gains[0], inner_zero, source_zero)
    send, partial, gradient = advance([head_chain] + chains_one, send, partial, gradient)
    got = swap(send, "tok", 1)
    keep, gradient, second_zero = channel_backward(gradient, middle_zero, gains[0], inner_zero, source_zero, partial)
    chains_zero = [Chain(reduce_rows(keep[0], got[0])), Chain(reduce_columns(keep[1], got[1]))]
    (gradient,) = advance([head_chain] + chains_one + chains_zero, gradient)
    gradient, first_zero, *token_zero = token_backward(
        gradient, stem_state, gains[0], before_zero, tok_all[0, 0], tok_turn[0, 1]
    )
    stem_grads, stem_bias = stem_backward(device, gradient, mixed)
    small = gather_small(
        column_source,
        [stem_bias, first_zero, second_zero, first_one, second_one, last_part],
        bias_part,
        loss_local,
    )
    token_part = jnp.stack([jnp.stack(token_zero), jnp.stack(token_one)])[:, :, :all_patches].astype(low)
    dp_steps = [("dp", mask) for mask in [1] + dp_masks()[::-1]]
    stem_chain = Chain(reduce_cores(stem_grads))
    token_chain = Chain(reduce_tokens(token_part))
    small_chain = Chain(sum_over(small, [("tok", 1), ("tok", 2)] + dp_steps))
    everything = [head_chain] + chains_one + chains_zero + [stem_chain, token_chain, small_chain]
    earlier = []
    while any(chain.state is not None for chain in everything):
        if not earlier and all(chain.result is not None for chain in chains_one):
            *earlier, squares_one = channel_step(
                1, device, chan_w, chan_m, chan_v, *[chain.result for chain in chains_one], []
            )
            earlier = list(advance(everything, *earlier))
        else:
            advance(everything)
    chan_first, chan_second, chan_update, squares_zero = channel_step(
        0, device, chan_w, chan_m, chan_v, *[chain.result for chain in chains_zero], earlier
    )
    token_grad = token_chain.result.astype(jnp.float32)
    small = small_chain.result
    vector_grad = small[:NV, :width]
    bias_grad = small[NV, :classes_all]
    loss_total = small[NV + 1, 0]
    placed = lambda parts: [parts[0], parts[2], parts[1], parts[3]]
    head_grad = ordered(placed(head_chain.result), 1)[:, :classes_all].astype(jnp.float32)
    stem_grad = ordered(placed(stem_chain.result), 1).astype(jnp.float32).T
    stem_first, stem_second, stem_update = moments(stem_w, stem_grad, stem_m, stem_v, weight_decay)
    tok_first, tok_second, tok_update = moments(tok_w, token_grad, tok_m, tok_v, weight_decay)
    head_first, head_second, head_update = moments(head_w, head_grad, head_m, head_v, weight_decay)
    vec_first, vec_second, vec_update = moments(vec_w, vector_grad, vec_m, vec_v, 0.0)
    hb_first, hb_second, hb_update = moments(hb_w, bias_grad, hb_m, hb_v, 0.0)
    matrix_groups = 2 * LAYERS
    squares = jnp.stack([squares_zero, squares_one])
    weight_squares = jnp.concatenate(
        [
            row_squares(stem_w, 1) / count_tok,
            row_squares(tok_w, matrix_groups) / count_dp,
            squares[:, :, 0].reshape(-1) / count_tok,
            row_squares(head_w, 1) / count_tok,
        ]
    )
    update_squares = jnp.concatenate(
        [
            row_squares(stem_update, 1) / count_tok,
            row_squares(tok_update, matrix_groups) / count_dp,
            squares[:, :, 1].reshape(-1) / count_tok,
            row_squares(head_update, 1) / count_tok,
        ]
    )
    norm_chain = Chain(
        sum_over(jnp.stack([weight_squares, update_squares]), [("tok", 1), ("tok", 2)] + dp_steps)
    )
    while norm_chain.state is not None:
        advance([norm_chain])
    weight_total, update_total = norm_chain.result
    weight_norms = jnp.sqrt(weight_total)
    update_norms = jnp.sqrt(update_total)
    stem_end = 1
    tok_end = 1 + matrix_groups
    chan_end = 1 + 2 * matrix_groups
    stem_new = renew(stem_w, stem_update, weight_norms[0:stem_end], update_norms[0:stem_end], 1)
    tok_new = renew(
        tok_w,
        tok_update,
        weight_norms[stem_end:tok_end],
        update_norms[stem_end:tok_end],
        matrix_groups,
    )
    chan_trust = weight_norms[tok_end:chan_end] / (update_norms[tok_end:chan_end] + epsilon)
    chan_new, chan_new_low = channel_renew(chan_trust.reshape(LAYERS, 2), chan_w, chan_update)
    head_new = renew(head_w, head_update, weight_norms[chan_end:], update_norms[chan_end:], 1)
    vec_weight_norm = jnp.sqrt(row_squares(vec_w, NV))
    vec_update_norm = jnp.sqrt(row_squares(vec_update, NV))
    hb_weight_norm = jnp.sqrt(row_squares(hb_w, 1))
    hb_update_norm = jnp.sqrt(row_squares(hb_update, 1))
    vec_new = renew(vec_w, vec_update, vec_weight_norm, vec_update_norm, NV)
    hb_new = renew(hb_w, hb_update, hb_weight_norm, hb_update_norm, 1)
    norms = jnp.stack(
        [
            jnp.concatenate([weight_norms, vec_weight_norm, hb_weight_norm]),
            jnp.concatenate([update_norms, vec_update_norm, hb_update_norm]),
        ],
        1,
    )
    loss_parts = jnp.stack([loss_total, total])
    return (
        stem_new,
        stem_first,
        stem_second,
        tok_new,
        tok_first,
        tok_second,
        chan_new,
        chan_first,
        chan_second,
        head_new,
        head_first,
        head_second,
        vec_new,
        vec_first,
        vec_second,
        hb_new,
        hb_first,
        hb_second,
        stem_new.astype(jnp.bfloat16),
        tok_new.astype(jnp.bfloat16),
        chan_new_low,
        head_new.astype(jnp.bfloat16),
        norms,
        loss_parts,
    )


def solution(mesh):
    in_specs = (
        P("tok", "dp", None),
        P(),
        P(),
        P(),
        P(),
        P(),
        P(None, "dp"),
        P(None, "dp"),
        P(None, "dp"),
        P(None, None, None, "tok"),
        P(None, None, None, "tok"),
        P(None, None, None, "tok"),
        P(None, None, "dp", None),
        P(None, None, "dp", None),
        P(None, None, "dp", None),
        P("dp", None),
        P("dp", None),
        P("dp", None),
        P(),
        P(),
        P(),
        P(),
        P(),
        P(),
    )
    out_specs = (
        P(None, "dp"),
        P(None, "dp"),
        P(None, "dp"),
        P(None, None, None, "tok"),
        P(None, None, None, "tok"),
        P(None, None, None, "tok"),
        P(None, None, "dp", None),
        P(None, None, "dp", None),
        P(None, None, "dp", None),
        P("dp", None),
        P("dp", None),
        P("dp", None),
        P(),
        P(),
        P(),
        P(),
        P(),
        P(),
        P(None, "dp"),
        P(None, None, None, "tok"),
        P(None, None, "dp", None),
        P("dp", None),
        P(),
        P(),
    )
    return jax.shard_map(body, mesh=mesh, in_specs=in_specs, out_specs=out_specs, check_vma=False)
```

```python
import functools

import jax
import jax.numpy as jnp
from jax import lax
from jax.experimental import pallas as pl
from jax.experimental.pallas import tpu as pltpu
from jax.sharding import PartitionSpec as P

LAYERS = 2
STEP = 5
IMG_MB = 8
NV = 11
LANES = 128
SUBLANES = 8
FOLD_MAX = 1200000
MISC = 256
SMALL = 64

low = jnp.bfloat16
beta_one = 0.9
beta_two = 0.999
epsilon = 1e-06
weight_decay = 0.01
learn_rate = 0.3
root = 0.7978845608028654
cubic = 0.044715
room = pltpu.CompilerParams(vmem_limit_bytes=44 * 1024 * 1024)
places = (0, 2, 1, 3)
large = pltpu.CompilerParams(vmem_limit_bytes=60 * 1024 * 1024)


def dot(left, right, contract=(1, 0)):
    return lax.dot_general(
        left, right, (((contract[0],), (contract[1],)), ((), ())), preferred_element_type=jnp.float32
    )


def gelu(values):
    return 0.5 * values * (1 + jnp.tanh(root * values * (1 + cubic * values * values)))


def gelu_both(values):
    square = values * values
    bend = jnp.tanh(root * values * (1 + cubic * square))
    half = 0.5 * (1 + bend)
    slope = half + 0.5 * values * (1 - bend * bend) * (root * (1 + 3 * cubic * square))
    return values * half, slope


def centred(values):
    centre = values - jnp.mean(values, -1, keepdims=True)
    inverse = lax.rsqrt(jnp.mean(centre * centre, -1, keepdims=True) + 1e-06)
    return centre * inverse, inverse


def centred_back(scaled, hat, inverse):
    return inverse * (
        scaled - jnp.mean(scaled, -1, keepdims=True) - hat * jnp.mean(scaled * hat, -1, keepdims=True)
    )


def whole(array):
    zeros = (0,) * array.ndim
    return pl.BlockSpec(array.shape, lambda *_: zeros)


def cost(flops, bytes_accessed, powers=0):
    return pl.CostEstimate(flops=flops, bytes_accessed=bytes_accessed, transcendentals=powers)


def token_forward_kernel(state, gains, token_in, token_out, middle, before):
    hat, _ = centred(state[...])
    normed = (hat * gains[0:1] + gains[1:2]).astype(low)
    pre = dot(token_in[...], normed)
    before[0] = pre.astype(low)
    middle[...] = state[...] + dot(token_out[...], gelu(pre).astype(low))


def token_forward(state, gains, token_in, token_out):
    hidden, rows = token_in.shape
    count, width = state.shape[0] // rows, state.shape[1]
    one = pl.BlockSpec((rows, width), lambda i: (i, 0))
    return pl.pallas_call(
        token_forward_kernel,
        grid=(count,),
        in_specs=[one, whole(gains), whole(token_in), whole(token_out)],
        out_specs=[one, pl.BlockSpec((1, hidden, width), lambda i: (i, 0, 0))],
        out_shape=[
            jax.ShapeDtypeStruct(state.shape, jnp.float32),
            jax.ShapeDtypeStruct((count, hidden, width), low),
        ],
        compiler_params=room,
        cost_estimate=cost(4 * count * rows * hidden * width, 10 * state.size, 0),
        name="token_forward",
    )(state, gains, token_in, token_out)


def block_copies(spots, blocks, lanes, held, sems):
    rows = blocks.shape[1]
    return [
        pltpu.make_async_copy(blocks.at[spots[i], :, lanes], held.at[pl.ds(i * rows, rows)], sems.at[i])
        for i in range(blocks.shape[0])
    ]


def hbm(arrays):
    return [pl.BlockSpec(memory_space=pl.ANY)] * len(arrays)


scalars = pl.BlockSpec(memory_space=pltpu.SMEM)


class Pieces:
    def __init__(self, first, second):
        self.arrays = [*first, *second]
        self.specs = hbm(self.arrays)
        self.width = 2 * second[0].shape[1]
        self.size = second[0].shape[2]
        self.sems = 4

    def copies(self, refs, held_in, held_out, sems, slot, place):
        half = self.width // 2
        out = []
        for side in range(2):
            rows = pl.ds(side * half, half)
            first = refs[place].at[side, pl.ds(0, half)]
            second = refs[4 + place // 2 * 2 + side].at[place % 2]
            out.append(pltpu.make_async_copy(first, held_in.at[slot, rows], sems.at[slot, side]))
            out.append(pltpu.make_async_copy(second, held_out.at[slot, rows], sems.at[slot, 2 + side]))
        return out


class Gathered:
    def __init__(self, array, shards, device, rows):
        self.arrays = [shards, device, array]
        self.specs = [scalars, scalars] + hbm([array])
        self.blocks, self.rows, self.size = array.shape[0], rows, array.shape[3]
        self.width = self.blocks * self.rows
        self.sems = 2 * self.blocks

    def copies(self, refs, held_in, held_out, sems, slot, place):
        shards, device, array = refs
        quarter_at = device[0] ^ places[place]
        out = []
        for block in range(self.blocks):
            rows = pl.ds(block * self.rows, self.rows)
            for way, held in enumerate((held_in, held_out)):
                out.append(
                    pltpu.make_async_copy(
                        array.at[shards[block], quarter_at, pl.ds(way * self.rows, self.rows)],
                        held.at[slot, rows],
                        sems.at[slot, 2 * block + way],
                    )
                )
        return out


def channel_forward_kernel(source, middle, gains, *rest):
    refs = rest[: len(source.arrays)]
    result, inner, normed, held_in, held_out, sems = rest[-6:]
    step = pl.program_id(0)

    @pl.when(step == 0)
    def _():
        for q in range(4):
            for copy in source.copies(refs, held_in, held_out, sems, q, q):
                copy.start()
        hat, _ = centred(middle[...])
        normed[...] = (hat * gains[2:3] + gains[3:4]).astype(low)
        result[...] = middle[...]

    for q in range(4):

        @pl.when(step == q)
        def _(q=q):
            for copy in source.copies(refs, held_in, held_out, sems, q, q):
                copy.wait()
            product = dot(normed[...], held_in[q])
            inner[...] = product.astype(low)
            result[...] += dot(gelu(product).astype(low), held_out[q], (1, 1))


def channel_forward(middle, gains, source):
    rows, width = middle.shape
    size = source.size
    total = 4 * size
    return pl.pallas_call(
        functools.partial(channel_forward_kernel, source),
        grid=(4,),
        in_specs=[whole(middle), whole(gains)] + source.specs,
        out_specs=[whole(middle), pl.BlockSpec((rows, size), lambda i: (0, i))],
        out_shape=[
            jax.ShapeDtypeStruct(middle.shape, jnp.float32),
            jax.ShapeDtypeStruct((rows, total), low),
        ],
        scratch_shapes=[
            pltpu.VMEM(middle.shape, low),
            pltpu.VMEM((4, width, size), low),
            pltpu.VMEM((4, width, size), low),
            pltpu.SemaphoreType.DMA((4, source.sems)),
        ],
        compiler_params=room,
        cost_estimate=cost(4 * rows * width * total, 4 * width * total + 2 * rows * total),
        name="channel_forward",
    )(middle, gains, *source.arrays)


def channel_backward_kernel(source, last, gradient, middle, gains, inner, *rest):
    if last:
        before, rest = rest[0], rest[1:]
    refs = rest[: len(source.arrays)]
    grads, total, grad_vectors, grad_low, grad_turn, normed_turn, held_in, held_out, sems = rest[-9:]
    step = pl.program_id(0)
    first = 0 if last else 2

    @pl.when(step == 0)
    def _():
        for q in range(2):
            for copy in source.copies(refs, held_in, held_out, sems, q, first + q):
                copy.start()
        grad_low[...] = gradient[...].astype(low)
        grad_turn[...] = gradient[...].T.astype(low)
        hat, _ = centred(middle[...])
        normed_turn[...] = (hat * gains[2:3] + gains[3:4]).T.astype(low)
        total[...] = before[...] if last else jnp.zeros_like(total)

    for q in range(2):

        @pl.when(step == q)
        def _(q=q):
            for copy in source.copies(refs, held_in, held_out, sems, q, first + q):
                copy.wait()
            active, slope = gelu_both(inner[...].astype(jnp.float32))
            grads[1, 0] = dot(grad_turn[...], active.astype(low)).astype(low)
            grad_inner = (slope * dot(grad_low[...], held_out[q])).astype(low)
            grads[0, 0] = dot(normed_turn[...], grad_inner).astype(low)
            total[...] += dot(grad_inner, held_in[q], (1, 1))

    if last:

        @pl.when(step == 1)
        def _():
            hat, inverse = centred(middle[...])
            upstream = total[...]
            grad_vectors[0:1] = jnp.sum(upstream * hat, 0, keepdims=True)
            grad_vectors[1:2] = jnp.sum(upstream, 0, keepdims=True)
            total[...] = gradient[...] + centred_back(upstream * gains[2:3], hat, inverse)


def channel_backward(gradient, middle, gains, inner, source, before=None):
    rows, width = middle.shape
    size = source.size
    last = before is not None
    shift = 0 if last else 2
    carried = [before] if last else []
    total = 2 * size
    return pl.pallas_call(
        functools.partial(channel_backward_kernel, source, last),
        grid=(2,),
        in_specs=[whole(middle), whole(middle), whole(gains), pl.BlockSpec((rows, size), lambda i: (0, i + shift))]
        + [whole(array) for array in carried]
        + source.specs,
        out_specs=[
            pl.BlockSpec((2, 1, width, size), lambda i: (0, i, 0, 0)),
            whole(middle),
            pl.BlockSpec((2, width), lambda i: (0, 0)),
        ],
        out_shape=[
            jax.ShapeDtypeStruct((2, 2, width, size), low),
            jax.ShapeDtypeStruct(middle.shape, jnp.float32),
            jax.ShapeDtypeStruct((2, width), jnp.float32),
        ],
        scratch_shapes=[
            pltpu.VMEM((rows, width), low),
            pltpu.VMEM((width, rows), low),
            pltpu.VMEM((width, rows), low),
            pltpu.VMEM((2, width, size), low),
            pltpu.VMEM((2, width, size), low),
            pltpu.SemaphoreType.DMA((2, source.sems)),
        ],
        compiler_params=room,
        cost_estimate=cost(8 * rows * width * total, 8 * width * total + 2 * rows * total),
        name="channel_backward",
    )(gradient, middle, gains, inner, *carried, *source.arrays)


def step_kernel(device, weight, mean, power, near, far, *rest):
    apart, (mean_new, power_new, update, sums) = rest[:4], rest[-4:]
    way = pl.program_id(0)
    size = near.shape[2]
    weight_part, update_part = 0.0, 0.0
    for a in range(4):
        rel = device[0] ^ a
        lanes = slice(a * size, (a + 1) * size)
        values = [
            jnp.where(way == 0, one.astype(jnp.float32), two[...].astype(jnp.float32))
            for one, two in zip((near[0], far[0], near[1], far[1]), apart, strict=True)
        ]
        grad = jnp.where(
            rel < 2, jnp.where(rel == 0, values[0], values[1]), jnp.where(rel == 2, values[2], values[3])
        )
        value = weight[0, 0, :, lanes]
        mean_next, power_next, change = moments(
            value, grad, mean[0, 0, :, lanes], power[0, 0, :, lanes], weight_decay
        )
        mean_new[0, 0, :, lanes] = mean_next
        power_new[0, 0, :, lanes] = power_next
        update[0, 0, :, lanes] = change
        weight_part += jnp.sum(jnp.sum(value * value, 0, keepdims=True))
        update_part += jnp.sum(jnp.sum(change * change, 0, keepdims=True))

    @pl.when(pl.program_id(1) == 0)
    def _():
        sums[way, 0] = weight_part
        sums[way, 1] = update_part

    @pl.when(pl.program_id(1) > 0)
    def _():
        sums[way, 0] += weight_part
        sums[way, 1] += update_part


def channel_step(layer, device, weight, mean, power, chain_in, chain_out, earlier):
    near, far = chain_in
    rows, size = near.shape[1:]
    columns = weight.shape[3]
    chunk = 32 if rows % 32 == 0 else rows
    block = pl.BlockSpec((1, 1, chunk, columns), lambda w, i: (layer, w, i, 0))
    two = pl.BlockSpec((2, chunk, size), lambda w, i: (0, i, 0))
    one = pl.BlockSpec((chunk, size), lambda w, i: (i, 0))
    shape = jax.ShapeDtypeStruct(weight.shape, jnp.float32)
    return pl.pallas_call(
        step_kernel,
        grid=(2, rows // chunk),
        in_specs=[scalars, block, block, block, two, two, one, one, one, one] + hbm(earlier),
        out_specs=[block, block, block, scalars],
        out_shape=[shape, shape, shape, jax.ShapeDtypeStruct((2, 2), jnp.float32)],
        input_output_aliases={10 + i: i for i in range(len(earlier))},
        compiler_params=large,
        cost_estimate=cost(40 * near.size, 104 * near.size),
        name="channel_step",
    )(device, weight, mean, power, near, far, *chain_out, *earlier)


def renew_kernel(trust, weight, update, fresh, fresh_low):
    value = weight[...] - learn_rate * (trust[pl.program_id(0), pl.program_id(1)] * update[...])
    fresh[...] = value
    fresh_low[...] = value.astype(low)


def channel_renew(trust, weight, update):
    layers, ways, rows, columns = weight.shape
    block = pl.BlockSpec((1, 1, rows, columns), lambda i, j: (i, j, 0, 0))
    return pl.pallas_call(
        renew_kernel,
        grid=(layers, ways),
        in_specs=[pl.BlockSpec(memory_space=pltpu.SMEM), block, block],
        out_specs=[block, block],
        out_shape=[jax.ShapeDtypeStruct(weight.shape, jnp.float32), jax.ShapeDtypeStruct(weight.shape, low)],
        compiler_params=large,
        cost_estimate=cost(3 * weight.size, 14 * weight.size),
        name="channel_renew",
    )(trust, weight, update)


def token_backward_kernel(gradient, state, gains, before, token_in, token_out_turn, *rest):
    grad_state, grad_vectors, grad_in, grad_out = rest[-4:]
    step = pl.program_id(0)
    token_grad = gradient[...].astype(low)
    hat, inverse = centred(state[...])
    normed = (hat * gains[0:1] + gains[1:2]).astype(low)
    hidden, slope = gelu_both(before[0].astype(jnp.float32))
    grad_before = (slope * dot(token_out_turn[...], token_grad)).astype(low)
    part_out = dot(hidden.astype(low), token_grad, (1, 1))
    part_in = dot(grad_before, normed, (1, 1))
    upstream = dot(token_in[...], grad_before)
    grad_state[...] = gradient[...] + centred_back(upstream * gains[0:1], hat, inverse)
    part_gain = jnp.sum(upstream * hat, 0, keepdims=True)
    part_shift = jnp.sum(upstream, 0, keepdims=True)

    @pl.when(step == 0)
    def _():
        grad_out[...] = part_out
        grad_in[...] = part_in
        grad_vectors[0:1] = part_gain
        grad_vectors[1:2] = part_shift

    @pl.when(step > 0)
    def _():
        grad_out[...] += part_out
        grad_in[...] += part_in
        grad_vectors[0:1] += part_gain
        grad_vectors[1:2] += part_shift


def token_backward(gradient, state, gains, before, token_in, token_out_turn, after=()):
    rows, hidden = token_in.shape
    count, width = state.shape[0] // rows, state.shape[1]
    one = pl.BlockSpec((rows, width), lambda i: (i, 0))
    still = lambda shape: pl.BlockSpec(shape, lambda i: (0, 0))
    return pl.pallas_call(
        token_backward_kernel,
        grid=(count,),
        in_specs=[
            one, one, whole(gains), pl.BlockSpec((1, hidden, width), lambda i: (i, 0, 0)),
            whole(token_in), whole(token_out_turn),
        ] + [pl.BlockSpec(memory_space=pl.ANY)] * len(after),
        out_specs=[one, still((2, width)), still((hidden, rows)), still((hidden, rows))],
        out_shape=[
            jax.ShapeDtypeStruct(state.shape, jnp.float32),
            jax.ShapeDtypeStruct((2, width), jnp.float32),
            jax.ShapeDtypeStruct((hidden, rows), jnp.float32),
            jax.ShapeDtypeStruct((hidden, rows), jnp.float32),
        ],
        compiler_params=room,
        cost_estimate=cost(8 * count * rows * hidden * width, 16 * state.size, 0),
        name="token_backward",
    )(gradient, state, gains, before, token_in, token_out_turn, *after)


def mix_kernel(place, share, device, own, incoming, *rest):
    outs, (own_wide, incoming_wide, joint) = rest[:-3], rest[-3:]
    patches, images, width = own.shape
    group = images // len(outs)
    for at in range(0, width, LANES):
        lanes = slice(at, at + LANES)
        own_wide[...] = own[:, :, lanes].astype(jnp.float32).reshape(own_wide.shape)
        incoming_wide[...] = incoming[:, :, lanes].astype(jnp.float32).reshape(own_wide.shape)
        for q, out in enumerate(outs):
            for i in range(group):
                image = (device[0] ^ q) * group + i
                first = own_wide[pl.ds(image, patches, stride=images), :]
                second = incoming_wide[pl.ds(place[image], patches, stride=images), :]
                joint[i * patches : (i + 1) * patches, :] = (
                    share[image] * first + (1 - share[image]) * second
                )
            out[:, lanes] = joint[...].astype(low)


def mix(place, share, device, own, incoming, groups):
    patches, images, width = own.shape
    rows = images // groups * patches
    scalar = pl.BlockSpec(memory_space=pltpu.SMEM)
    return pl.pallas_call(
        mix_kernel,
        in_specs=[scalar, scalar, scalar, pl.BlockSpec(), pl.BlockSpec()],
        out_shape=[jax.ShapeDtypeStruct((rows, width), low)] * groups,
        scratch_shapes=[
            pltpu.VMEM((patches * images, LANES), jnp.float32),
            pltpu.VMEM((patches * images, LANES), jnp.float32),
            pltpu.VMEM((rows, LANES), jnp.float32),
        ],
        compiler_params=room,
        cost_estimate=cost(4 * own.size, 6 * own.size),
        name="mix",
    )(place, share, device, own, incoming)


def stem_kernel(device, spots, *rest):
    pieces, (blocks, gains, mixed, state, joint, spare, weights, sems) = rest[:-8], rest[-8:]
    copies = block_copies(spots, blocks, pl.ds(0, weights.shape[1]), weights, sems)
    for copy in copies:
        copy.start()
    count = len(pieces) // 2
    odd, upper = (device[0] & 1) == 1, (device[0] & 2) == 2
    patches = pieces[0].shape[0] // 2
    rows = joint.shape[0] // (2 * 2)
    joint[...] = jnp.zeros_like(joint)
    for side in range(2):
        arrived = [ref[...].astype(jnp.float32) for ref in pieces[side * count : (side + 1) * count]]
        arrived = [jnp.where(odd, arrived[k ^ 1], arrived[k]) for k in range(count)]
        for k in range(count):
            spare[...] = jnp.where(upper, arrived[k ^ 2], arrived[k])
            for i in range(2):
                at = (side * 2 + i) * rows + k * patches
                joint[at : at + patches, :] = spare[i * patches : (i + 1) * patches, :]
    mixed[...] = joint[...].astype(low)
    for copy in copies:
        copy.wait()
    state[...] = dot(mixed[...], weights[...], (1, 1)) + gains[0:1]


def stem(device, spots, pieces, blocks, gains, rows):
    width, pixels = blocks.shape[0] * blocks.shape[1], pieces[0].shape[1]
    return pl.pallas_call(
        stem_kernel,
        in_specs=[scalars, scalars] + [pl.BlockSpec()] * len(pieces) + hbm([blocks]) + [pl.BlockSpec()],
        out_shape=[
            jax.ShapeDtypeStruct((rows, pixels), low),
            jax.ShapeDtypeStruct((rows, width), jnp.float32),
        ],
        scratch_shapes=[
            pltpu.VMEM((rows, pixels), jnp.float32),
            pltpu.VMEM(pieces[0].shape, jnp.float32),
            pltpu.VMEM((width, pixels), low),
            pltpu.SemaphoreType.DMA((blocks.shape[0],)),
        ],
        compiler_params=room,
        cost_estimate=cost(2 * rows * width * pixels, 12 * rows * width),
        name="stem",
    )(device, spots, *pieces, blocks, gains)


def head_kernel(
    patches, pixels, device, spots, state, gains, blocks, bias, numbers, labels, others, lam, weight, scale,
    gradient, grad_vectors, grads, grad_bias, loss, pooled, upstream, head, sems,
):
    copies = block_copies(spots, blocks, pl.ds(pixels, head.shape[1]), head, sems)
    for copy in copies:
        copy.start()
    rows, width = state.shape
    count = lam.shape[0]
    each = rows // count
    live = lax.broadcasted_iota(jnp.int32, (each, 1), 0) < patches
    hat, inverse = centred(state[...])
    pooled[...] = jnp.zeros_like(pooled)
    sums = []
    for i in range(count):
        sums.append(jnp.sum(jnp.where(live, hat[i * each : (i + 1) * each], 0.0), 0, keepdims=True))
        pooled[i : i + 1] = sums[i] / patches * gains[0:1] + gains[1:2]
    pooled_low = pooled[...].astype(low)
    for copy in copies:
        copy.wait()
    logits = dot(pooled_low, head[...])[:count] + bias[...]
    logits = jnp.where(numbers[...] >= 0, logits, -jnp.inf)
    peak = jnp.max(logits, -1, keepdims=True)
    powers = jnp.exp(logits - peak)
    mass = jnp.sum(powers, -1, keepdims=True)
    targets = jnp.where(numbers[...] == labels[...], lam[...], 0.0) + jnp.where(
        numbers[...] == others[...], 1 - lam[...], 0.0
    )
    log_probs = jnp.where(numbers[...] >= 0, logits - peak - jnp.log(mass), 0.0)
    losses = -jnp.sum(targets * log_probs, -1, keepdims=True)
    loss[...] = jnp.sum(weight[...] * losses, 0, keepdims=True)
    grad_logits = scale[...] * (powers / mass * jnp.sum(targets, -1, keepdims=True) - targets)
    grad_bias[...] = jnp.sum(grad_logits, 0, keepdims=True)
    pad = jnp.zeros((pooled.shape[0] - count, grad_logits.shape[1]), jnp.float32)
    grad_logits = jnp.concatenate([grad_logits, pad], 0)
    main = grad_logits.astype(low)
    rest = (grad_logits - main.astype(jnp.float32)).astype(low)
    size = main.shape[1] // 4
    for a in range(4):
        lanes = slice(a * size, (a + 1) * size)
        part = dot(pooled_low, main[:, lanes], (0, 0)) + dot(pooled_low, rest[:, lanes], (0, 0))
        rel = device[0] ^ a
        grads[(rel & 1) * 2 + (rel >> 1)] = part.astype(low)
    spread_back = (dot(main, head[...], (1, 1)) + dot(rest, head[...], (1, 1))) / patches
    upstream[...] = jnp.zeros_like(upstream)
    grad_gain = jnp.zeros((1, width), jnp.float32)
    for i in range(count):
        one = spread_back[i : i + 1]
        grad_gain = grad_gain + one * sums[i]
        upstream[i * each : (i + 1) * each] = jnp.where(live, one, 0.0)
    grad_vectors[0:1] = grad_gain
    grad_vectors[1:2] = jnp.sum(spread_back[:count], 0, keepdims=True) * patches
    gradient[...] = centred_back(upstream[...] * gains[0:1], hat, inverse)


def head_step(device, spots, state, gains, blocks, bias, numbers, labels, others, lam, weight, scale, patches, pixels):
    rows, width = state.shape
    columns = bias.shape[1]
    return pl.pallas_call(
        functools.partial(head_kernel, patches, pixels),
        in_specs=[scalars, scalars] + [pl.BlockSpec()] * 2 + hbm([blocks]) + [pl.BlockSpec()] * 7,
        out_shape=[
            jax.ShapeDtypeStruct(state.shape, jnp.float32),
            jax.ShapeDtypeStruct((2, width), jnp.float32),
            jax.ShapeDtypeStruct((4, width, columns // 4), low),
            jax.ShapeDtypeStruct((1, columns), jnp.float32),
            jax.ShapeDtypeStruct((1, 1), jnp.float32),
        ],
        scratch_shapes=[
            pltpu.VMEM((16, width), jnp.float32),
            pltpu.VMEM(state.shape, jnp.float32),
            pltpu.VMEM((width, columns), low),
            pltpu.SemaphoreType.DMA((blocks.shape[0],)),
        ],
        compiler_params=room,
        cost_estimate=cost(64 * width * columns, 8 * rows * width),
        name="head_step",
    )(device, spots, state, gains, blocks, bias, numbers, labels, others, lam, weight, scale)


def stem_backward_kernel(device, gradient, mixed, grads, shift):
    rounded = gradient[...].astype(low)
    shift[...] = jnp.sum(rounded.astype(jnp.float32), 0, keepdims=True)
    whole_grad = dot(gradient[...].T.astype(low), mixed[...]).astype(low)
    size = whole_grad.shape[1] // 4
    grads[...] = jnp.zeros_like(grads)
    for a in range(4):
        rel = device[0] ^ a
        grads[(rel & 1) * 2 + (rel >> 1), :, :size] = whole_grad[:, a * size : (a + 1) * size]


def stem_backward(device, gradient, mixed):
    width, pixels = gradient.shape[1], mixed.shape[1]
    return pl.pallas_call(
        stem_backward_kernel,
        in_specs=[scalars] + [pl.BlockSpec()] * 2,
        out_shape=[
            jax.ShapeDtypeStruct((4, width, MISC), low),
            jax.ShapeDtypeStruct((1, width), jnp.float32),
        ],
        compiler_params=room,
        cost_estimate=cost(2 * gradient.size * pixels, 8 * gradient.size),
        name="stem_backward",
    )(device, gradient, mixed)


def moved(values, source, way):
    spots = (lax.broadcasted_iota(jnp.int32, (values.shape[1],) * 2, 0) == source).astype(low)
    main = values.astype(low)
    rest = values - main.astype(jnp.float32)
    middle = rest.astype(low)
    rest = (rest - middle.astype(jnp.float32)).astype(low)
    return sum(dot(part, spots, (1, way)) for part in (main, middle, rest))


def vectors_kernel(vectors, source, out):
    out[...] = moved(vectors[...], source[...], 0)


def relative_vectors(vectors, source):
    return pl.pallas_call(
        vectors_kernel,
        out_shape=jax.ShapeDtypeStruct(vectors.shape, jnp.float32),
        compiler_params=room,
        name="relative_vectors",
    )(vectors, source)


def gather_misc_kernel(count, source, stem_grads, *rest):
    tokens, parts, (bias, loss), outs, (joint, small) = (
        rest[:4],
        rest[4:count],
        rest[count : count + 2],
        rest[count + 2 : count + 6],
        rest[count + 6 :],
    )
    joint[...] = jnp.zeros_like(joint)
    at = 0
    for part in parts:
        joint[at : at + part.shape[0]] = part[...]
        at += part.shape[0]
    true = moved(joint[...], source[...], 1)
    small[...] = jnp.zeros_like(small)
    for j in range(joint.shape[1] // MISC):
        small[j * 16 : (j + 1) * 16] = true[:, j * MISC : (j + 1) * MISC]
    at = joint.shape[1] // MISC * 16
    for j in range(bias.shape[1] // MISC):
        small[at + j : at + j + 1] = bias[:, j * MISC : (j + 1) * MISC]
    at += bias.shape[1] // MISC
    small[at : at + 1, 0:1] = loss[...]
    stem_rows = stem_grads.shape[1]
    rows = tokens[0].shape[0] // 4
    patches = tokens[0].shape[1]
    for place, out in enumerate(outs):
        out[:stem_rows] = stem_grads[place]
        for j, token in enumerate(tokens):
            at = stem_rows + j * rows
            out[at : at + rows] = jnp.zeros((rows, MISC), low)
            out[at : at + rows, :patches] = token[place * rows : (place + 1) * rows].astype(low)
        out[stem_rows + 4 * rows :] = small[...].astype(low)


def gather_misc(source, stem_grads, tokens, parts, bias, loss):
    rows = stem_grads.shape[1] + tokens[0].shape[0] + SMALL
    return pl.pallas_call(
        functools.partial(gather_misc_kernel, 4 + len(parts)),
        out_shape=[jax.ShapeDtypeStruct((rows, MISC), low)] * 4,
        scratch_shapes=[
            pltpu.VMEM((16, parts[0].shape[1]), jnp.float32),
            pltpu.VMEM((SMALL, MISC), jnp.float32),
        ],
        compiler_params=room,
        name="gather_misc",
    )(source, stem_grads, *tokens, *parts, bias, loss)


def swap(array, axis, mask):
    count = lax.axis_size(axis)
    return lax.ppermute(array, axis, [(i, i ^ mask) for i in range(count)])


def fence(*trees):
    return lax.optimization_barrier(trees)


def dp_masks():
    masks = []
    mask = lax.axis_size("dp") // 2
    while mask > 1:
        masks.append(mask)
        mask //= 2
    return masks


def row_order():
    order = [0]
    for mask in dp_masks() + [1]:
        order = order + [r ^ mask for r in order]
    return order


def packed(blocks):
    return jnp.concatenate(blocks, 0)


def unpacked(array, blocks):
    out = []
    at = 0
    for block in blocks:
        out.append(lax.slice_in_dim(array, at, at + block.shape[0], axis=0))
        at += block.shape[0]
    return out


def doubled(blocks, got):
    return [jnp.concatenate(pair, 0) for pair in zip(blocks, unpacked(got, blocks), strict=True)]


def added(keep, got):
    return (keep.astype(jnp.float32) + got.astype(jnp.float32)).astype(keep.dtype)


def added_four(keep, second, first, both):
    wide = lambda array: array.astype(jnp.float32)
    return ((wide(keep) + wide(first)) + (wide(second) + wide(both))).astype(keep.dtype)


def cut_rows(array, half):
    middle = array.shape[-2] // 2
    return array[..., half * middle : (half + 1) * middle, :]


def folded(keep, got, kind):
    if kind == "rows":
        return [added(cut_rows(keep, half), cut_rows(got, half)) for half in range(2)]
    if kind == "blocks":
        return [added(keep[0], got[0]), added(keep[1], got[1])]
    if isinstance(kind, int):
        total = added(keep, got) if not isinstance(got, (list, tuple)) else added_four(keep, *got)
        return [
            jnp.concatenate([total[: kind // 2], total[kind:]]),
            jnp.concatenate([total[kind // 2 : kind], total[kind:]]),
        ]
    if kind == "turned":
        return [jnp.stack([added(keep[0], got[1]), added(keep[1], got[0])])]
    return [added(keep, got)]


def fold_kernel(jobs, *refs):
    refs = list(refs)
    values = [jax.tree.map(lambda _: refs.pop(0)[...], job[:2]) for job in jobs]
    for (keep, got), (_, _, kind) in zip(values, jobs, strict=True):
        for value in folded(keep, got, kind):
            refs.pop(0)[...] = value


def fold_all(jobs):
    arrays = jax.tree.leaves([job[:2] for job in jobs])
    shapes = [jax.eval_shape(functools.partial(folded, kind=kind), keep, got) for keep, got, kind in jobs]
    flat = [shape for group in shapes for shape in group]
    blank = [(*jax.tree.map(lambda _: 0, job[:2]), job[2]) for job in jobs]
    outs = pl.pallas_call(
        functools.partial(fold_kernel, blank),
        out_shape=flat,
        compiler_params=room,
        cost_estimate=cost(sum(a.size for a in arrays), sum(4 * a.size for a in arrays)),
        name="fold_all",
    )(*arrays)
    out = []
    for group in shapes:
        out.append(outs[: len(group)])
        outs = outs[len(group) :]
    return out


def split_kernel(*refs):
    further = len(refs) > 10
    keep_low, keep_high, keep_out, got_low, got_high, got_out = refs[:6]
    in_keep, in_send, out_keep, out_send = refs[-4:]
    columns = keep_out.shape[3]
    in_keep[...] = added(keep_low[0], got_low[0])
    in_send[...] = added(keep_high[0], got_high[0])
    for half, out in enumerate((out_keep, out_send)):
        out[:, :columns] = added(keep_out[0, half], got_out[0, half])
        if further:
            out[:, columns:] = added(refs[6][half], refs[7][half])


def split_cores(keep, got, further=(), steps=4):
    rows, columns = keep.shape[2:]
    few, many = rows // 2 // steps, rows // steps
    low_rows = pl.BlockSpec((1, 2, few, columns), lambda i: (0, 0, i, 0))
    high_rows = pl.BlockSpec((1, 2, few, columns), lambda i: (0, 0, i + steps, 0))
    out_rows = pl.BlockSpec((1, 2, many, columns), lambda i: (1, 0, i, 0))
    total = columns + (further[0].shape[2] if further else 0)
    two = pl.BlockSpec((2, few, columns), lambda i: (0, i, 0))
    one = pl.BlockSpec((many, total), lambda i: (i, 0))
    pair = jax.ShapeDtypeStruct((2, rows // 2, columns), keep.dtype)
    single = jax.ShapeDtypeStruct((rows, total), keep.dtype)
    return pl.pallas_call(
        split_kernel,
        grid=(steps,),
        in_specs=[low_rows, high_rows, out_rows] * 2
        + [pl.BlockSpec((2, many, total - columns), lambda i: (0, i, 0))] * len(further),
        out_specs=[two, two, one, one],
        out_shape=[pair, pair, single, single],
        compiler_params=large,
        cost_estimate=cost(keep.size, 6 * keep.size),
        name="split_cores",
    )(keep, keep, keep, got, got, got, *further)


def reduce_rows(keep, send):
    steps = [1] + dp_masks()[::-1]
    for mask in steps[:-1]:
        keep, send = yield keep, swap(send, "dp", mask), "rows"
    (keep,) = yield keep, swap(send, "dp", steps[-1]), "sum"
    (keep,) = yield keep, swap(keep, "tok", 2), "turned"
    near, far = yield keep, swap(keep, "tok", 1), "none"
    return near, far


def reduce_columns(keep, send):
    keep, send = yield keep, swap(send, "tok", 2), "rows"
    steps = [1] + dp_masks()[::-1]
    for mask in steps[:-1]:
        keep, send = yield keep, swap(send, "dp", mask), "rows"
    (keep,) = yield keep, swap(send, "dp", steps[-1]), "sum"
    keep, others = yield keep, [swap(keep, "tok", q) for q in range(1, 4)], "none"
    return [keep, *others]


def reduce_misc(stem_rows, keep, far, near, both):
    arrived = [swap(array, "tok", mask) for mask, array in ((2, far), (1, near), (3, both))]
    keep, send = yield keep, arrived, stem_rows
    steps = [1] + dp_masks()[::-1]
    for mask in steps[:-1]:
        stem_rows //= 2
        keep, send = yield keep, swap(send, "dp", mask), stem_rows
    (keep,) = yield keep, swap(send, "dp", steps[-1]), "sum"
    block = keep[: stem_rows // 2]
    rest, others = yield keep, [swap(block, "tok", q) for q in range(1, 4)], "none"
    return [block, *others], rest[stem_rows // 2 :]


def sum_over(array, steps):
    for axis, mask in steps:
        (array,) = yield array, swap(array, axis, mask), "sum"
    return array


class Chain:
    def __init__(self, moves):
        self.moves, self.result = moves, None
        self.state = next(moves)

    def push(self, state):
        try:
            self.state = self.moves.send(state)
        except StopIteration as end:
            self.state, self.result = None, end.value


def advance(chains, *others):
    chains = [chain for chain in chains if chain.state is not None]
    states, others = fence([chain.state[:2] for chain in chains], others)
    jobs = []
    for chain, (keep, got) in zip(chains, states, strict=True):
        kind = chain.state[2]
        small = keep.size <= FOLD_MAX and kind != "none"
        if (kind == "rows" and keep.shape[-2] % 32) or (isinstance(kind, int) and kind % 32):
            small = False
        if small:
            jobs.append((chain, keep, got, kind))
    results = dict(
        zip([id(job[0]) for job in jobs], fold_all([job[1:] for job in jobs]) if jobs else [], strict=True)
    )
    others, fenced = fence(others, results)
    results = fenced
    for chain, (keep, got) in zip(chains, states, strict=True):
        kind = chain.state[2]
        if id(chain) in results:
            chain.push(results[id(chain)])
        elif kind == "none":
            chain.push((keep, got))
        else:
            chain.push(folded(keep, got, kind))
    return others


def exchanged(blocks):
    row = lax.axis_index("tok")
    blocks = [jnp.where((row & 1) == 1, blocks[k ^ 1], blocks[k]) for k in range(4)]
    return [jnp.where((row & 2) == 2, blocks[k ^ 2], blocks[k]) for k in range(4)]


def ordered(blocks, axis):
    return jnp.concatenate(exchanged([blocks[0], blocks[2], blocks[1], blocks[3]]), axis)


def quarter(array, axis):
    size = array.shape[axis] // lax.axis_size("tok")
    return lax.dynamic_slice_in_dim(array, lax.axis_index("tok") * size, size, axis)


def moments(weight, gradient, first, second, decay_rate):
    first_new = beta_one * first + (1 - beta_one) * gradient
    second_new = beta_two * second + (1 - beta_two) * gradient * gradient
    scale_one, scale_two = 1 / (1 - beta_one**STEP), 1 / (1 - beta_two**STEP)
    update = scale_one * first_new / (jnp.sqrt(scale_two * second_new) + epsilon) + decay_rate * weight
    return (first_new, second_new, update)


def row_squares(array, groups):
    flat = array.reshape(groups, -1)
    return jnp.sum(flat * flat, 1)


def renew(weight, update, weight_norm, update_norm, groups):
    trust = weight_norm / (update_norm + epsilon)
    return weight - learn_rate * (trust[:, None] * update.reshape(groups, -1)).reshape(weight.shape)


def body(
    images,
    partner,
    lam,
    labels,
    counts,
    class_weights,
    stem_w,
    stem_m,
    stem_v,
    tok_w,
    tok_m,
    tok_v,
    chan_w,
    chan_m,
    chan_v,
    head_w,
    head_m,
    head_v,
    vec_w,
    vec_m,
    vec_v,
    hb_w,
    hb_m,
    hb_v,
):
    count_dp = lax.axis_size("dp")
    count_tok = lax.axis_size("tok")
    device_row = lax.axis_index("dp")
    token_row = lax.axis_index("tok")
    patches = images.shape[0]
    all_patches = patches * count_tok
    per_device = images.shape[1]
    per_tok = per_device // count_tok
    classes_all = hb_w.shape[0]
    class_pad = -classes_all % (count_tok * LANES)
    width = vec_w.shape[1]
    each = all_patches + -all_patches % SUBLANES

    masks = dp_masks()
    batches = per_device // IMG_MB
    start = device_row * per_device
    own_parts, owners, shares = [], [], []
    for batch in range(batches):
        at = start + batch * IMG_MB
        own_parts.append(images[:, batch * IMG_MB : (batch + 1) * IMG_MB])
        owners.append(lax.dynamic_slice_in_dim(partner, at, IMG_MB, 0) % IMG_MB)
        shares.append(lax.dynamic_slice_in_dim(lam, at, IMG_MB, 0))
    device = token_row.astype(jnp.int32)[None]

    def mixed_pieces(batch, incoming):
        sends = mix(owners[batch], shares[batch], device, own_parts[batch], incoming, count_tok)
        return [sends[0]] + [swap(sends[q], "tok", q) for q in range(1, count_tok)]

    chan_low = quarter(chan_w.astype(low), 3)
    shard, size = chan_low.shape[2:]
    order = row_order()
    rows = jnp.asarray(order, jnp.int32) ^ device_row
    column_source = (rows[:, None] * shard + jnp.arange(shard, dtype=jnp.int32)[None, :]).reshape(1, width)
    ends = jnp.concatenate([stem_w.astype(low).T, jnp.pad(head_w.astype(low), ((0, 0), (0, class_pad)))], 1)
    ends = lax.all_gather(quarter(ends, 0), ("dp", "tok"))
    pixels = stem_w.shape[0]
    later = chan_low[1].reshape(2 * shard, size)

    later = lax.all_gather(later, ("dp", "tok")).reshape(count_dp, count_tok, -1, size)

    vectors = relative_vectors(vec_w, column_source)
    numbers = jnp.arange(classes_all + class_pad, dtype=jnp.int32)
    numbers = jnp.where(numbers < classes_all, numbers, -1)[None]
    bias = jnp.pad(hb_w, (0, class_pad))[None]
    own_hot = (labels[:, None] == jnp.arange(classes_all, dtype=jnp.int32)[None, :]).astype(jnp.float32)
    other_labels = jnp.take(labels, partner)
    own_weight = jnp.sum(own_hot * class_weights[None, :], 1)
    other_weight = jnp.take(own_weight, partner)
    live = (
        (jnp.arange(IMG_MB, dtype=jnp.int32)[None, :] < counts.reshape(-1)[:, None])
        .astype(jnp.float32)
        .reshape(-1)
    )
    weights = live * (lam * own_weight + (1 - lam) * other_weight)
    total = jnp.sum(weights)
    group = IMG_MB // count_tok

    def row_of(array):
        return jnp.concatenate(
            [
                lax.dynamic_slice_in_dim(array, start + batch * IMG_MB + token_row * group, group, 0)
                for batch in range(batches)
            ]
        )[:, None]

    image_rows = [row_of(array) for array in (labels, other_labels, lam, weights, weights / total)]

    blocks = [chan_low[0, 0], chan_low[0, 1]]
    tok_low = jnp.swapaxes(tok_w, 2, 3).astype(low)
    partner_mask = count_dp // 2
    incoming = swap(own_parts[0], "dp", partner_mask)
    for step, mask in enumerate(masks):
        got = swap(packed(blocks), "dp", mask)
        if step == 0:
            blocks, got, tok_far, own_parts[1], incoming = fence(
                blocks, got, swap(tok_low, "tok", 2), own_parts[1], incoming
            )
            pieces = mixed_pieces(0, incoming)
            tok_half = jnp.concatenate([tok_low, tok_far], 2)
            tok_near = swap(tok_half, "tok", 1)
        elif step == 1:
            blocks, got, tok_near, own_parts[1], vectors, image_rows, pieces = fence(
                blocks, got, tok_near, own_parts[1], vectors, image_rows, pieces
            )
        else:
            blocks, got = fence(blocks, got)
        blocks = doubled(blocks, got)
    tok_turn = jnp.concatenate([tok_half, tok_near], 2)
    tok_turn = jnp.pad(tok_turn, ((0, 0), (0, 0), (0, 0), (0, each - all_patches)))
    tok_all = jnp.swapaxes(tok_turn, 2, 3)

    incoming_two = swap(own_parts[1], "dp", partner_mask)
    first, second = blocks
    first_low, second_far = swap(first, "dp", 1), swap(second, "tok", 2)
    first, second, first_low, second_far, incoming_two, tok_all, tok_turn = fence(
        first, second, first_low, second_far, incoming_two, tok_all, tok_turn
    )
    more = mixed_pieces(1, incoming_two)
    firsts, seconds = jnp.stack([first, first_low]), jnp.stack([second, second_far])
    firsts_far, seconds_low = swap(firsts, "tok", 2), swap(seconds, "dp", 1)
    firsts, seconds, firsts_far, seconds_low, pieces, more = fence(
        firsts, seconds, firsts_far, seconds_low, pieces, more
    )
    source_zero = Pieces(
        [firsts, firsts_far, swap(firsts, "tok", 1), swap(firsts_far, "tok", 1)],
        [seconds, seconds_low, swap(seconds, "tok", 1), swap(seconds_low, "tok", 1)],
    )
    if shard % 16:
        many = 96 // shard
        groups = count_dp // many
        later = jnp.take(later, rows, axis=0).reshape(groups, many, count_tok, 2, shard, size)
        later = later.transpose(0, 2, 3, 1, 4, 5).reshape(groups, count_tok, 2 * many * shard, size)
        ends = jnp.take(ends.reshape(count_dp, shard, -1), rows, axis=0).reshape(groups, many * shard, -1)
        spots = jnp.arange(groups, dtype=jnp.int32)
        source_one = Gathered(later, spots, device, many * shard)
    else:
        spots = rows
        ends = ends.reshape(count_dp, shard, -1)
        source_one = Gathered(later, spots, device, shard)

    gains = [vectors[1 + 4 * layer : 5 + 4 * layer] for layer in range(LAYERS)]
    mixed, stem_state = stem(device, spots, pieces + more, ends, vectors, each * per_tok)
    middle_zero, before_zero = token_forward(stem_state, gains[0], tok_turn[0, 0], tok_all[0, 1])
    first_state, inner_zero = channel_forward(middle_zero, gains[0], source_zero)
    middle_one, before_one = token_forward(first_state, gains[1], tok_turn[1, 0], tok_all[1, 1])
    second_state, inner_one = channel_forward(middle_one, gains[1], source_one)
    gradient, last_part, head_grads, bias_part, loss_local = head_step(
        device, spots, second_state, vectors[NV - 2 :], ends, bias, numbers, *image_rows, all_patches, pixels
    )

    head_got = swap(head_grads[2:], "tok", 1)
    send, partial, _ = channel_backward(gradient, middle_one, gains[1], inner_one, source_one)
    got = swap(send, "tok", 1)
    keep, gradient, second_one = channel_backward(gradient, middle_one, gains[1], inner_one, source_one, partial)
    in_keep, in_send, out_keep, out_send = split_cores(keep, got, (head_grads[:2], head_got))
    in_keep, in_send, out_keep, out_send, gradient = fence(in_keep, in_send, out_keep, out_send, gradient)
    chains_one = [Chain(reduce_rows(in_keep, in_send)), Chain(reduce_columns(out_keep, out_send))]
    gradient, first_one, *token_one = token_backward(
        gradient, first_state, gains[1], before_one, tok_all[1, 0], tok_turn[1, 1]
    )
    send, partial, _ = channel_backward(gradient, middle_zero, gains[0], inner_zero, source_zero)
    send, partial, gradient = advance(chains_one, send, partial, gradient)
    got = swap(send, "tok", 1)
    keep, gradient, second_zero = channel_backward(gradient, middle_zero, gains[0], inner_zero, source_zero, partial)
    in_keep, in_send, out_keep, out_send = split_cores(keep, got)
    in_keep, in_send, out_keep, out_send, gradient = advance(
        chains_one, in_keep, in_send, out_keep, out_send, gradient
    )
    chains_zero = [Chain(reduce_rows(in_keep, in_send)), Chain(reduce_columns(out_keep, out_send))]
    gradient, first_zero, *token_zero = token_backward(
        gradient, stem_state, gains[0], before_zero, tok_all[0, 0], tok_turn[0, 1]
    )
    stem_grads, stem_bias = stem_backward(device, gradient, mixed)
    misc = gather_misc(
        column_source,
        stem_grads,
        token_zero + token_one,
        [stem_bias, first_zero, second_zero, first_one, second_one, last_part],
        bias_part,
        loss_local,
    )
    misc = advance(chains_one + chains_zero, *misc)
    misc_chain = Chain(reduce_misc(width, *misc))
    dp_steps = [("dp", mask) for mask in [1] + dp_masks()[::-1]]
    everything = chains_one + chains_zero + [misc_chain]
    earlier = []
    while any(chain.state is not None for chain in everything):
        if not earlier and all(chain.result is not None for chain in chains_one):
            *earlier, squares_one = channel_step(
                1, device, chan_w, chan_m, chan_v, *[chain.result for chain in chains_one], []
            )
            earlier = list(advance(everything, *earlier))
        else:
            advance(everything)
    chan_first, chan_second, chan_update, squares_zero = channel_step(
        0, device, chan_w, chan_m, chan_v, *[chain.result for chain in chains_zero], earlier
    )
    stem_parts, misc = misc_chain.result
    hidden = tok_w.shape[3]
    token_grad = misc[: 4 * hidden].reshape(LAYERS, 2, hidden, MISC)[..., :all_patches].astype(jnp.float32)
    small = misc[4 * hidden :].astype(jnp.float32)
    blocks = width // MISC
    vector_grad = jnp.concatenate([small[16 * j : 16 * j + NV] for j in range(blocks)], 1)
    bias_grad = small[16 * blocks : 16 * blocks + numbers.shape[1] // MISC].reshape(-1)[:classes_all]
    loss_total = small[16 * blocks + numbers.shape[1] // MISC, 0]
    turned = lambda array: jnp.swapaxes(array, -1, -2)
    tok_w, tok_m, tok_v, stem_w, stem_m, stem_v = [turned(a) for a in (tok_w, tok_m, tok_v, stem_w, stem_m, stem_v)]
    placed = lambda parts: [parts[0], parts[2], parts[1], parts[3]]
    head_parts = [part[:, size:] for part in chains_one[1].result]
    head_grad = ordered(placed(head_parts), 1)[:, :classes_all].astype(jnp.float32)
    stem_parts = [part[:, : pixels // count_tok] for part in stem_parts]
    stem_grad = ordered(placed(stem_parts), 1).astype(jnp.float32)
    stem_first, stem_second, stem_update = moments(stem_w, stem_grad, stem_m, stem_v, weight_decay)
    tok_first, tok_second, tok_update = moments(tok_w, token_grad, tok_m, tok_v, weight_decay)
    head_first, head_second, head_update = moments(head_w, head_grad, head_m, head_v, weight_decay)
    vec_first, vec_second, vec_update = moments(vec_w, vector_grad, vec_m, vec_v, 0.0)
    hb_first, hb_second, hb_update = moments(hb_w, bias_grad, hb_m, hb_v, 0.0)
    matrix_groups = 2 * LAYERS
    squares = jnp.stack([squares_zero, squares_one])
    pair_of = lambda array, other, groups: jnp.stack([row_squares(array, groups), row_squares(other, groups)])
    token_squares = Chain(sum_over(pair_of(tok_w, tok_update, matrix_groups), [("tok", 1), ("tok", 2)]))
    while token_squares.state is not None:
        advance([token_squares])
    shard_squares = jnp.concatenate(
        [
            pair_of(stem_w, stem_update, 1),
            squares.transpose(2, 0, 1).reshape(2, matrix_groups),
            pair_of(head_w, head_update, 1),
        ],
        1,
    )
    norm_chain = Chain(sum_over(shard_squares, dp_steps))
    while norm_chain.state is not None:
        advance([norm_chain])
    weight_total, update_total = jnp.concatenate(
        [norm_chain.result[:, :1], token_squares.result, norm_chain.result[:, 1:]], 1
    )
    weight_norms = jnp.sqrt(weight_total)
    update_norms = jnp.sqrt(update_total)
    stem_end = 1
    tok_end = 1 + matrix_groups
    chan_end = 1 + 2 * matrix_groups
    stem_new = renew(stem_w, stem_update, weight_norms[0:stem_end], update_norms[0:stem_end], 1)
    tok_new = renew(
        tok_w,
        tok_update,
        weight_norms[stem_end:tok_end],
        update_norms[stem_end:tok_end],
        matrix_groups,
    )
    chan_trust = weight_norms[tok_end:chan_end] / (update_norms[tok_end:chan_end] + epsilon)
    chan_new, chan_new_low = channel_renew(chan_trust.reshape(LAYERS, 2), chan_w, chan_update)
    head_new = renew(head_w, head_update, weight_norms[chan_end:], update_norms[chan_end:], 1)
    vec_weight_norm = jnp.sqrt(row_squares(vec_w, NV))
    vec_update_norm = jnp.sqrt(row_squares(vec_update, NV))
    hb_weight_norm = jnp.sqrt(row_squares(hb_w, 1))
    hb_update_norm = jnp.sqrt(row_squares(hb_update, 1))
    vec_new = renew(vec_w, vec_update, vec_weight_norm, vec_update_norm, NV)
    hb_new = renew(hb_w, hb_update, hb_weight_norm, hb_update_norm, 1)
    stem_new, stem_first, stem_second, tok_new, tok_first, tok_second = [
        turned(a) for a in (stem_new, stem_first, stem_second, tok_new, tok_first, tok_second)
    ]
    norms = jnp.stack(
        [
            jnp.concatenate([weight_norms, vec_weight_norm, hb_weight_norm]),
            jnp.concatenate([update_norms, vec_update_norm, hb_update_norm]),
        ],
        1,
    )
    loss_parts = jnp.stack([loss_total, total])
    return (
        stem_new,
        stem_first,
        stem_second,
        tok_new,
        tok_first,
        tok_second,
        chan_new,
        chan_first,
        chan_second,
        head_new,
        head_first,
        head_second,
        vec_new,
        vec_first,
        vec_second,
        hb_new,
        hb_first,
        hb_second,
        stem_new.astype(jnp.bfloat16),
        tok_new.astype(jnp.bfloat16),
        chan_new_low,
        head_new.astype(jnp.bfloat16),
        norms,
        loss_parts,
    )


def solution(mesh):
    in_specs = (
        P("tok", "dp", None),
        P(),
        P(),
        P(),
        P(),
        P(),
        P(None, "dp"),
        P(None, "dp"),
        P(None, "dp"),
        P(None, None, None, "tok"),
        P(None, None, None, "tok"),
        P(None, None, None, "tok"),
        P(None, None, "dp", None),
        P(None, None, "dp", None),
        P(None, None, "dp", None),
        P("dp", None),
        P("dp", None),
        P("dp", None),
        P(),
        P(),
        P(),
        P(),
        P(),
        P(),
    )
    out_specs = (
        P(None, "dp"),
        P(None, "dp"),
        P(None, "dp"),
        P(None, None, None, "tok"),
        P(None, None, None, "tok"),
        P(None, None, None, "tok"),
        P(None, None, "dp", None),
        P(None, None, "dp", None),
        P(None, None, "dp", None),
        P("dp", None),
        P("dp", None),
        P("dp", None),
        P(),
        P(),
        P(),
        P(),
        P(),
        P(),
        P(None, "dp"),
        P(None, None, None, "tok"),
        P(None, None, "dp", None),
        P("dp", None),
        P(),
        P(),
    )
    return jax.shard_map(body, mesh=mesh, in_specs=in_specs, out_specs=out_specs, check_vma=False)
```

```python
import functools

import jax
import jax.numpy as jnp
from jax import lax
from jax.experimental import pallas as pl
from jax.experimental.pallas import tpu as pltpu
from jax.sharding import PartitionSpec as P

LAYERS = 2
STEP = 5
IMG_MB = 8
NV = 11
LANES = 128
SUBLANES = 8
FOLD_MAX = 1200000
MISC = 256
SMALL = 64

low = jnp.bfloat16
beta_one = 0.9
beta_two = 0.999
epsilon = 1e-06
weight_decay = 0.01
learn_rate = 0.3
root = 0.7978845608028654
cubic = 0.044715
room = pltpu.CompilerParams(vmem_limit_bytes=44 * 1024 * 1024)
places = (0, 2, 1, 3)
large = pltpu.CompilerParams(vmem_limit_bytes=60 * 1024 * 1024)
slim = pltpu.CompilerParams(vmem_limit_bytes=36 * 1024 * 1024)
lean = pltpu.CompilerParams(vmem_limit_bytes=24 * 1024 * 1024)


def dot(left, right, contract=(1, 0)):
    return lax.dot_general(
        left, right, (((contract[0],), (contract[1],)), ((), ())), preferred_element_type=jnp.float32
    )


def gelu(values):
    return 0.5 * values * (1 + jnp.tanh(root * values * (1 + cubic * values * values)))


def gelu_both(values):
    square = values * values
    bend = jnp.tanh(root * values * (1 + cubic * square))
    half = 0.5 * (1 + bend)
    slope = half + 0.5 * values * (1 - bend * bend) * (root * (1 + 3 * cubic * square))
    return values * half, slope


def centred(values):
    centre = values - jnp.mean(values, -1, keepdims=True)
    inverse = lax.rsqrt(jnp.mean(centre * centre, -1, keepdims=True) + 1e-06)
    return centre * inverse, inverse


def centred_back(scaled, hat, inverse):
    return inverse * (
        scaled - jnp.mean(scaled, -1, keepdims=True) - hat * jnp.mean(scaled * hat, -1, keepdims=True)
    )


def whole(array):
    zeros = (0,) * array.ndim
    return pl.BlockSpec(array.shape, lambda *_: zeros)


def cost(flops, bytes_accessed, powers=0):
    return pl.CostEstimate(flops=flops, bytes_accessed=bytes_accessed, transcendentals=powers)


def token_forward_kernel(state, gains, token_in, token_out, middle, before):
    hat, _ = centred(state[...])
    normed = (hat * gains[0:1] + gains[1:2]).astype(low)
    pre = dot(token_in[...], normed)
    before[0] = pre.astype(low)
    middle[...] = state[...] + dot(token_out[...], gelu(pre).astype(low))


def token_forward(state, gains, token_in, token_out):
    hidden, rows = token_in.shape
    count, width = state.shape[0] // rows, state.shape[1]
    one = pl.BlockSpec((rows, width), lambda i: (i, 0))
    return pl.pallas_call(
        token_forward_kernel,
        grid=(count,),
        in_specs=[one, whole(gains), whole(token_in), whole(token_out)],
        out_specs=[one, pl.BlockSpec((1, hidden, width), lambda i: (i, 0, 0))],
        out_shape=[
            jax.ShapeDtypeStruct(state.shape, jnp.float32),
            jax.ShapeDtypeStruct((count, hidden, width), low),
        ],
        compiler_params=lean,
        cost_estimate=cost(4 * count * rows * hidden * width, 10 * state.size, 0),
        name="token_forward",
    )(state, gains, token_in, token_out)


def block_copies(spots, blocks, lanes, held, sems):
    rows = blocks.shape[1]
    return [
        pltpu.make_async_copy(blocks.at[spots[i], :, lanes], held.at[pl.ds(i * rows, rows)], sems.at[i])
        for i in range(blocks.shape[0])
    ]


def hbm(arrays):
    return [pl.BlockSpec(memory_space=pltpu.HBM)] * len(arrays)


scalars = pl.BlockSpec(memory_space=pltpu.SMEM)


class Pieces:
    def __init__(self, first, second):
        self.arrays = [*first, *second]
        self.specs = hbm(self.arrays)
        self.width = 2 * second[0].shape[1]
        self.size = second[0].shape[2]
        self.sems = 4

    def copies(self, refs, held_in, held_out, sems, slot, place):
        half = self.width // 2
        out = []
        for side in range(2):
            rows = pl.ds(side * half, half)
            first = refs[place].at[side, pl.ds(0, half)]
            second = refs[4 + place // 2 * 2 + side].at[place % 2]
            out.append(pltpu.make_async_copy(first, held_in.at[slot, rows], sems.at[slot, side]))
            out.append(pltpu.make_async_copy(second, held_out.at[slot, rows], sems.at[slot, 2 + side]))
        return out


class Gathered:
    def __init__(self, array, shards, device, rows):
        self.arrays = [shards, device, array]
        self.specs = [scalars, scalars] + hbm([array])
        self.blocks, self.rows, self.size = array.shape[0], rows, array.shape[3]
        self.width = self.blocks * self.rows
        self.sems = 2 * self.blocks

    def copies(self, refs, held_in, held_out, sems, slot, place):
        shards, device, array = refs
        quarter_at = device[0] ^ places[place]
        out = []
        for block in range(self.blocks):
            rows = pl.ds(block * self.rows, self.rows)
            for way, held in enumerate((held_in, held_out)):
                out.append(
                    pltpu.make_async_copy(
                        array.at[shards[block], quarter_at, pl.ds(way * self.rows, self.rows)],
                        held.at[slot, rows],
                        sems.at[slot, 2 * block + way],
                    )
                )
        return out


def channel_forward_kernel(source, middle, gains, *rest):
    refs = rest[: len(source.arrays)]
    result, inner, normed, held_in, held_out, sems = rest[-6:]
    step = pl.program_id(0)

    @pl.when(step == 0)
    def _():
        for q in range(4):
            for copy in source.copies(refs, held_in, held_out, sems, q, q):
                copy.start()
        hat, _ = centred(middle[...])
        normed[...] = (hat * gains[2:3] + gains[3:4]).astype(low)
        result[...] = middle[...]

    for q in range(4):

        @pl.when(step == q)
        def _(q=q):
            for copy in source.copies(refs, held_in, held_out, sems, q, q):
                copy.wait()
            product = dot(normed[...], held_in[q])
            inner[...] = product.astype(low)
            result[...] += dot(gelu(product).astype(low), held_out[q], (1, 1))


def channel_forward(middle, gains, source):
    rows, width = middle.shape
    size = source.size
    total = 4 * size
    return pl.pallas_call(
        functools.partial(channel_forward_kernel, source),
        grid=(4,),
        in_specs=[whole(middle), whole(gains)] + source.specs,
        out_specs=[whole(middle), pl.BlockSpec((rows, size), lambda i: (0, i))],
        out_shape=[
            jax.ShapeDtypeStruct(middle.shape, jnp.float32),
            jax.ShapeDtypeStruct((rows, total), low),
        ],
        scratch_shapes=[
            pltpu.VMEM(middle.shape, low),
            pltpu.VMEM((4, width, size), low),
            pltpu.VMEM((4, width, size), low),
            pltpu.SemaphoreType.DMA((4, source.sems)),
        ],
        compiler_params=slim,
        cost_estimate=cost(4 * rows * width * total, 4 * width * total + 2 * rows * total),
        name="channel_forward",
    )(middle, gains, *source.arrays)


def channel_backward_kernel(source, last, gradient, middle, gains, inner, *rest):
    if last:
        before, rest = rest[0], rest[1:]
    refs = rest[: len(source.arrays)]
    grads, total, grad_vectors, grad_low, grad_turn, normed_turn, held_in, held_out, sems = rest[-9:]
    step = pl.program_id(0)
    first = 0 if last else 2

    @pl.when(step == 0)
    def _():
        for q in range(2):
            for copy in source.copies(refs, held_in, held_out, sems, q, first + q):
                copy.start()
        grad_low[...] = gradient[...].astype(low)
        grad_turn[...] = gradient[...].T.astype(low)
        hat, _ = centred(middle[...])
        normed_turn[...] = (hat * gains[2:3] + gains[3:4]).T.astype(low)
        total[...] = before[...] if last else jnp.zeros_like(total)

    for q in range(2):

        @pl.when(step == q)
        def _(q=q):
            for copy in source.copies(refs, held_in, held_out, sems, q, first + q):
                copy.wait()
            active, slope = gelu_both(inner[...].astype(jnp.float32))
            grads[1, 0] = dot(grad_turn[...], active.astype(low)).astype(low)
            grad_inner = (slope * dot(grad_low[...], held_out[q])).astype(low)
            grads[0, 0] = dot(normed_turn[...], grad_inner).astype(low)
            total[...] += dot(grad_inner, held_in[q], (1, 1))

    if last:

        @pl.when(step == 1)
        def _():
            hat, inverse = centred(middle[...])
            upstream = total[...]
            grad_vectors[0:1] = jnp.sum(upstream * hat, 0, keepdims=True)
            grad_vectors[1:2] = jnp.sum(upstream, 0, keepdims=True)
            total[...] = gradient[...] + centred_back(upstream * gains[2:3], hat, inverse)


def channel_backward(gradient, middle, gains, inner, source, before=None):
    rows, width = middle.shape
    size = source.size
    last = before is not None
    shift = 0 if last else 2
    carried = [before] if last else []
    total = 2 * size
    return pl.pallas_call(
        functools.partial(channel_backward_kernel, source, last),
        grid=(2,),
        in_specs=[whole(middle), whole(middle), whole(gains), pl.BlockSpec((rows, size), lambda i: (0, i + shift))]
        + [whole(array) for array in carried]
        + source.specs,
        out_specs=[
            pl.BlockSpec((2, 1, width, size), lambda i: (0, i, 0, 0)),
            whole(middle),
            pl.BlockSpec((2, width), lambda i: (0, 0)),
        ],
        out_shape=[
            jax.ShapeDtypeStruct((2, 2, width, size), low),
            jax.ShapeDtypeStruct(middle.shape, jnp.float32),
            jax.ShapeDtypeStruct((2, width), jnp.float32),
        ],
        scratch_shapes=[
            pltpu.VMEM((rows, width), low),
            pltpu.VMEM((width, rows), low),
            pltpu.VMEM((width, rows), low),
            pltpu.VMEM((2, width, size), low),
            pltpu.VMEM((2, width, size), low),
            pltpu.SemaphoreType.DMA((2, source.sems)),
        ],
        compiler_params=room,
        cost_estimate=cost(8 * rows * width * total, 8 * width * total + 2 * rows * total),
        name="channel_backward",
    )(gradient, middle, gains, inner, *carried, *source.arrays)


def step_kernel(device, weight, mean, power, near, far, *rest):
    apart, (mean_new, power_new, update, sums) = rest[:4], rest[-4:]
    way = pl.program_id(0)
    size = near.shape[2]
    weight_part, update_part = 0.0, 0.0
    for a in range(4):
        rel = device[0] ^ a
        lanes = slice(a * size, (a + 1) * size)
        values = [
            jnp.where(way == 0, one.astype(jnp.float32), two[...].astype(jnp.float32))
            for one, two in zip((near[0], far[0], near[1], far[1]), apart, strict=True)
        ]
        grad = jnp.where(
            rel < 2, jnp.where(rel == 0, values[0], values[1]), jnp.where(rel == 2, values[2], values[3])
        )
        value = weight[0, 0, :, lanes]
        mean_next, power_next, change = moments(
            value, grad, mean[0, 0, :, lanes], power[0, 0, :, lanes], weight_decay
        )
        mean_new[0, 0, :, lanes] = mean_next
        power_new[0, 0, :, lanes] = power_next
        update[0, 0, :, lanes] = change
        weight_part += jnp.sum(jnp.sum(value * value, 0, keepdims=True))
        update_part += jnp.sum(jnp.sum(change * change, 0, keepdims=True))

    @pl.when(pl.program_id(1) == 0)
    def _():
        sums[way, 0] = weight_part
        sums[way, 1] = update_part

    @pl.when(pl.program_id(1) > 0)
    def _():
        sums[way, 0] += weight_part
        sums[way, 1] += update_part


def channel_step(layer, device, weight, mean, power, chain_in, chain_out, earlier):
    near, far = chain_in
    rows, size = near.shape[1:]
    columns = weight.shape[3]
    chunk = 32 if rows % 32 == 0 else rows
    block = pl.BlockSpec((1, 1, chunk, columns), lambda w, i: (layer, w, i, 0))
    two = pl.BlockSpec((2, chunk, size), lambda w, i: (0, i, 0))
    one = pl.BlockSpec((chunk, size), lambda w, i: (i, 0))
    shape = jax.ShapeDtypeStruct(weight.shape, jnp.float32)
    return pl.pallas_call(
        step_kernel,
        grid=(2, rows // chunk),
        in_specs=[scalars, block, block, block, two, two, one, one, one, one] + hbm(earlier),
        out_specs=[block, block, block, scalars],
        out_shape=[shape, shape, shape, jax.ShapeDtypeStruct((2, 2), jnp.float32)],
        input_output_aliases={10 + i: i for i in range(len(earlier))},
        compiler_params=large,
        cost_estimate=cost(40 * near.size, 104 * near.size),
        name="channel_step",
    )(device, weight, mean, power, near, far, *chain_out, *earlier)


def ends_kernel(
    device, squares_zero, squares_one, stem_w, stem_m, stem_v, head_w, head_m, head_v, *rest
):
    stem_grads, head_grads, outs, sums = rest[:4], rest[4:8], rest[8:14], rest[14]

    def step(sources, grads, first, results):
        weight, mean, power = sources
        mean_new, power_new, update = results
        parts = [grad[:, first:].astype(jnp.float32) for grad in grads]
        size = -(-weight.shape[1] // (4 * 64)) * 64
        weight_part, update_part = 0.0, 0.0
        for a in range(4):
            rel = device[0] ^ a
            lanes = slice(a * size, min((a + 1) * size, weight.shape[1]))
            cut = [part[:, : lanes.stop - lanes.start] for part in parts]
            grad = jnp.where(rel < 2, jnp.where(rel == 0, cut[0], cut[1]), jnp.where(rel == 2, cut[2], cut[3]))
            value = weight[:, lanes]
            mean_new[:, lanes], power_new[:, lanes], change = moments(
                value, grad, mean[:, lanes], power[:, lanes], weight_decay
            )
            update[:, lanes] = change
            weight_part += jnp.sum(jnp.sum(value * value, 0, keepdims=True), 1, keepdims=True)
            update_part += jnp.sum(jnp.sum(change * change, 0, keepdims=True), 1, keepdims=True)
        return weight_part, update_part

    stem_part = step((stem_w, stem_m, stem_v), stem_grads, 0, outs[:3])
    head_part = step((head_w, head_m, head_v), head_grads, head_grads[0].shape[1] - MISC, outs[3:])
    lane = lax.broadcasted_iota(jnp.int32, (1, LANES), 1)
    sums[...] = jnp.zeros_like(sums)
    for kind in range(2):
        values = [stem_part[kind]]
        values += [squares[way, kind] for squares in (squares_zero, squares_one) for way in range(2)]
        values += [head_part[kind]]
        sums[kind : kind + 1] = sum(jnp.where(lane == k, value, 0.0) for k, value in enumerate(values))


def ends_step(device, squares, stem, head, stem_grads, head_grads):
    shapes = [jax.ShapeDtypeStruct(arrays[0].shape, jnp.float32) for arrays in (stem, head) for _ in range(3)]
    return pl.pallas_call(
        ends_kernel,
        in_specs=[scalars] * 3 + [pl.BlockSpec()] * 14,
        out_shape=shapes + [jax.ShapeDtypeStruct((SUBLANES, LANES), jnp.float32)],
        compiler_params=lean,
        name="ends_step",
    )(device, *squares, *stem, *head, *stem_grads, *head_grads)


def renew_kernel(squares, weight, update, fresh, fresh_low):
    norms = jnp.sqrt(squares[0:2])
    trust = norms[0:1] / (norms[1:2] + epsilon)
    spot = 1 + pl.program_id(0) * pl.num_programs(1) + pl.program_id(1)
    lane = lax.broadcasted_iota(jnp.int32, trust.shape, 1)
    trust = jnp.sum(jnp.where(lane == spot, trust, 0.0), 1, keepdims=True)
    value = weight[0, 0] - learn_rate * (trust * update[0, 0])
    fresh[0, 0] = value
    fresh_low[0, 0] = value.astype(low)


def channel_renew(squares, weight, update):
    layers, ways, rows, columns = weight.shape
    block = pl.BlockSpec((1, 1, rows, columns), lambda i, j: (i, j, 0, 0))
    return pl.pallas_call(
        renew_kernel,
        grid=(layers, ways),
        in_specs=[whole(squares), block, block],
        out_specs=[block, block],
        out_shape=[jax.ShapeDtypeStruct(weight.shape, jnp.float32), jax.ShapeDtypeStruct(weight.shape, low)],
        compiler_params=large,
        cost_estimate=cost(3 * weight.size, 14 * weight.size),
        name="channel_renew",
    )(squares, weight, update)


def token_backward_kernel(gradient, state, gains, before, token_in, token_out_turn, *rest):
    grad_state, grad_vectors, grad_in, grad_out = rest[-4:]
    step = pl.program_id(0)
    token_grad = gradient[...].astype(low)
    hat, inverse = centred(state[...])
    normed = (hat * gains[0:1] + gains[1:2]).astype(low)
    hidden, slope = gelu_both(before[0].astype(jnp.float32))
    grad_before = (slope * dot(token_out_turn[...], token_grad)).astype(low)
    part_out = dot(hidden.astype(low), token_grad, (1, 1))
    part_in = dot(grad_before, normed, (1, 1))
    upstream = dot(token_in[...], grad_before)
    grad_state[...] = gradient[...] + centred_back(upstream * gains[0:1], hat, inverse)
    part_gain = jnp.sum(upstream * hat, 0, keepdims=True)
    part_shift = jnp.sum(upstream, 0, keepdims=True)

    @pl.when(step == 0)
    def _():
        grad_out[...] = part_out
        grad_in[...] = part_in
        grad_vectors[0:1] = part_gain
        grad_vectors[1:2] = part_shift

    @pl.when(step > 0)
    def _():
        grad_out[...] += part_out
        grad_in[...] += part_in
        grad_vectors[0:1] += part_gain
        grad_vectors[1:2] += part_shift


def token_backward(gradient, state, gains, before, token_in, token_out_turn, after=()):
    rows, hidden = token_in.shape
    count, width = state.shape[0] // rows, state.shape[1]
    one = pl.BlockSpec((rows, width), lambda i: (i, 0))
    still = lambda shape: pl.BlockSpec(shape, lambda i: (0, 0))
    return pl.pallas_call(
        token_backward_kernel,
        grid=(count,),
        in_specs=[
            one, one, whole(gains), pl.BlockSpec((1, hidden, width), lambda i: (i, 0, 0)),
            whole(token_in), whole(token_out_turn),
        ] + [pl.BlockSpec(memory_space=pl.ANY)] * len(after),
        out_specs=[one, still((2, width)), still((hidden, rows)), still((hidden, rows))],
        out_shape=[
            jax.ShapeDtypeStruct(state.shape, jnp.float32),
            jax.ShapeDtypeStruct((2, width), jnp.float32),
            jax.ShapeDtypeStruct((hidden, rows), jnp.float32),
            jax.ShapeDtypeStruct((hidden, rows), jnp.float32),
        ],
        compiler_params=lean,
        cost_estimate=cost(8 * count * rows * hidden * width, 16 * state.size, 0),
        name="token_backward",
    )(gradient, state, gains, before, token_in, token_out_turn, *after)


def mix_kernel(place, share, device, own, incoming, *rest):
    outs, (own_wide, incoming_wide, joint) = rest[:-3], rest[-3:]
    patches, images, width = own.shape
    group = images // len(outs)
    for at in range(0, width, LANES):
        lanes = slice(at, at + LANES)
        own_wide[...] = own[:, :, lanes].astype(jnp.float32).reshape(own_wide.shape)
        incoming_wide[...] = incoming[:, :, lanes].astype(jnp.float32).reshape(own_wide.shape)
        for q, out in enumerate(outs):
            for i in range(group):
                image = (device[0] ^ q) * group + i
                first = own_wide[pl.ds(image, patches, stride=images), :]
                second = incoming_wide[pl.ds(place[image], patches, stride=images), :]
                joint[i * patches : (i + 1) * patches, :] = (
                    share[image] * first + (1 - share[image]) * second
                )
            out[:, lanes] = joint[...].astype(low)


def mix(place, share, device, own, incoming, groups):
    patches, images, width = own.shape
    rows = images // groups * patches
    scalar = pl.BlockSpec(memory_space=pltpu.SMEM)
    return pl.pallas_call(
        mix_kernel,
        in_specs=[scalar, scalar, scalar, pl.BlockSpec(), pl.BlockSpec()],
        out_shape=[jax.ShapeDtypeStruct((rows, width), low)] * groups,
        scratch_shapes=[
            pltpu.VMEM((patches * images, LANES), jnp.float32),
            pltpu.VMEM((patches * images, LANES), jnp.float32),
            pltpu.VMEM((rows, LANES), jnp.float32),
        ],
        compiler_params=lean,
        cost_estimate=cost(4 * own.size, 6 * own.size),
        name="mix",
    )(place, share, device, own, incoming)


def stem_kernel(device, spots, *rest):
    sources, (blocks, gains, mixed, state, joint, spare, pieces, weights, piece_sems, sems) = rest[:-10], rest[-10:]
    piece_copies = [
        pltpu.make_async_copy(source, pieces.at[k], piece_sems.at[k]) for k, source in enumerate(sources)
    ]
    copies = block_copies(spots, blocks, pl.ds(0, weights.shape[1]), weights, sems)
    for copy in piece_copies + copies:
        copy.start()
    count = len(sources) // 2
    odd, upper = (device[0] & 1) == 1, (device[0] & 2) == 2
    patches = pieces.shape[1] // 2
    rows = joint.shape[0] // (2 * 2)
    joint[...] = jnp.zeros_like(joint)
    for copy in piece_copies:
        copy.wait()
    for side in range(2):
        arrived = [pieces[side * count + k].astype(jnp.float32) for k in range(count)]
        arrived = [jnp.where(odd, arrived[k ^ 1], arrived[k]) for k in range(count)]
        for k in range(count):
            spare[...] = jnp.where(upper, arrived[k ^ 2], arrived[k])
            for i in range(2):
                at = (side * 2 + i) * rows + k * patches
                joint[at : at + patches, :] = spare[i * patches : (i + 1) * patches, :]
    mixed[...] = joint[...].astype(low)
    for copy in copies:
        copy.wait()
    state[...] = dot(mixed[...], weights[...], (1, 1)) + gains[0:1]


def stem(device, spots, pieces, blocks, gains, rows):
    width, pixels = blocks.shape[0] * blocks.shape[1], pieces[0].shape[1]
    return pl.pallas_call(
        stem_kernel,
        in_specs=[scalars, scalars] + hbm(pieces) + hbm([blocks]) + [pl.BlockSpec()],
        out_shape=[
            jax.ShapeDtypeStruct((rows, pixels), low),
            jax.ShapeDtypeStruct((rows, width), jnp.float32),
        ],
        scratch_shapes=[
            pltpu.VMEM((rows, pixels), jnp.float32),
            pltpu.VMEM(pieces[0].shape, jnp.float32),
            pltpu.VMEM((len(pieces), *pieces[0].shape), low),
            pltpu.VMEM((width, pixels), low),
            pltpu.SemaphoreType.DMA((len(pieces),)),
            pltpu.SemaphoreType.DMA((blocks.shape[0],)),
        ],
        compiler_params=large,
        cost_estimate=cost(2 * rows * width * pixels, 12 * rows * width),
        name="stem",
    )(device, spots, *pieces, blocks, gains)


def head_kernel(
    patches, pixels, device, spots, state, gains, blocks, bias, numbers, labels, others, lam, weight, scale,
    gradient, grad_vectors, grads, grad_bias, loss, pooled, upstream, head, sems,
):
    copies = block_copies(spots, blocks, pl.ds(pixels, head.shape[1]), head, sems)
    for copy in copies:
        copy.start()
    rows, width = state.shape
    count = lam.shape[0]
    each = rows // count
    live = lax.broadcasted_iota(jnp.int32, (each, 1), 0) < patches
    hat, inverse = centred(state[...])
    pooled[...] = jnp.zeros_like(pooled)
    sums = []
    for i in range(count):
        sums.append(jnp.sum(jnp.where(live, hat[i * each : (i + 1) * each], 0.0), 0, keepdims=True))
        pooled[i : i + 1] = sums[i] / patches * gains[0:1] + gains[1:2]
    pooled_low = pooled[...].astype(low)
    for copy in copies:
        copy.wait()
    logits = dot(pooled_low, head[...])[:count] + bias[...]
    logits = jnp.where(numbers[...] >= 0, logits, -jnp.inf)
    peak = jnp.max(logits, -1, keepdims=True)
    powers = jnp.exp(logits - peak)
    mass = jnp.sum(powers, -1, keepdims=True)
    targets = jnp.where(numbers[...] == labels[...], lam[...], 0.0) + jnp.where(
        numbers[...] == others[...], 1 - lam[...], 0.0
    )
    log_probs = jnp.where(numbers[...] >= 0, logits - peak - jnp.log(mass), 0.0)
    losses = -jnp.sum(targets * log_probs, -1, keepdims=True)
    loss[...] = jnp.sum(weight[...] * losses, 0, keepdims=True)
    grad_logits = scale[...] * (powers / mass * jnp.sum(targets, -1, keepdims=True) - targets)
    grad_bias[...] = jnp.sum(grad_logits, 0, keepdims=True)
    pad = jnp.zeros((pooled.shape[0] - count, grad_logits.shape[1]), jnp.float32)
    grad_logits = jnp.concatenate([grad_logits, pad], 0)
    main = grad_logits.astype(low)
    rest = (grad_logits - main.astype(jnp.float32)).astype(low)
    size = main.shape[1] // 4
    for a in range(4):
        lanes = slice(a * size, (a + 1) * size)
        part = dot(pooled_low, main[:, lanes], (0, 0)) + dot(pooled_low, rest[:, lanes], (0, 0))
        rel = device[0] ^ a
        grads[(rel & 1) * 2 + (rel >> 1)] = part.astype(low)
    spread_back = (dot(main, head[...], (1, 1)) + dot(rest, head[...], (1, 1))) / patches
    upstream[...] = jnp.zeros_like(upstream)
    grad_gain = jnp.zeros((1, width), jnp.float32)
    for i in range(count):
        one = spread_back[i : i + 1]
        grad_gain = grad_gain + one * sums[i]
        upstream[i * each : (i + 1) * each] = jnp.where(live, one, 0.0)
    grad_vectors[0:1] = grad_gain
    grad_vectors[1:2] = jnp.sum(spread_back[:count], 0, keepdims=True) * patches
    gradient[...] = centred_back(upstream[...] * gains[0:1], hat, inverse)


def head_step(device, spots, state, gains, blocks, bias, numbers, labels, others, lam, weight, scale, patches, pixels):
    rows, width = state.shape
    columns = bias.shape[1]
    return pl.pallas_call(
        functools.partial(head_kernel, patches, pixels),
        in_specs=[scalars, scalars] + [pl.BlockSpec()] * 2 + hbm([blocks]) + [pl.BlockSpec()] * 7,
        out_shape=[
            jax.ShapeDtypeStruct(state.shape, jnp.float32),
            jax.ShapeDtypeStruct((2, width), jnp.float32),
            jax.ShapeDtypeStruct((4, width, columns // 4), low),
            jax.ShapeDtypeStruct((1, columns), jnp.float32),
            jax.ShapeDtypeStruct((1, 1), jnp.float32),
        ],
        scratch_shapes=[
            pltpu.VMEM((16, width), jnp.float32),
            pltpu.VMEM(state.shape, jnp.float32),
            pltpu.VMEM((width, columns), low),
            pltpu.SemaphoreType.DMA((blocks.shape[0],)),
        ],
        compiler_params=lean,
        cost_estimate=cost(64 * width * columns, 8 * rows * width),
        name="head_step",
    )(device, spots, state, gains, blocks, bias, numbers, labels, others, lam, weight, scale)


def stem_backward_kernel(device, gradient, mixed, grads, shift):
    rounded = gradient[...].astype(low)
    shift[...] = jnp.sum(rounded.astype(jnp.float32), 0, keepdims=True)
    whole_grad = dot(gradient[...].T.astype(low), mixed[...]).astype(low)
    size = whole_grad.shape[1] // 4
    grads[...] = jnp.zeros_like(grads)
    for a in range(4):
        rel = device[0] ^ a
        grads[(rel & 1) * 2 + (rel >> 1), :, :size] = whole_grad[:, a * size : (a + 1) * size]


def stem_backward(device, gradient, mixed):
    width, pixels = gradient.shape[1], mixed.shape[1]
    return pl.pallas_call(
        stem_backward_kernel,
        in_specs=[scalars] + [pl.BlockSpec()] * 2,
        out_shape=[
            jax.ShapeDtypeStruct((4, width, MISC), low),
            jax.ShapeDtypeStruct((1, width), jnp.float32),
        ],
        compiler_params=lean,
        cost_estimate=cost(2 * gradient.size * pixels, 8 * gradient.size),
        name="stem_backward",
    )(device, gradient, mixed)


def moved(values, source, way):
    spots = (lax.broadcasted_iota(jnp.int32, (values.shape[1],) * 2, 0) == source).astype(low)
    main = values.astype(low)
    rest = values - main.astype(jnp.float32)
    middle = rest.astype(low)
    rest = (rest - middle.astype(jnp.float32)).astype(low)
    return sum(dot(part, spots, (1, way)) for part in (main, middle, rest))


def vectors_kernel(vectors, source, out):
    out[...] = moved(vectors[...], source[...], 0)


def relative_vectors(vectors, source):
    return pl.pallas_call(
        vectors_kernel,
        out_shape=jax.ShapeDtypeStruct(vectors.shape, jnp.float32),
        compiler_params=lean,
        name="relative_vectors",
    )(vectors, source)


def gather_misc_kernel(count, source, stem_grads, *rest):
    tokens, parts, (bias, loss), outs, (joint, small) = (
        rest[:4],
        rest[4:count],
        rest[count : count + 2],
        [rest[count + 2 + place // 2].at[place % 2] for place in range(4)],
        rest[count + 4 :],
    )
    joint[...] = jnp.zeros_like(joint)
    at = 0
    for part in parts:
        joint[at : at + part.shape[0]] = part[...]
        at += part.shape[0]
    true = moved(joint[...], source[...], 1)
    small[...] = jnp.zeros_like(small)
    for j in range(joint.shape[1] // MISC):
        small[j * 16 : (j + 1) * 16] = true[:, j * MISC : (j + 1) * MISC]
    at = joint.shape[1] // MISC * 16
    for j in range(bias.shape[1] // MISC):
        small[at + j : at + j + 1] = bias[:, j * MISC : (j + 1) * MISC]
    at += bias.shape[1] // MISC
    small[at : at + 1, 0:1] = loss[...]
    stem_rows = stem_grads.shape[1]
    rows = tokens[0].shape[0] // 4
    patches = tokens[0].shape[1]
    for place, out in enumerate(outs):
        out[:stem_rows] = stem_grads[place]
        for j, token in enumerate(tokens):
            at = stem_rows + j * rows
            out[at : at + rows] = jnp.zeros((rows, MISC), low)
            out[at : at + rows, :patches] = token[place * rows : (place + 1) * rows].astype(low)
        out[stem_rows + 4 * rows :] = small[...].astype(low)


def gather_misc(source, stem_grads, tokens, parts, bias, loss):
    rows = stem_grads.shape[1] + tokens[0].shape[0] + SMALL
    return pl.pallas_call(
        functools.partial(gather_misc_kernel, 4 + len(parts)),
        out_shape=[jax.ShapeDtypeStruct((2, rows, MISC), low)] * 2,
        scratch_shapes=[
            pltpu.VMEM((16, parts[0].shape[1]), jnp.float32),
            pltpu.VMEM((SMALL, MISC), jnp.float32),
        ],
        compiler_params=lean,
        name="gather_misc",
    )(source, stem_grads, *tokens, *parts, bias, loss)


def swap(array, axis, mask):
    count = lax.axis_size(axis)
    return lax.ppermute(array, axis, [(i, i ^ mask) for i in range(count)])


def fence(*trees):
    return lax.optimization_barrier(trees)


def dp_masks():
    masks = []
    mask = lax.axis_size("dp") // 2
    while mask > 1:
        masks.append(mask)
        mask //= 2
    return masks


def row_order():
    order = [0]
    for mask in dp_masks() + [1]:
        order = order + [r ^ mask for r in order]
    return order


def packed(blocks):
    return jnp.concatenate(blocks, 0)


def unpacked(array, blocks):
    out = []
    at = 0
    for block in blocks:
        out.append(lax.slice_in_dim(array, at, at + block.shape[0], axis=0))
        at += block.shape[0]
    return out


def doubled(blocks, got):
    return [jnp.concatenate(pair, 0) for pair in zip(blocks, unpacked(got, blocks), strict=True)]


def added(keep, got):
    return (keep.astype(jnp.float32) + got.astype(jnp.float32)).astype(keep.dtype)


def cut_rows(array, half):
    middle = array.shape[-2] // 2
    return array[..., half * middle : (half + 1) * middle, :]


def folded(keep, got, kind):
    if kind == "rows":
        return [added(cut_rows(keep, half), cut_rows(got, half)) for half in range(2)]
    if kind == "blocks":
        return [added(keep[0], got[0]), added(keep[1], got[1])]
    if isinstance(kind, int):
        total = added(keep, got)
        return [
            jnp.concatenate([total[: kind // 2], total[kind:]]),
            jnp.concatenate([total[kind // 2 : kind], total[kind:]]),
        ]
    if kind == "turned":
        return [jnp.stack([added(keep[0], got[1]), added(keep[1], got[0])])]
    return [added(keep, got)]


def fold_kernel(jobs, *refs):
    refs = list(refs)
    values = [jax.tree.map(lambda _: refs.pop(0)[...], job[:2]) for job in jobs]
    for (keep, got), (_, _, kind) in zip(values, jobs, strict=True):
        for value in folded(keep, got, kind):
            refs.pop(0)[...] = value


def fold_all(jobs):
    arrays = jax.tree.leaves([job[:2] for job in jobs])
    shapes = [jax.eval_shape(functools.partial(folded, kind=kind), keep, got) for keep, got, kind in jobs]
    flat = [shape for group in shapes for shape in group]
    blank = [(*jax.tree.map(lambda _: 0, job[:2]), job[2]) for job in jobs]
    outs = pl.pallas_call(
        functools.partial(fold_kernel, blank),
        out_shape=flat,
        compiler_params=lean,
        cost_estimate=cost(sum(a.size for a in arrays), sum(4 * a.size for a in arrays)),
        name="fold_all",
    )(*arrays)
    out = []
    for group in shapes:
        out.append(outs[: len(group)])
        outs = outs[len(group) :]
    return out


def split_kernel(*refs):
    further = len(refs) > 10
    keep_low, keep_high, keep_out, got_low, got_high, got_out = refs[:6]
    in_keep, in_send, out_keep, out_send = refs[-4:]
    columns = keep_out.shape[3]
    in_keep[...] = added(keep_low[0], got_low[0])
    in_send[...] = added(keep_high[0], got_high[0])
    for half, out in enumerate((out_keep, out_send)):
        out[:, :columns] = added(keep_out[0, half], got_out[0, half])
        if further:
            out[:, columns:] = added(refs[6][half], refs[7][half])


def split_cores(keep, got, further=(), steps=4):
    rows, columns = keep.shape[2:]
    few, many = rows // 2 // steps, rows // steps
    low_rows = pl.BlockSpec((1, 2, few, columns), lambda i: (0, 0, i, 0))
    high_rows = pl.BlockSpec((1, 2, few, columns), lambda i: (0, 0, i + steps, 0))
    out_rows = pl.BlockSpec((1, 2, many, columns), lambda i: (1, 0, i, 0))
    total = columns + (further[0].shape[2] if further else 0)
    two = pl.BlockSpec((2, few, columns), lambda i: (0, i, 0))
    one = pl.BlockSpec((many, total), lambda i: (i, 0))
    pair = jax.ShapeDtypeStruct((2, rows // 2, columns), keep.dtype)
    single = jax.ShapeDtypeStruct((rows, total), keep.dtype)
    return pl.pallas_call(
        split_kernel,
        grid=(steps,),
        in_specs=[low_rows, high_rows, out_rows] * 2
        + [pl.BlockSpec((2, many, total - columns), lambda i: (0, i, 0))] * len(further),
        out_specs=[two, two, one, one],
        out_shape=[pair, pair, single, single],
        compiler_params=large,
        cost_estimate=cost(keep.size, 6 * keep.size),
        name="split_cores",
    )(keep, keep, keep, got, got, got, *further)


def reduce_rows(keep, send):
    steps = [1] + dp_masks()[::-1]
    for mask in steps[:-1]:
        keep, send = yield keep, swap(send, "dp", mask), "rows"
    (keep,) = yield keep, swap(send, "dp", steps[-1]), "sum"
    (keep,) = yield keep, swap(keep, "tok", 2), "turned"
    near, far = yield keep, swap(keep, "tok", 1), "none"
    return near, far


def reduce_columns(keep, send):
    keep, send = yield keep, swap(send, "tok", 2), "rows"
    steps = [1] + dp_masks()[::-1]
    for mask in steps[:-1]:
        keep, send = yield keep, swap(send, "dp", mask), "rows"
    (keep,) = yield keep, swap(send, "dp", steps[-1]), "sum"
    keep, others = yield keep, [swap(keep, "tok", q) for q in range(1, 4)], "none"
    return [keep, *others]


def reduce_misc(stem_rows, keep, send):
    keep, send = yield keep, swap(send, "tok", 2), stem_rows
    steps = [1] + dp_masks()[::-1]
    for mask in steps[:-1]:
        stem_rows //= 2
        keep, send = yield keep, swap(send, "dp", mask), stem_rows
    (keep,) = yield keep, swap(send, "dp", steps[-1]), "sum"
    block = keep[: stem_rows // 2]
    rest, others = yield keep, [swap(block, "tok", q) for q in range(1, 4)], "none"
    return [block, *others], rest[stem_rows // 2 :]


def sum_over(array, steps):
    for axis, mask in steps:
        (array,) = yield array, swap(array, axis, mask), "sum"
    return array


class Chain:
    def __init__(self, moves):
        self.moves, self.result = moves, None
        self.state = next(moves)

    def push(self, state):
        try:
            self.state = self.moves.send(state)
        except StopIteration as end:
            self.state, self.result = None, end.value


def advance(chains, *others):
    chains = [chain for chain in chains if chain.state is not None]
    states, others = fence([chain.state[:2] for chain in chains], others)
    jobs = []
    for chain, (keep, got) in zip(chains, states, strict=True):
        kind = chain.state[2]
        small = keep.size <= FOLD_MAX and kind != "none"
        if (kind == "rows" and keep.shape[-2] % 32) or (isinstance(kind, int) and kind % 32):
            small = False
        if small:
            jobs.append((chain, keep, got, kind))
    results = dict(
        zip([id(job[0]) for job in jobs], fold_all([job[1:] for job in jobs]) if jobs else [], strict=True)
    )
    others, fenced = fence(others, results)
    results = fenced
    for chain, (keep, got) in zip(chains, states, strict=True):
        kind = chain.state[2]
        if id(chain) in results:
            chain.push(results[id(chain)])
        elif kind == "none":
            chain.push((keep, got))
        else:
            chain.push(folded(keep, got, kind))
    return others


def exchanged(blocks):
    row = lax.axis_index("tok")
    blocks = [jnp.where((row & 1) == 1, blocks[k ^ 1], blocks[k]) for k in range(4)]
    return [jnp.where((row & 2) == 2, blocks[k ^ 2], blocks[k]) for k in range(4)]


def ordered(blocks, axis):
    return jnp.concatenate(exchanged([blocks[0], blocks[2], blocks[1], blocks[3]]), axis)


def quarter(array, axis):
    size = array.shape[axis] // lax.axis_size("tok")
    return lax.dynamic_slice_in_dim(array, lax.axis_index("tok") * size, size, axis)


def moments(weight, gradient, first, second, decay_rate):
    first_new = beta_one * first + (1 - beta_one) * gradient
    second_new = beta_two * second + (1 - beta_two) * gradient * gradient
    scale_one, scale_two = 1 / (1 - beta_one**STEP), 1 / (1 - beta_two**STEP)
    update = scale_one * first_new / (jnp.sqrt(scale_two * second_new) + epsilon) + decay_rate * weight
    return (first_new, second_new, update)


def row_squares(array, groups):
    flat = array.reshape(groups, -1)
    return jnp.sum(flat * flat, 1)


def renew(weight, update, weight_norm, update_norm, groups):
    trust = weight_norm / (update_norm + epsilon)
    return weight - learn_rate * (trust[:, None] * update.reshape(groups, -1)).reshape(weight.shape)


def body(
    images,
    partner,
    lam,
    labels,
    counts,
    class_weights,
    stem_w,
    stem_m,
    stem_v,
    tok_w,
    tok_m,
    tok_v,
    chan_w,
    chan_m,
    chan_v,
    head_w,
    head_m,
    head_v,
    vec_w,
    vec_m,
    vec_v,
    hb_w,
    hb_m,
    hb_v,
):
    count_dp = lax.axis_size("dp")
    count_tok = lax.axis_size("tok")
    device_row = lax.axis_index("dp")
    token_row = lax.axis_index("tok")
    patches = images.shape[0]
    all_patches = patches * count_tok
    per_device = images.shape[1]
    per_tok = per_device // count_tok
    classes_all = hb_w.shape[0]
    class_pad = -classes_all % (count_tok * LANES)
    width = vec_w.shape[1]
    each = all_patches + -all_patches % SUBLANES

    masks = dp_masks()
    batches = per_device // IMG_MB
    start = device_row * per_device
    own_parts, owners, shares = [], [], []
    for batch in range(batches):
        at = start + batch * IMG_MB
        own_parts.append(images[:, batch * IMG_MB : (batch + 1) * IMG_MB])
        owners.append(lax.dynamic_slice_in_dim(partner, at, IMG_MB, 0) % IMG_MB)
        shares.append(lax.dynamic_slice_in_dim(lam, at, IMG_MB, 0))
    device = token_row.astype(jnp.int32)[None]

    def mixed_pieces(batch, incoming):
        sends = mix(owners[batch], shares[batch], device, own_parts[batch], incoming, count_tok)
        return [sends[0]] + [swap(sends[q], "tok", q) for q in range(1, count_tok)]

    chan_low = quarter(chan_w.astype(low), 3)
    shard, size = chan_low.shape[2:]
    order = row_order()
    rows = jnp.asarray(order, jnp.int32) ^ device_row
    column_source = (rows[:, None] * shard + jnp.arange(shard, dtype=jnp.int32)[None, :]).reshape(1, width)
    ends = jnp.concatenate([stem_w.astype(low).T, jnp.pad(head_w.astype(low), ((0, 0), (0, class_pad)))], 1)
    ends = lax.all_gather(quarter(ends, 0), ("dp", "tok"))
    pixels = stem_w.shape[0]
    later = chan_low[1].reshape(2 * shard, size)

    later = lax.all_gather(later, ("dp", "tok")).reshape(count_dp, count_tok, -1, size)

    vectors = relative_vectors(vec_w, column_source)
    numbers = jnp.arange(classes_all + class_pad, dtype=jnp.int32)
    numbers = jnp.where(numbers < classes_all, numbers, -1)[None]
    bias = jnp.pad(hb_w, (0, class_pad))[None]
    own_hot = (labels[:, None] == jnp.arange(classes_all, dtype=jnp.int32)[None, :]).astype(jnp.float32)
    other_labels = jnp.take(labels, partner)
    own_weight = jnp.sum(own_hot * class_weights[None, :], 1)
    other_weight = jnp.take(own_weight, partner)
    live = (
        (jnp.arange(IMG_MB, dtype=jnp.int32)[None, :] < counts.reshape(-1)[:, None])
        .astype(jnp.float32)
        .reshape(-1)
    )
    weights = live * (lam * own_weight + (1 - lam) * other_weight)
    total = jnp.sum(weights)
    group = IMG_MB // count_tok

    def row_of(array):
        return jnp.concatenate(
            [
                lax.dynamic_slice_in_dim(array, start + batch * IMG_MB + token_row * group, group, 0)
                for batch in range(batches)
            ]
        )[:, None]

    image_rows = [row_of(array) for array in (labels, other_labels, lam, weights, weights / total)]

    blocks = [chan_low[0, 0], chan_low[0, 1]]
    tok_low = jnp.swapaxes(tok_w, 2, 3).astype(low)
    partner_mask = count_dp // 2
    incoming = swap(own_parts[0], "dp", partner_mask)
    for step, mask in enumerate(masks):
        got = swap(packed(blocks), "dp", mask)
        if step == 0:
            blocks, got, tok_low, own_parts[1], incoming = fence(blocks, got, tok_low, own_parts[1], incoming)
            pieces = mixed_pieces(0, incoming)
            incoming_two = swap(own_parts[1], "dp", partner_mask)
            tok_far = swap(tok_low, "tok", 2)
        elif step == 1:
            blocks, got, vectors, image_rows, pieces, tok_low, tok_far = fence(
                blocks, got, vectors, image_rows, pieces, tok_low, tok_far
            )
        else:
            blocks, got = fence(blocks, got)
        blocks = doubled(blocks, got)
    tok_half = jnp.concatenate([tok_low, tok_far], 2)
    tok_turn = jnp.concatenate([tok_half, swap(tok_half, "tok", 1)], 2)
    tok_turn = jnp.pad(tok_turn, ((0, 0), (0, 0), (0, 0), (0, each - all_patches)))
    token_turn = [[tok_turn[layer, way] for way in range(2)] for layer in range(LAYERS)]
    token_all = [[array.T for array in pair] for pair in token_turn]

    first, second = blocks
    first_low, second_far = swap(first, "dp", 1), swap(second, "tok", 2)
    first, second, first_low, second_far, incoming_two, token_all, token_turn = fence(
        first, second, first_low, second_far, incoming_two, token_all, token_turn
    )
    more = mixed_pieces(1, incoming_two)
    firsts, seconds = jnp.stack([first, first_low]), jnp.stack([second, second_far])
    firsts_far, seconds_low = swap(firsts, "tok", 2), swap(seconds, "dp", 1)
    firsts, seconds, firsts_far, seconds_low, more = fence(firsts, seconds, firsts_far, seconds_low, more)
    source_zero = Pieces(
        [firsts, firsts_far, swap(firsts, "tok", 1), swap(firsts_far, "tok", 1)],
        [seconds, seconds_low, swap(seconds, "tok", 1), swap(seconds_low, "tok", 1)],
    )
    if shard % 16:
        many = 96 // shard
        groups = count_dp // many
        later = jnp.take(later, rows, axis=0).reshape(groups, many, count_tok, 2, shard, size)
        later = later.transpose(0, 2, 3, 1, 4, 5).reshape(groups, count_tok, 2 * many * shard, size)
        ends = jnp.take(ends.reshape(count_dp, shard, -1), rows, axis=0).reshape(groups, many * shard, -1)
        spots = jnp.arange(groups, dtype=jnp.int32)
        source_one = Gathered(later, spots, device, many * shard)
    else:
        spots = rows
        ends = ends.reshape(count_dp, shard, -1)
        source_one = Gathered(later, spots, device, shard)

    gains = [vectors[1 + 4 * layer : 5 + 4 * layer] for layer in range(LAYERS)]
    mixed, stem_state = stem(device, spots, pieces + more, ends, vectors, each * per_tok)
    middle_zero, before_zero = token_forward(stem_state, gains[0], token_turn[0][0], token_all[0][1])
    first_state, inner_zero = channel_forward(middle_zero, gains[0], source_zero)
    middle_one, before_one = token_forward(first_state, gains[1], token_turn[1][0], token_all[1][1])
    second_state, inner_one = channel_forward(middle_one, gains[1], source_one)
    gradient, last_part, head_grads, bias_part, loss_local = head_step(
        device, spots, second_state, vectors[NV - 2 :], ends, bias, numbers, *image_rows, all_patches, pixels
    )

    head_got = swap(head_grads[2:], "tok", 1)
    send, partial, _ = channel_backward(gradient, middle_one, gains[1], inner_one, source_one)
    got = swap(send, "tok", 1)
    keep, gradient, second_one = channel_backward(gradient, middle_one, gains[1], inner_one, source_one, partial)
    in_keep, in_send, out_keep, out_send = split_cores(keep, got, (head_grads[:2], head_got))
    in_keep, in_send, out_keep, out_send, gradient = fence(in_keep, in_send, out_keep, out_send, gradient)
    chains_one = [Chain(reduce_rows(in_keep, in_send)), Chain(reduce_columns(out_keep, out_send))]
    gradient, first_one, *token_one = token_backward(
        gradient, first_state, gains[1], before_one, token_all[1][0], token_turn[1][1]
    )
    send, partial, _ = channel_backward(gradient, middle_zero, gains[0], inner_zero, source_zero)
    send, partial, gradient = advance(chains_one, send, partial, gradient)
    got = swap(send, "tok", 1)
    keep, gradient, second_zero = channel_backward(gradient, middle_zero, gains[0], inner_zero, source_zero, partial)
    in_keep, in_send, out_keep, out_send = split_cores(keep, got)
    in_keep, in_send, out_keep, out_send, gradient = advance(
        chains_one, in_keep, in_send, out_keep, out_send, gradient
    )
    chains_zero = [Chain(reduce_rows(in_keep, in_send)), Chain(reduce_columns(out_keep, out_send))]
    gradient, first_zero, *token_zero = token_backward(
        gradient, stem_state, gains[0], before_zero, token_all[0][0], token_turn[0][1]
    )
    stem_grads, stem_bias = stem_backward(device, gradient, mixed)
    misc = gather_misc(
        column_source,
        stem_grads,
        token_zero + token_one,
        [stem_bias, first_zero, second_zero, first_one, second_one, last_part],
        bias_part,
        loss_local,
    )
    misc = advance(chains_one + chains_zero, *misc)
    ((misc_keep, misc_send),) = fold_all([(misc[0], swap(misc[1], "tok", 1), "blocks")])
    misc_chain = Chain(reduce_misc(width, misc_keep, misc_send))
    dp_steps = [("dp", mask) for mask in [1] + dp_masks()[::-1]]
    everything = chains_one + chains_zero + [misc_chain]
    earlier = []
    while any(chain.state is not None for chain in everything):
        if not earlier and all(chain.result is not None for chain in chains_one):
            *earlier, squares_one = channel_step(
                1, device, chan_w, chan_m, chan_v, *[chain.result for chain in chains_one], []
            )
            earlier = list(advance(everything, *earlier))
        else:
            advance(everything)
    chan_first, chan_second, chan_update, squares_zero = channel_step(
        0, device, chan_w, chan_m, chan_v, *[chain.result for chain in chains_zero], earlier
    )
    stem_parts, misc = misc_chain.result
    hidden = tok_w.shape[3]
    token_grad = misc[: 4 * hidden].reshape(LAYERS, 2, hidden, MISC)[..., :all_patches].astype(jnp.float32)
    small = misc[4 * hidden :].astype(jnp.float32)
    blocks = width // MISC
    vector_grad = jnp.concatenate([small[16 * j : 16 * j + NV] for j in range(blocks)], 1)
    bias_grad = small[16 * blocks : 16 * blocks + numbers.shape[1] // MISC].reshape(-1)[:classes_all]
    loss_total = small[16 * blocks + numbers.shape[1] // MISC, 0]
    turned = lambda array: jnp.swapaxes(array, -1, -2)
    tok_w, tok_m, tok_v, stem_w, stem_m, stem_v = [turned(a) for a in (tok_w, tok_m, tok_v, stem_w, stem_m, stem_v)]
    stem_first, stem_second, stem_update, head_first, head_second, head_update, shard_squares = ends_step(
        device,
        (squares_zero, squares_one),
        (stem_w, stem_m, stem_v),
        (head_w, head_m, head_v),
        stem_parts,
        chains_one[1].result,
    )
    tok_first, tok_second, tok_update = moments(tok_w, token_grad, tok_m, tok_v, weight_decay)
    vec_first, vec_second, vec_update = moments(vec_w, vector_grad, vec_m, vec_v, 0.0)
    hb_first, hb_second, hb_update = moments(hb_w, bias_grad, hb_m, hb_v, 0.0)
    matrix_groups = 2 * LAYERS
    pair_of = lambda array, other, groups: jnp.stack([row_squares(array, groups), row_squares(other, groups)])
    token_squares = pair_of(tok_w, tok_update, matrix_groups)
    token_squares = token_squares + swap(token_squares, "tok", 1)
    at = 1
    while at < count_dp:
        if 4 * at <= count_dp:
            one, two, three = [swap(shard_squares, "dp", k * at) for k in (1, 2, 3)]
            shard_squares = (shard_squares + one) + (two + three)
            at *= 4
        else:
            shard_squares = shard_squares + swap(shard_squares, "dp", at)
            at *= 2
    last = 2 + matrix_groups
    token_squares, shard_squares = fence(token_squares, shard_squares)
    token_squares = token_squares + swap(token_squares, "tok", 2)
    weight_total, update_total = jnp.concatenate(
        [shard_squares[:2, :1], token_squares, shard_squares[:2, 1:last]], 1
    )
    weight_norms = jnp.sqrt(weight_total)
    update_norms = jnp.sqrt(update_total)
    stem_end = 1
    tok_end = 1 + matrix_groups
    chan_end = 1 + 2 * matrix_groups
    stem_new = renew(stem_w, stem_update, weight_norms[0:stem_end], update_norms[0:stem_end], 1)
    tok_new = renew(
        tok_w,
        tok_update,
        weight_norms[stem_end:tok_end],
        update_norms[stem_end:tok_end],
        matrix_groups,
    )
    chan_new, chan_new_low = channel_renew(shard_squares, chan_w, chan_update)
    head_new = renew(head_w, head_update, weight_norms[chan_end:], update_norms[chan_end:], 1)
    vec_weight_norm = jnp.sqrt(row_squares(vec_w, NV))
    vec_update_norm = jnp.sqrt(row_squares(vec_update, NV))
    hb_weight_norm = jnp.sqrt(row_squares(hb_w, 1))
    hb_update_norm = jnp.sqrt(row_squares(hb_update, 1))
    vec_new = renew(vec_w, vec_update, vec_weight_norm, vec_update_norm, NV)
    hb_new = renew(hb_w, hb_update, hb_weight_norm, hb_update_norm, 1)
    stem_new, stem_first, stem_second, tok_new, tok_first, tok_second = [
        turned(a) for a in (stem_new, stem_first, stem_second, tok_new, tok_first, tok_second)
    ]
    norms = jnp.stack(
        [
            jnp.concatenate([weight_norms, vec_weight_norm, hb_weight_norm]),
            jnp.concatenate([update_norms, vec_update_norm, hb_update_norm]),
        ],
        1,
    )
    loss_parts = jnp.stack([loss_total, total])
    return (
        stem_new,
        stem_first,
        stem_second,
        tok_new,
        tok_first,
        tok_second,
        chan_new,
        chan_first,
        chan_second,
        head_new,
        head_first,
        head_second,
        vec_new,
        vec_first,
        vec_second,
        hb_new,
        hb_first,
        hb_second,
        stem_new.astype(jnp.bfloat16),
        tok_new.astype(jnp.bfloat16),
        chan_new_low,
        head_new.astype(jnp.bfloat16),
        norms,
        loss_parts,
    )


def solution(mesh):
    in_specs = (
        P("tok", "dp", None),
        P(),
        P(),
        P(),
        P(),
        P(),
        P(None, "dp"),
        P(None, "dp"),
        P(None, "dp"),
        P(None, None, None, "tok"),
        P(None, None, None, "tok"),
        P(None, None, None, "tok"),
        P(None, None, "dp", None),
        P(None, None, "dp", None),
        P(None, None, "dp", None),
        P("dp", None),
        P("dp", None),
        P("dp", None),
        P(),
        P(),
        P(),
        P(),
        P(),
        P(),
    )
    out_specs = (
        P(None, "dp"),
        P(None, "dp"),
        P(None, "dp"),
        P(None, None, None, "tok"),
        P(None, None, None, "tok"),
        P(None, None, None, "tok"),
        P(None, None, "dp", None),
        P(None, None, "dp", None),
        P(None, None, "dp", None),
        P("dp", None),
        P("dp", None),
        P("dp", None),
        P(),
        P(),
        P(),
        P(),
        P(),
        P(),
        P(None, "dp"),
        P(None, None, None, "tok"),
        P(None, None, "dp", None),
        P("dp", None),
        P(),
        P(),
    )
    return jax.shard_map(body, mesh=mesh, in_specs=in_specs, out_specs=out_specs, check_vma=False)
```

```python
import functools

import jax
import jax.numpy as jnp
from jax import lax
from jax.experimental import pallas as pl
from jax.experimental.pallas import tpu as pltpu
from jax.sharding import PartitionSpec as P

LAYERS = 2
STEP = 5
IMG_MB = 8
NV = 11
LANES = 128
SUBLANES = 8
FOLD_MAX = 1200000
MISC = 256
SMALL = 64

low = jnp.bfloat16
beta_one = 0.9
beta_two = 0.999
epsilon = 1e-06
weight_decay = 0.01
learn_rate = 0.3
root = 0.7978845608028654
cubic = 0.044715
room = pltpu.CompilerParams(vmem_limit_bytes=44 * 1024 * 1024)
places = (0, 2, 1, 3)
large = pltpu.CompilerParams(vmem_limit_bytes=60 * 1024 * 1024)
slim = pltpu.CompilerParams(vmem_limit_bytes=36 * 1024 * 1024)
lean = pltpu.CompilerParams(vmem_limit_bytes=24 * 1024 * 1024)


def dot(left, right, contract=(1, 0)):
    return lax.dot_general(
        left, right, (((contract[0],), (contract[1],)), ((), ())), preferred_element_type=jnp.float32
    )


def gelu(values):
    return 0.5 * values * (1 + jnp.tanh(root * values * (1 + cubic * values * values)))


def gelu_both(values):
    square = values * values
    bend = jnp.tanh(root * values * (1 + cubic * square))
    half = 0.5 * (1 + bend)
    slope = half + 0.5 * values * (1 - bend * bend) * (root * (1 + 3 * cubic * square))
    return values * half, slope


def centred(values):
    centre = values - jnp.mean(values, -1, keepdims=True)
    inverse = lax.rsqrt(jnp.mean(centre * centre, -1, keepdims=True) + 1e-06)
    return centre * inverse, inverse


def centred_back(scaled, hat, inverse):
    return inverse * (
        scaled - jnp.mean(scaled, -1, keepdims=True) - hat * jnp.mean(scaled * hat, -1, keepdims=True)
    )


def whole(array):
    zeros = (0,) * array.ndim
    return pl.BlockSpec(array.shape, lambda *_: zeros)


def cost(flops, bytes_accessed, powers=0):
    return pl.CostEstimate(flops=flops, bytes_accessed=bytes_accessed, transcendentals=powers)


def token_forward_kernel(state, gains, token_in, token_out, middle, before):
    hat, _ = centred(state[...])
    normed = (hat * gains[0:1] + gains[1:2]).astype(low)
    pre = dot(token_in[...], normed)
    before[0] = pre.astype(low)
    middle[...] = state[...] + dot(token_out[...], gelu(pre).astype(low))


def token_forward(state, gains, token_in, token_out):
    hidden, rows = token_in.shape
    count, width = state.shape[0] // rows, state.shape[1]
    one = pl.BlockSpec((rows, width), lambda i: (i, 0))
    return pl.pallas_call(
        token_forward_kernel,
        grid=(count,),
        in_specs=[one, whole(gains), whole(token_in), whole(token_out)],
        out_specs=[one, pl.BlockSpec((1, hidden, width), lambda i: (i, 0, 0))],
        out_shape=[
            jax.ShapeDtypeStruct(state.shape, jnp.float32),
            jax.ShapeDtypeStruct((count, hidden, width), low),
        ],
        compiler_params=lean,
        cost_estimate=cost(4 * count * rows * hidden * width, 10 * state.size, 0),
        name="token_forward",
    )(state, gains, token_in, token_out)


def block_copies(spots, blocks, lanes, held, sems):
    rows = blocks.shape[1]
    return [
        pltpu.make_async_copy(blocks.at[spots[i], :, lanes], held.at[pl.ds(i * rows, rows)], sems.at[i])
        for i in range(blocks.shape[0])
    ]


def hbm(arrays):
    return [pl.BlockSpec(memory_space=pltpu.HBM)] * len(arrays)


scalars = pl.BlockSpec(memory_space=pltpu.SMEM)


class Pieces:
    def __init__(self, first, second):
        self.arrays = [*first, *second]
        self.specs = hbm(self.arrays)
        self.width = 2 * second[0].shape[1]
        self.size = second[0].shape[2]
        self.sems = 4

    def copies(self, refs, held_in, held_out, sems, slot, place):
        half = self.width // 2
        out = []
        for side in range(2):
            rows = pl.ds(side * half, half)
            first = refs[place].at[side, pl.ds(0, half)]
            second = refs[4 + place // 2 * 2 + side].at[place % 2]
            out.append(pltpu.make_async_copy(first, held_in.at[slot, rows], sems.at[slot, side]))
            out.append(pltpu.make_async_copy(second, held_out.at[slot, rows], sems.at[slot, 2 + side]))
        return out


class Gathered:
    def __init__(self, array, shards, device, rows):
        self.arrays = [shards, device, array]
        self.specs = [scalars, scalars] + hbm([array])
        self.blocks, self.rows, self.size = array.shape[0], rows, array.shape[3]
        self.width = self.blocks * self.rows
        self.sems = 2 * self.blocks

    def copies(self, refs, held_in, held_out, sems, slot, place):
        shards, device, array = refs
        quarter_at = device[0] ^ places[place]
        out = []
        for block in range(self.blocks):
            rows = pl.ds(block * self.rows, self.rows)
            for way, held in enumerate((held_in, held_out)):
                out.append(
                    pltpu.make_async_copy(
                        array.at[shards[block], quarter_at, pl.ds(way * self.rows, self.rows)],
                        held.at[slot, rows],
                        sems.at[slot, 2 * block + way],
                    )
                )
        return out


def channel_forward_kernel(source, middle, gains, *rest):
    refs = rest[: len(source.arrays)]
    result, inner, normed, held_in, held_out, sems = rest[-6:]
    step = pl.program_id(0)

    @pl.when(step == 0)
    def _():
        for q in range(4):
            for copy in source.copies(refs, held_in, held_out, sems, q, q):
                copy.start()
        hat, _ = centred(middle[...])
        normed[...] = (hat * gains[2:3] + gains[3:4]).astype(low)
        result[...] = middle[...]

    for q in range(4):

        @pl.when(step == q)
        def _(q=q):
            for copy in source.copies(refs, held_in, held_out, sems, q, q):
                copy.wait()
            product = dot(normed[...], held_in[q])
            inner[...] = product.astype(low)
            result[...] += dot(gelu(product).astype(low), held_out[q], (1, 1))


def channel_forward(middle, gains, source):
    rows, width = middle.shape
    size = source.size
    total = 4 * size
    return pl.pallas_call(
        functools.partial(channel_forward_kernel, source),
        grid=(4,),
        in_specs=[whole(middle), whole(gains)] + source.specs,
        out_specs=[whole(middle), pl.BlockSpec((rows, size), lambda i: (0, i))],
        out_shape=[
            jax.ShapeDtypeStruct(middle.shape, jnp.float32),
            jax.ShapeDtypeStruct((rows, total), low),
        ],
        scratch_shapes=[
            pltpu.VMEM(middle.shape, low),
            pltpu.VMEM((4, width, size), low),
            pltpu.VMEM((4, width, size), low),
            pltpu.SemaphoreType.DMA((4, source.sems)),
        ],
        compiler_params=slim,
        cost_estimate=cost(4 * rows * width * total, 4 * width * total + 2 * rows * total),
        name="channel_forward",
    )(middle, gains, *source.arrays)


def channel_backward_kernel(source, last, gradient, middle, gains, inner, *rest):
    if last:
        before, rest = rest[0], rest[1:]
    refs = rest[: len(source.arrays)]
    grads, total, grad_vectors, grad_low, grad_turn, normed_turn, held_in, held_out, sems = rest[-9:]
    step = pl.program_id(0)
    first = 0 if last else 2

    @pl.when(step == 0)
    def _():
        for q in range(2):
            for copy in source.copies(refs, held_in, held_out, sems, q, first + q):
                copy.start()
        grad_low[...] = gradient[...].astype(low)
        grad_turn[...] = gradient[...].T.astype(low)
        hat, _ = centred(middle[...])
        normed_turn[...] = (hat * gains[2:3] + gains[3:4]).T.astype(low)
        total[...] = before[...] if last else jnp.zeros_like(total)

    for q in range(2):

        @pl.when(step == q)
        def _(q=q):
            for copy in source.copies(refs, held_in, held_out, sems, q, first + q):
                copy.wait()
            active, slope = gelu_both(inner[...].astype(jnp.float32))
            grads[1, 0] = dot(grad_turn[...], active.astype(low)).astype(low)
            grad_inner = (slope * dot(grad_low[...], held_out[q])).astype(low)
            grads[0, 0] = dot(normed_turn[...], grad_inner).astype(low)
            total[...] += dot(grad_inner, held_in[q], (1, 1))

    if last:

        @pl.when(step == 1)
        def _():
            hat, inverse = centred(middle[...])
            upstream = total[...]
            grad_vectors[0:1] = jnp.sum(upstream * hat, 0, keepdims=True)
            grad_vectors[1:2] = jnp.sum(upstream, 0, keepdims=True)
            total[...] = gradient[...] + centred_back(upstream * gains[2:3], hat, inverse)


def channel_backward(gradient, middle, gains, inner, source, before=None):
    rows, width = middle.shape
    size = source.size
    last = before is not None
    shift = 0 if last else 2
    carried = [before] if last else []
    total = 2 * size
    return pl.pallas_call(
        functools.partial(channel_backward_kernel, source, last),
        grid=(2,),
        in_specs=[whole(middle), whole(middle), whole(gains), pl.BlockSpec((rows, size), lambda i: (0, i + shift))]
        + [whole(array) for array in carried]
        + source.specs,
        out_specs=[
            pl.BlockSpec((2, 1, width, size), lambda i: (0, i, 0, 0)),
            whole(middle),
            pl.BlockSpec((2, width), lambda i: (0, 0)),
        ],
        out_shape=[
            jax.ShapeDtypeStruct((2, 2, width, size), low),
            jax.ShapeDtypeStruct(middle.shape, jnp.float32),
            jax.ShapeDtypeStruct((2, width), jnp.float32),
        ],
        scratch_shapes=[
            pltpu.VMEM((rows, width), low),
            pltpu.VMEM((width, rows), low),
            pltpu.VMEM((width, rows), low),
            pltpu.VMEM((2, width, size), low),
            pltpu.VMEM((2, width, size), low),
            pltpu.SemaphoreType.DMA((2, source.sems)),
        ],
        compiler_params=room,
        cost_estimate=cost(8 * rows * width * total, 8 * width * total + 2 * rows * total),
        name="channel_backward",
    )(gradient, middle, gains, inner, *carried, *source.arrays)


def step_kernel(device, weight, mean, power, near, far, *rest):
    apart, (mean_new, power_new, update, sums) = rest[:4], rest[-4:]
    way = pl.program_id(0)
    size = near.shape[2]
    weight_part, update_part = 0.0, 0.0
    for a in range(4):
        rel = device[0] ^ a
        lanes = slice(a * size, (a + 1) * size)
        values = [
            jnp.where(way == 0, one.astype(jnp.float32), two[...].astype(jnp.float32))
            for one, two in zip((near[0], far[0], near[1], far[1]), apart, strict=True)
        ]
        grad = jnp.where(
            rel < 2, jnp.where(rel == 0, values[0], values[1]), jnp.where(rel == 2, values[2], values[3])
        )
        value = weight[0, 0, :, lanes]
        mean_next, power_next, change = moments(
            value, grad, mean[0, 0, :, lanes], power[0, 0, :, lanes], weight_decay
        )
        mean_new[0, 0, :, lanes] = mean_next
        power_new[0, 0, :, lanes] = power_next
        update[0, 0, :, lanes] = change
        weight_part += jnp.sum(jnp.sum(value * value, 0, keepdims=True))
        update_part += jnp.sum(jnp.sum(change * change, 0, keepdims=True))

    @pl.when(pl.program_id(1) == 0)
    def _():
        sums[way, 0] = weight_part
        sums[way, 1] = update_part

    @pl.when(pl.program_id(1) > 0)
    def _():
        sums[way, 0] += weight_part
        sums[way, 1] += update_part


def channel_step(layer, device, weight, mean, power, chain_in, chain_out, earlier):
    near, far = chain_in
    rows, size = near.shape[1:]
    columns = weight.shape[3]
    chunk = 32 if rows % 32 == 0 else rows
    block = pl.BlockSpec((1, 1, chunk, columns), lambda w, i: (layer, w, i, 0))
    two = pl.BlockSpec((2, chunk, size), lambda w, i: (0, i, 0))
    one = pl.BlockSpec((chunk, size), lambda w, i: (i, 0))
    shape = jax.ShapeDtypeStruct(weight.shape, jnp.float32)
    return pl.pallas_call(
        step_kernel,
        grid=(2, rows // chunk),
        in_specs=[scalars, block, block, block, two, two, one, one, one, one] + hbm(earlier),
        out_specs=[block, block, block, scalars],
        out_shape=[shape, shape, shape, jax.ShapeDtypeStruct((2, 2), jnp.float32)],
        input_output_aliases={10 + i: i for i in range(len(earlier))},
        compiler_params=large,
        cost_estimate=cost(40 * near.size, 104 * near.size),
        name="channel_step",
    )(device, weight, mean, power, near, far, *chain_out, *earlier)


def ends_kernel(
    device, squares_zero, squares_one, stem_w, stem_m, stem_v, head_w, head_m, head_v, *rest
):
    stem_grads, head_grads, outs, sums = rest[:4], rest[4:8], rest[8:14], rest[14]

    def step(sources, grads, first, results):
        weight, mean, power = sources
        mean_new, power_new, update = results
        parts = [grad[:, first:].astype(jnp.float32) for grad in grads]
        size = -(-weight.shape[1] // (4 * 64)) * 64
        weight_part, update_part = 0.0, 0.0
        for a in range(4):
            rel = device[0] ^ a
            lanes = slice(a * size, min((a + 1) * size, weight.shape[1]))
            cut = [part[:, : lanes.stop - lanes.start] for part in parts]
            grad = jnp.where(rel < 2, jnp.where(rel == 0, cut[0], cut[1]), jnp.where(rel == 2, cut[2], cut[3]))
            value = weight[:, lanes]
            mean_new[:, lanes], power_new[:, lanes], change = moments(
                value, grad, mean[:, lanes], power[:, lanes], weight_decay
            )
            update[:, lanes] = change
            weight_part += jnp.sum(jnp.sum(value * value, 0, keepdims=True), 1, keepdims=True)
            update_part += jnp.sum(jnp.sum(change * change, 0, keepdims=True), 1, keepdims=True)
        return weight_part, update_part

    stem_part = step((stem_w, stem_m, stem_v), stem_grads, 0, outs[:3])
    head_part = step((head_w, head_m, head_v), head_grads, head_grads[0].shape[1] - MISC, outs[3:])
    lane = lax.broadcasted_iota(jnp.int32, (1, LANES), 1)
    sums[...] = jnp.zeros_like(sums)
    for kind in range(2):
        values = [stem_part[kind]]
        values += [squares[way, kind] for squares in (squares_zero, squares_one) for way in range(2)]
        values += [head_part[kind]]
        sums[kind : kind + 1] = sum(jnp.where(lane == k, value, 0.0) for k, value in enumerate(values))


def ends_step(device, squares, stem, head, stem_grads, head_grads):
    shapes = [jax.ShapeDtypeStruct(arrays[0].shape, jnp.float32) for arrays in (stem, head) for _ in range(3)]
    return pl.pallas_call(
        ends_kernel,
        in_specs=[scalars] * 3 + [pl.BlockSpec()] * 14,
        out_shape=shapes + [jax.ShapeDtypeStruct((SUBLANES, LANES), jnp.float32)],
        compiler_params=lean,
        name="ends_step",
    )(device, *squares, *stem, *head, *stem_grads, *head_grads)


def renew_kernel(squares, weight, update, fresh, fresh_low):
    norms = jnp.sqrt(squares[0:2])
    trust = norms[0:1] / (norms[1:2] + epsilon)
    spot = 1 + pl.program_id(0) * pl.num_programs(1) + pl.program_id(1)
    lane = lax.broadcasted_iota(jnp.int32, trust.shape, 1)
    trust = jnp.sum(jnp.where(lane == spot, trust, 0.0), 1, keepdims=True)
    value = weight[0, 0] - learn_rate * (trust * update[0, 0])
    fresh[0, 0] = value
    fresh_low[0, 0] = value.astype(low)


def channel_renew(squares, weight, update):
    layers, ways, rows, columns = weight.shape
    block = pl.BlockSpec((1, 1, rows, columns), lambda i, j: (i, j, 0, 0))
    return pl.pallas_call(
        renew_kernel,
        grid=(layers, ways),
        in_specs=[whole(squares), block, block],
        out_specs=[block, block],
        out_shape=[jax.ShapeDtypeStruct(weight.shape, jnp.float32), jax.ShapeDtypeStruct(weight.shape, low)],
        compiler_params=large,
        cost_estimate=cost(3 * weight.size, 14 * weight.size),
        name="channel_renew",
    )(squares, weight, update)


def token_backward_kernel(gradient, state, gains, before, token_in, token_out_turn, *rest):
    grad_state, grad_vectors, grad_in, grad_out = rest[-4:]
    step = pl.program_id(0)
    token_grad = gradient[...].astype(low)
    hat, inverse = centred(state[...])
    normed = (hat * gains[0:1] + gains[1:2]).astype(low)
    hidden, slope = gelu_both(before[0].astype(jnp.float32))
    grad_before = (slope * dot(token_out_turn[...], token_grad)).astype(low)
    part_out = dot(hidden.astype(low), token_grad, (1, 1))
    part_in = dot(grad_before, normed, (1, 1))
    upstream = dot(token_in[...], grad_before)
    grad_state[...] = gradient[...] + centred_back(upstream * gains[0:1], hat, inverse)
    part_gain = jnp.sum(upstream * hat, 0, keepdims=True)
    part_shift = jnp.sum(upstream, 0, keepdims=True)

    @pl.when(step == 0)
    def _():
        grad_out[...] = part_out
        grad_in[...] = part_in
        grad_vectors[0:1] = part_gain
        grad_vectors[1:2] = part_shift

    @pl.when(step > 0)
    def _():
        grad_out[...] += part_out
        grad_in[...] += part_in
        grad_vectors[0:1] += part_gain
        grad_vectors[1:2] += part_shift


def token_backward(gradient, state, gains, before, token_in, token_out_turn, after=()):
    rows, hidden = token_in.shape
    count, width = state.shape[0] // rows, state.shape[1]
    one = pl.BlockSpec((rows, width), lambda i: (i, 0))
    still = lambda shape: pl.BlockSpec(shape, lambda i: (0, 0))
    return pl.pallas_call(
        token_backward_kernel,
        grid=(count,),
        in_specs=[
            one, one, whole(gains), pl.BlockSpec((1, hidden, width), lambda i: (i, 0, 0)),
            whole(token_in), whole(token_out_turn),
        ] + [pl.BlockSpec(memory_space=pl.ANY)] * len(after),
        out_specs=[one, still((2, width)), still((hidden, rows)), still((hidden, rows))],
        out_shape=[
            jax.ShapeDtypeStruct(state.shape, jnp.float32),
            jax.ShapeDtypeStruct((2, width), jnp.float32),
            jax.ShapeDtypeStruct((hidden, rows), jnp.float32),
            jax.ShapeDtypeStruct((hidden, rows), jnp.float32),
        ],
        compiler_params=lean,
        cost_estimate=cost(8 * count * rows * hidden * width, 16 * state.size, 0),
        name="token_backward",
    )(gradient, state, gains, before, token_in, token_out_turn, *after)


def mix_kernel(place, share, device, own, incoming, *rest):
    outs, (own_wide, incoming_wide, joint) = rest[:-3], rest[-3:]
    patches, images, width = own.shape
    group = images // len(outs)
    for at in range(0, width, LANES):
        lanes = slice(at, at + LANES)
        held = slice(0, patches * images)
        own_wide[held] = own[:, :, lanes].astype(jnp.float32).reshape(-1, LANES)
        incoming_wide[held] = incoming[:, :, lanes].astype(jnp.float32).reshape(-1, LANES)
        for q, out in enumerate(outs):
            for i in range(group):
                image = (device[0] ^ q) * group + i
                first = own_wide[pl.ds(image, patches, stride=images), :]
                second = incoming_wide[pl.ds(place[image], patches, stride=images), :]
                joint[i * patches : (i + 1) * patches, :] = (
                    share[image] * first + (1 - share[image]) * second
                )
            out[:, lanes] = joint[: group * patches].astype(low)


def mix(place, share, device, own, incoming, groups):
    patches, images, width = own.shape
    rows = images // groups * patches
    scalar = pl.BlockSpec(memory_space=pltpu.SMEM)
    return pl.pallas_call(
        mix_kernel,
        in_specs=[scalar, scalar, scalar, pl.BlockSpec(), pl.BlockSpec()],
        out_shape=[jax.ShapeDtypeStruct((rows, width), low)] * groups,
        scratch_shapes=[
            pltpu.VMEM(((patches + SUBLANES) * images, LANES), jnp.float32),
            pltpu.VMEM(((patches + SUBLANES) * images, LANES), jnp.float32),
            pltpu.VMEM((rows + 2 * SUBLANES, LANES), jnp.float32),
        ],
        compiler_params=lean,
        cost_estimate=cost(4 * own.size, 6 * own.size),
        name="mix",
    )(place, share, device, own, incoming)


def stem_kernel(device, spots, *rest):
    sources, (blocks, gains, mixed, state, joint, spare, pieces, weights, piece_sems, sems) = rest[:-10], rest[-10:]
    piece_copies = [
        pltpu.make_async_copy(source, pieces.at[k], piece_sems.at[k]) for k, source in enumerate(sources)
    ]
    copies = block_copies(spots, blocks, pl.ds(0, weights.shape[1]), weights, sems)
    for copy in piece_copies + copies:
        copy.start()
    count = len(sources) // 2
    odd, upper = (device[0] & 1) == 1, (device[0] & 2) == 2
    patches = pieces.shape[1] // 2
    rows = mixed.shape[0] // (2 * 2)
    joint[...] = jnp.zeros_like(joint)
    for copy in piece_copies:
        copy.wait()
    for side in range(2):
        arrived = [pieces[side * count + k].astype(jnp.float32) for k in range(count)]
        arrived = [jnp.where(odd, arrived[k ^ 1], arrived[k]) for k in range(count)]
        for k in range(count):
            spare[: 2 * patches] = jnp.where(upper, arrived[k ^ 2], arrived[k])
            for i in range(2):
                at = (side * 2 + i) * rows + k * patches
                joint[at : at + patches, :] = spare[i * patches : (i + 1) * patches, :]
    mixed[...] = joint[: mixed.shape[0]].astype(low)
    for copy in copies:
        copy.wait()
    state[...] = dot(mixed[...], weights[...], (1, 1)) + gains[0:1]


def stem(device, spots, pieces, blocks, gains, rows):
    width, pixels = blocks.shape[0] * blocks.shape[1], pieces[0].shape[1]
    return pl.pallas_call(
        stem_kernel,
        in_specs=[scalars, scalars] + hbm(pieces) + hbm([blocks]) + [pl.BlockSpec()],
        out_shape=[
            jax.ShapeDtypeStruct((rows, pixels), low),
            jax.ShapeDtypeStruct((rows, width), jnp.float32),
        ],
        scratch_shapes=[
            pltpu.VMEM((rows + 2 * SUBLANES, pixels), jnp.float32),
            pltpu.VMEM((pieces[0].shape[0] + 2 * SUBLANES, pixels), jnp.float32),
            pltpu.VMEM((len(pieces), *pieces[0].shape), low),
            pltpu.VMEM((width, pixels), low),
            pltpu.SemaphoreType.DMA((len(pieces),)),
            pltpu.SemaphoreType.DMA((blocks.shape[0],)),
        ],
        compiler_params=large,
        cost_estimate=cost(2 * rows * width * pixels, 12 * rows * width),
        name="stem",
    )(device, spots, *pieces, blocks, gains)


def head_kernel(
    patches, pixels, device, spots, state, gains, blocks, bias, numbers, labels, others, lam, weight, scale,
    gradient, grad_vectors, grads, grad_bias, loss, pooled, upstream, head, sems,
):
    copies = block_copies(spots, blocks, pl.ds(pixels, head.shape[1]), head, sems)
    for copy in copies:
        copy.start()
    rows, width = state.shape
    count = lam.shape[0]
    each = rows // count
    live = lax.broadcasted_iota(jnp.int32, (each, 1), 0) < patches
    hat, inverse = centred(state[...])
    pooled[...] = jnp.zeros_like(pooled)
    sums = []
    for i in range(count):
        sums.append(jnp.sum(jnp.where(live, hat[i * each : (i + 1) * each], 0.0), 0, keepdims=True))
        pooled[i : i + 1] = sums[i] / patches * gains[0:1] + gains[1:2]
    pooled_low = pooled[...].astype(low)
    for copy in copies:
        copy.wait()
    logits = dot(pooled_low, head[...])[:count] + bias[...]
    logits = jnp.where(numbers[...] >= 0, logits, -jnp.inf)
    peak = jnp.max(logits, -1, keepdims=True)
    powers = jnp.exp(logits - peak)
    mass = jnp.sum(powers, -1, keepdims=True)
    targets = jnp.where(numbers[...] == labels[...], lam[...], 0.0) + jnp.where(
        numbers[...] == others[...], 1 - lam[...], 0.0
    )
    log_probs = jnp.where(numbers[...] >= 0, logits - peak - jnp.log(mass), 0.0)
    losses = -jnp.sum(targets * log_probs, -1, keepdims=True)
    loss[...] = jnp.sum(weight[...] * losses, 0, keepdims=True)
    grad_logits = scale[...] * (powers / mass * jnp.sum(targets, -1, keepdims=True) - targets)
    grad_bias[...] = jnp.sum(grad_logits, 0, keepdims=True)
    pad = jnp.zeros((pooled.shape[0] - count, grad_logits.shape[1]), jnp.float32)
    grad_logits = jnp.concatenate([grad_logits, pad], 0)
    main = grad_logits.astype(low)
    rest = (grad_logits - main.astype(jnp.float32)).astype(low)
    size = main.shape[1] // 4
    for a in range(4):
        lanes = slice(a * size, (a + 1) * size)
        part = dot(pooled_low, main[:, lanes], (0, 0)) + dot(pooled_low, rest[:, lanes], (0, 0))
        rel = device[0] ^ a
        grads[(rel & 1) * 2 + (rel >> 1)] = part.astype(low)
    spread_back = (dot(main, head[...], (1, 1)) + dot(rest, head[...], (1, 1))) / patches
    upstream[...] = jnp.zeros_like(upstream)
    grad_gain = jnp.zeros((1, width), jnp.float32)
    for i in range(count):
        one = spread_back[i : i + 1]
        grad_gain = grad_gain + one * sums[i]
        upstream[i * each : (i + 1) * each] = jnp.where(live, one, 0.0)
    grad_vectors[0:1] = grad_gain
    grad_vectors[1:2] = jnp.sum(spread_back[:count], 0, keepdims=True) * patches
    gradient[...] = centred_back(upstream[...] * gains[0:1], hat, inverse)


def head_step(device, spots, state, gains, blocks, bias, numbers, labels, others, lam, weight, scale, patches, pixels):
    rows, width = state.shape
    columns = bias.shape[1]
    return pl.pallas_call(
        functools.partial(head_kernel, patches, pixels),
        in_specs=[scalars, scalars] + [pl.BlockSpec()] * 2 + hbm([blocks]) + [pl.BlockSpec()] * 7,
        out_shape=[
            jax.ShapeDtypeStruct(state.shape, jnp.float32),
            jax.ShapeDtypeStruct((2, width), jnp.float32),
            jax.ShapeDtypeStruct((4, width, columns // 4), low),
            jax.ShapeDtypeStruct((1, columns), jnp.float32),
            jax.ShapeDtypeStruct((1, 1), jnp.float32),
        ],
        scratch_shapes=[
            pltpu.VMEM((16, width), jnp.float32),
            pltpu.VMEM(state.shape, jnp.float32),
            pltpu.VMEM((width, columns), low),
            pltpu.SemaphoreType.DMA((blocks.shape[0],)),
        ],
        compiler_params=lean,
        cost_estimate=cost(64 * width * columns, 8 * rows * width),
        name="head_step",
    )(device, spots, state, gains, blocks, bias, numbers, labels, others, lam, weight, scale)


def stem_backward_kernel(device, gradient, mixed, grads, shift):
    rounded = gradient[...].astype(low)
    shift[...] = jnp.sum(rounded.astype(jnp.float32), 0, keepdims=True)
    whole_grad = dot(gradient[...].T.astype(low), mixed[...]).astype(low)
    size = whole_grad.shape[1] // 4
    grads[...] = jnp.zeros_like(grads)
    for a in range(4):
        rel = device[0] ^ a
        grads[(rel & 1) * 2 + (rel >> 1), :, :size] = whole_grad[:, a * size : (a + 1) * size]


def stem_backward(device, gradient, mixed):
    width, pixels = gradient.shape[1], mixed.shape[1]
    return pl.pallas_call(
        stem_backward_kernel,
        in_specs=[scalars] + [pl.BlockSpec()] * 2,
        out_shape=[
            jax.ShapeDtypeStruct((4, width, MISC), low),
            jax.ShapeDtypeStruct((1, width), jnp.float32),
        ],
        compiler_params=lean,
        cost_estimate=cost(2 * gradient.size * pixels, 8 * gradient.size),
        name="stem_backward",
    )(device, gradient, mixed)


def moved(values, source, way):
    spots = (lax.broadcasted_iota(jnp.int32, (values.shape[1],) * 2, 0) == source).astype(low)
    main = values.astype(low)
    rest = values - main.astype(jnp.float32)
    middle = rest.astype(low)
    rest = (rest - middle.astype(jnp.float32)).astype(low)
    return sum(dot(part, spots, (1, way)) for part in (main, middle, rest))


def vectors_kernel(vectors, source, out):
    out[...] = moved(vectors[...], source[...], 0)


def relative_vectors(vectors, source):
    return pl.pallas_call(
        vectors_kernel,
        out_shape=jax.ShapeDtypeStruct(vectors.shape, jnp.float32),
        compiler_params=lean,
        name="relative_vectors",
    )(vectors, source)


def gather_misc_kernel(count, source, stem_grads, *rest):
    tokens, parts, (bias, loss), outs, (joint, small) = (
        rest[:4],
        rest[4:count],
        rest[count : count + 2],
        [rest[count + 2 + place // 2].at[place % 2] for place in range(4)],
        rest[count + 4 :],
    )
    joint[...] = jnp.zeros_like(joint)
    at = 0
    for part in parts:
        joint[at : at + part.shape[0]] = part[...]
        at += part.shape[0]
    true = moved(joint[:16], source[...], 1)
    small[...] = jnp.zeros_like(small)
    for j in range(joint.shape[1] // MISC):
        small[j * 16 : (j + 1) * 16] = true[:, j * MISC : (j + 1) * MISC]
    at = joint.shape[1] // MISC * 16
    for j in range(bias.shape[1] // MISC):
        small[at + j : at + j + 1] = bias[:, j * MISC : (j + 1) * MISC]
    at += bias.shape[1] // MISC
    small[at : at + 1, 0:1] = loss[...]
    stem_rows = stem_grads.shape[1]
    rows = tokens[0].shape[0] // 4
    patches = tokens[0].shape[1]
    for place, out in enumerate(outs):
        out[:stem_rows] = stem_grads[place]
        for j, token in enumerate(tokens):
            at = stem_rows + j * rows
            out[at : at + rows] = jnp.zeros((rows, MISC), low)
            out[at : at + rows, :patches] = token[place * rows : (place + 1) * rows].astype(low)
        out[stem_rows + 4 * rows :] = small[...].astype(low)


def gather_misc(source, stem_grads, tokens, parts, bias, loss):
    rows = stem_grads.shape[1] + tokens[0].shape[0] + SMALL
    return pl.pallas_call(
        functools.partial(gather_misc_kernel, 4 + len(parts)),
        out_shape=[jax.ShapeDtypeStruct((2, rows, MISC), low)] * 2,
        scratch_shapes=[
            pltpu.VMEM((32, parts[0].shape[1]), jnp.float32),
            pltpu.VMEM((SMALL, MISC), jnp.float32),
        ],
        compiler_params=lean,
        name="gather_misc",
    )(source, stem_grads, *tokens, *parts, bias, loss)


def swap(array, axis, mask):
    count = lax.axis_size(axis)
    return lax.ppermute(array, axis, [(i, i ^ mask) for i in range(count)])


def fence(*trees):
    return lax.optimization_barrier(trees)


def dp_masks():
    masks = []
    mask = lax.axis_size("dp") // 2
    while mask > 1:
        masks.append(mask)
        mask //= 2
    return masks


def row_order():
    order = [0]
    for mask in dp_masks() + [1]:
        order = order + [r ^ mask for r in order]
    return order


def packed(blocks):
    return jnp.concatenate(blocks, 0)


def unpacked(array, blocks):
    out = []
    at = 0
    for block in blocks:
        out.append(lax.slice_in_dim(array, at, at + block.shape[0], axis=0))
        at += block.shape[0]
    return out


def doubled(blocks, got):
    return [jnp.concatenate(pair, 0) for pair in zip(blocks, unpacked(got, blocks), strict=True)]


def added(keep, got):
    return (keep.astype(jnp.float32) + got.astype(jnp.float32)).astype(keep.dtype)


def cut_rows(array, half):
    middle = array.shape[-2] // 2
    return array[..., half * middle : (half + 1) * middle, :]


def folded(keep, got, kind):
    if kind == "rows":
        return [added(cut_rows(keep, half), cut_rows(got, half)) for half in range(2)]
    if kind == "blocks":
        return [added(keep[0], got[0]), added(keep[1], got[1])]
    if isinstance(kind, int):
        total = added(keep, got)
        return [
            jnp.concatenate([total[: kind // 2], total[kind:]]),
            jnp.concatenate([total[kind // 2 : kind], total[kind:]]),
        ]
    if kind == "turned":
        return [jnp.stack([added(keep[0], got[1]), added(keep[1], got[0])])]
    return [added(keep, got)]


def fold_kernel(jobs, *refs):
    refs = list(refs)
    values = [jax.tree.map(lambda _: refs.pop(0)[...], job[:2]) for job in jobs]
    for (keep, got), (_, _, kind) in zip(values, jobs, strict=True):
        for value in folded(keep, got, kind):
            refs.pop(0)[...] = value


def fold_all(jobs):
    arrays = jax.tree.leaves([job[:2] for job in jobs])
    shapes = [jax.eval_shape(functools.partial(folded, kind=kind), keep, got) for keep, got, kind in jobs]
    flat = [shape for group in shapes for shape in group]
    blank = [(*jax.tree.map(lambda _: 0, job[:2]), job[2]) for job in jobs]
    outs = pl.pallas_call(
        functools.partial(fold_kernel, blank),
        out_shape=flat,
        compiler_params=lean,
        cost_estimate=cost(sum(a.size for a in arrays), sum(4 * a.size for a in arrays)),
        name="fold_all",
    )(*arrays)
    out = []
    for group in shapes:
        out.append(outs[: len(group)])
        outs = outs[len(group) :]
    return out


def split_kernel(*refs):
    further = len(refs) > 10
    keep_low, keep_high, keep_out, got_low, got_high, got_out = refs[:6]
    in_keep, in_send, out_keep, out_send = refs[-4:]
    columns = keep_out.shape[3]
    in_keep[...] = added(keep_low[0], got_low[0])
    in_send[...] = added(keep_high[0], got_high[0])
    for half, out in enumerate((out_keep, out_send)):
        out[:, :columns] = added(keep_out[0, half], got_out[0, half])
        if further:
            out[:, columns:] = added(refs[6][half], refs[7][half])


def split_cores(keep, got, further=(), steps=4):
    rows, columns = keep.shape[2:]
    few, many = rows // 2 // steps, rows // steps
    low_rows = pl.BlockSpec((1, 2, few, columns), lambda i: (0, 0, i, 0))
    high_rows = pl.BlockSpec((1, 2, few, columns), lambda i: (0, 0, i + steps, 0))
    out_rows = pl.BlockSpec((1, 2, many, columns), lambda i: (1, 0, i, 0))
    total = columns + (further[0].shape[2] if further else 0)
    two = pl.BlockSpec((2, few, columns), lambda i: (0, i, 0))
    one = pl.BlockSpec((many, total), lambda i: (i, 0))
    pair = jax.ShapeDtypeStruct((2, rows // 2, columns), keep.dtype)
    single = jax.ShapeDtypeStruct((rows, total), keep.dtype)
    return pl.pallas_call(
        split_kernel,
        grid=(steps,),
        in_specs=[low_rows, high_rows, out_rows] * 2
        + [pl.BlockSpec((2, many, total - columns), lambda i: (0, i, 0))] * len(further),
        out_specs=[two, two, one, one],
        out_shape=[pair, pair, single, single],
        compiler_params=large,
        cost_estimate=cost(keep.size, 6 * keep.size),
        name="split_cores",
    )(keep, keep, keep, got, got, got, *further)


def reduce_rows(keep, send):
    steps = [1] + dp_masks()[::-1]
    for mask in steps[:-1]:
        keep, send = yield keep, swap(send, "dp", mask), "rows"
    (keep,) = yield keep, swap(send, "dp", steps[-1]), "sum"
    (keep,) = yield keep, swap(keep, "tok", 2), "turned"
    near, far = yield keep, swap(keep, "tok", 1), "none"
    return near, far


def reduce_columns(keep, send):
    keep, send = yield keep, swap(send, "tok", 2), "rows"
    steps = [1] + dp_masks()[::-1]
    for mask in steps[:-1]:
        keep, send = yield keep, swap(send, "dp", mask), "rows"
    (keep,) = yield keep, swap(send, "dp", steps[-1]), "sum"
    keep, others = yield keep, [swap(keep, "tok", q) for q in range(1, 4)], "none"
    return [keep, *others]


def reduce_misc(stem_rows, keep, send):
    keep, send = yield keep, swap(send, "tok", 2), stem_rows
    steps = [1] + dp_masks()[::-1]
    for mask in steps[:-1]:
        stem_rows //= 2
        keep, send = yield keep, swap(send, "dp", mask), stem_rows
    (keep,) = yield keep, swap(send, "dp", steps[-1]), "sum"
    block = keep[: stem_rows // 2]
    rest, others = yield keep, [swap(block, "tok", q) for q in range(1, 4)], "none"
    return [block, *others], rest[stem_rows // 2 :]


def sum_over(array, steps):
    for axis, mask in steps:
        (array,) = yield array, swap(array, axis, mask), "sum"
    return array


class Chain:
    def __init__(self, moves):
        self.moves, self.result = moves, None
        self.state = next(moves)

    def push(self, state):
        try:
            self.state = self.moves.send(state)
        except StopIteration as end:
            self.state, self.result = None, end.value


def advance(chains, *others):
    chains = [chain for chain in chains if chain.state is not None]
    states, others = fence([chain.state[:2] for chain in chains], others)
    jobs = []
    for chain, (keep, got) in zip(chains, states, strict=True):
        kind = chain.state[2]
        small = keep.size <= FOLD_MAX and kind != "none"
        if (kind == "rows" and keep.shape[-2] % 32) or (isinstance(kind, int) and kind % 32):
            small = False
        if small:
            jobs.append((chain, keep, got, kind))
    results = dict(
        zip([id(job[0]) for job in jobs], fold_all([job[1:] for job in jobs]) if jobs else [], strict=True)
    )
    others, fenced = fence(others, results)
    results = fenced
    for chain, (keep, got) in zip(chains, states, strict=True):
        kind = chain.state[2]
        if id(chain) in results:
            chain.push(results[id(chain)])
        elif kind == "none":
            chain.push((keep, got))
        else:
            chain.push(folded(keep, got, kind))
    return others


def exchanged(blocks):
    row = lax.axis_index("tok")
    blocks = [jnp.where((row & 1) == 1, blocks[k ^ 1], blocks[k]) for k in range(4)]
    return [jnp.where((row & 2) == 2, blocks[k ^ 2], blocks[k]) for k in range(4)]


def ordered(blocks, axis):
    return jnp.concatenate(exchanged([blocks[0], blocks[2], blocks[1], blocks[3]]), axis)


def quarter(array, axis):
    size = array.shape[axis] // lax.axis_size("tok")
    return lax.dynamic_slice_in_dim(array, lax.axis_index("tok") * size, size, axis)


def moments(weight, gradient, first, second, decay_rate):
    first_new = beta_one * first + (1 - beta_one) * gradient
    second_new = beta_two * second + (1 - beta_two) * gradient * gradient
    scale_one, scale_two = 1 / (1 - beta_one**STEP), 1 / (1 - beta_two**STEP)
    update = scale_one * first_new / (jnp.sqrt(scale_two * second_new) + epsilon) + decay_rate * weight
    return (first_new, second_new, update)


def row_squares(array, groups):
    flat = array.reshape(groups, -1)
    return jnp.sum(flat * flat, 1)


def renew(weight, update, weight_norm, update_norm, groups):
    trust = weight_norm / (update_norm + epsilon)
    return weight - learn_rate * (trust[:, None] * update.reshape(groups, -1)).reshape(weight.shape)


def body(
    images,
    partner,
    lam,
    labels,
    counts,
    class_weights,
    stem_w,
    stem_m,
    stem_v,
    tok_w,
    tok_m,
    tok_v,
    chan_w,
    chan_m,
    chan_v,
    head_w,
    head_m,
    head_v,
    vec_w,
    vec_m,
    vec_v,
    hb_w,
    hb_m,
    hb_v,
):
    count_dp = lax.axis_size("dp")
    count_tok = lax.axis_size("tok")
    device_row = lax.axis_index("dp")
    token_row = lax.axis_index("tok")
    patches = images.shape[0]
    all_patches = patches * count_tok
    per_device = images.shape[1]
    per_tok = per_device // count_tok
    classes_all = hb_w.shape[0]
    class_pad = -classes_all % (count_tok * LANES)
    width = vec_w.shape[1]
    each = all_patches + -all_patches % SUBLANES

    masks = dp_masks()
    batches = per_device // IMG_MB
    start = device_row * per_device
    own_parts, owners, shares = [], [], []
    for batch in range(batches):
        at = start + batch * IMG_MB
        own_parts.append(images[:, batch * IMG_MB : (batch + 1) * IMG_MB])
        owners.append(lax.dynamic_slice_in_dim(partner, at, IMG_MB, 0) % IMG_MB)
        shares.append(lax.dynamic_slice_in_dim(lam, at, IMG_MB, 0))
    device = token_row.astype(jnp.int32)[None]

    def mixed_pieces(batch, incoming):
        sends = mix(owners[batch], shares[batch], device, own_parts[batch], incoming, count_tok)
        return [sends[0]] + [swap(sends[q], "tok", q) for q in range(1, count_tok)]

    chan_low = quarter(chan_w.astype(low), 3)
    shard, size = chan_low.shape[2:]
    order = row_order()
    rows = jnp.asarray(order, jnp.int32) ^ device_row
    column_source = (rows[:, None] * shard + jnp.arange(shard, dtype=jnp.int32)[None, :]).reshape(1, width)
    ends = jnp.concatenate([stem_w.astype(low).T, jnp.pad(head_w.astype(low), ((0, 0), (0, class_pad)))], 1)
    ends = lax.all_gather(quarter(ends, 0), ("dp", "tok"))
    pixels = stem_w.shape[0]
    later = chan_low[1].reshape(2 * shard, size)

    later = lax.all_gather(later, ("dp", "tok")).reshape(count_dp, count_tok, -1, size)

    vectors = relative_vectors(vec_w, column_source)
    numbers = jnp.arange(classes_all + class_pad, dtype=jnp.int32)
    numbers = jnp.where(numbers < classes_all, numbers, -1)[None]
    bias = jnp.pad(hb_w, (0, class_pad))[None]
    own_hot = (labels[:, None] == jnp.arange(classes_all, dtype=jnp.int32)[None, :]).astype(jnp.float32)
    other_labels = jnp.take(labels, partner)
    own_weight = jnp.sum(own_hot * class_weights[None, :], 1)
    other_weight = jnp.take(own_weight, partner)
    live = (
        (jnp.arange(IMG_MB, dtype=jnp.int32)[None, :] < counts.reshape(-1)[:, None])
        .astype(jnp.float32)
        .reshape(-1)
    )
    weights = live * (lam * own_weight + (1 - lam) * other_weight)
    total = jnp.sum(weights)
    group = IMG_MB // count_tok

    def row_of(array):
        return jnp.concatenate(
            [
                lax.dynamic_slice_in_dim(array, start + batch * IMG_MB + token_row * group, group, 0)
                for batch in range(batches)
            ]
        )[:, None]

    image_rows = [row_of(array) for array in (labels, other_labels, lam, weights, weights / total)]

    blocks = [chan_low[0, 0], chan_low[0, 1]]
    tok_low = jnp.swapaxes(tok_w, 2, 3).astype(low)
    partner_mask = count_dp // 2
    for step, mask in enumerate(masks):
        got = swap(packed(blocks), "dp", mask)
        if step == 0:
            blocks, got, tok_low, tok_far, own_parts = fence(
                blocks, got, tok_low, swap(tok_low, "tok", 2), own_parts
            )
            incoming = swap(own_parts[0], "dp", partner_mask)
            tok_half = jnp.concatenate([tok_low, tok_far], 2)
            tok_near = swap(tok_half, "tok", 1)
        elif step == 1:
            blocks, got, vectors, image_rows, own_parts, incoming, tok_half, tok_near = fence(
                blocks, got, vectors, image_rows, own_parts, incoming, tok_half, tok_near
            )
            incoming_two = swap(own_parts[1], "dp", partner_mask)
            pieces = mixed_pieces(0, incoming)
        else:
            blocks, got = fence(blocks, got)
        blocks = doubled(blocks, got)
    tok_turn = jnp.concatenate([tok_half, tok_near], 2)
    tok_turn = jnp.pad(tok_turn, ((0, 0), (0, 0), (0, 0), (0, each - all_patches)))
    token_turn = [[tok_turn[layer, way] for way in range(2)] for layer in range(LAYERS)]
    token_all = [[array.T for array in pair] for pair in token_turn]

    first, second = blocks
    first_low, second_far = swap(first, "dp", 1), swap(second, "tok", 2)
    first, second, first_low, second_far, incoming_two, pieces, token_all, token_turn = fence(
        first, second, first_low, second_far, incoming_two, pieces, token_all, token_turn
    )
    more = mixed_pieces(1, incoming_two)
    firsts, seconds = jnp.stack([first, first_low]), jnp.stack([second, second_far])
    firsts_far, seconds_low = swap(firsts, "tok", 2), swap(seconds, "dp", 1)
    firsts, seconds, firsts_far, seconds_low, more = fence(firsts, seconds, firsts_far, seconds_low, more)
    source_zero = Pieces(
        [firsts, firsts_far, swap(firsts, "tok", 1), swap(firsts_far, "tok", 1)],
        [seconds, seconds_low, swap(seconds, "tok", 1), swap(seconds_low, "tok", 1)],
    )
    if shard % 16:
        many = 96 // shard
        groups = count_dp // many
        later = jnp.take(later, rows, axis=0).reshape(groups, many, count_tok, 2, shard, size)
        later = later.transpose(0, 2, 3, 1, 4, 5).reshape(groups, count_tok, 2 * many * shard, size)
        ends = jnp.take(ends.reshape(count_dp, shard, -1), rows, axis=0).reshape(groups, many * shard, -1)
        spots = jnp.arange(groups, dtype=jnp.int32)
        source_one = Gathered(later, spots, device, many * shard)
    else:
        spots = rows
        ends = ends.reshape(count_dp, shard, -1)
        source_one = Gathered(later, spots, device, shard)

    gains = [vectors[1 + 4 * layer : 5 + 4 * layer] for layer in range(LAYERS)]
    mixed, stem_state = stem(device, spots, pieces + more, ends, vectors, each * per_tok)
    middle_zero, before_zero = token_forward(stem_state, gains[0], token_turn[0][0], token_all[0][1])
    first_state, inner_zero = channel_forward(middle_zero, gains[0], source_zero)
    middle_one, before_one = token_forward(first_state, gains[1], token_turn[1][0], token_all[1][1])
    second_state, inner_one = channel_forward(middle_one, gains[1], source_one)
    gradient, last_part, head_grads, bias_part, loss_local = head_step(
        device, spots, second_state, vectors[NV - 2 :], ends, bias, numbers, *image_rows, all_patches, pixels
    )

    head_got = swap(head_grads[2:], "tok", 1)
    send, partial, _ = channel_backward(gradient, middle_one, gains[1], inner_one, source_one)
    got = swap(send, "tok", 1)
    keep, gradient, second_one = channel_backward(gradient, middle_one, gains[1], inner_one, source_one, partial)
    in_keep, in_send, out_keep, out_send = split_cores(keep, got, (head_grads[:2], head_got))
    in_keep, in_send, out_keep, out_send, gradient = fence(in_keep, in_send, out_keep, out_send, gradient)
    chains_one = [Chain(reduce_rows(in_keep, in_send)), Chain(reduce_columns(out_keep, out_send))]
    gradient, first_one, *token_one = token_backward(
        gradient, first_state, gains[1], before_one, token_all[1][0], token_turn[1][1]
    )
    send, partial, _ = channel_backward(gradient, middle_zero, gains[0], inner_zero, source_zero)
    send, partial, gradient = advance(chains_one, send, partial, gradient)
    got = swap(send, "tok", 1)
    keep, gradient, second_zero = channel_backward(gradient, middle_zero, gains[0], inner_zero, source_zero, partial)
    in_keep, in_send, out_keep, out_send = split_cores(keep, got)
    in_keep, in_send, out_keep, out_send, gradient = advance(
        chains_one, in_keep, in_send, out_keep, out_send, gradient
    )
    chains_zero = [Chain(reduce_rows(in_keep, in_send)), Chain(reduce_columns(out_keep, out_send))]
    gradient, first_zero, *token_zero = token_backward(
        gradient, stem_state, gains[0], before_zero, token_all[0][0], token_turn[0][1]
    )
    stem_grads, stem_bias = stem_backward(device, gradient, mixed)
    misc = gather_misc(
        column_source,
        stem_grads,
        token_zero + token_one,
        [stem_bias, first_zero, second_zero, first_one, second_one, last_part],
        bias_part,
        loss_local,
    )
    misc = advance(chains_one + chains_zero, *misc)
    ((misc_keep, misc_send),) = fold_all([(misc[0], swap(misc[1], "tok", 1), "blocks")])
    misc_chain = Chain(reduce_misc(width, misc_keep, misc_send))
    dp_steps = [("dp", mask) for mask in [1] + dp_masks()[::-1]]
    everything = chains_one + chains_zero + [misc_chain]
    earlier = []
    while any(chain.state is not None for chain in everything):
        if not earlier and all(chain.result is not None for chain in chains_one):
            *earlier, squares_one = channel_step(
                1, device, chan_w, chan_m, chan_v, *[chain.result for chain in chains_one], []
            )
            earlier = list(advance(everything, *earlier))
        else:
            advance(everything)
    chan_first, chan_second, chan_update, squares_zero = channel_step(
        0, device, chan_w, chan_m, chan_v, *[chain.result for chain in chains_zero], earlier
    )
    stem_parts, misc = misc_chain.result
    hidden = tok_w.shape[3]
    token_grad = misc[: 4 * hidden].reshape(LAYERS, 2, hidden, MISC)[..., :all_patches].astype(jnp.float32)
    small = misc[4 * hidden :].astype(jnp.float32)
    blocks = width // MISC
    vector_grad = jnp.concatenate([small[16 * j : 16 * j + NV] for j in range(blocks)], 1)
    bias_grad = small[16 * blocks : 16 * blocks + numbers.shape[1] // MISC].reshape(-1)[:classes_all]
    loss_total = small[16 * blocks + numbers.shape[1] // MISC, 0]
    turned = lambda array: jnp.swapaxes(array, -1, -2)
    tok_w, tok_m, tok_v, stem_w, stem_m, stem_v = [turned(a) for a in (tok_w, tok_m, tok_v, stem_w, stem_m, stem_v)]
    stem_first, stem_second, stem_update, head_first, head_second, head_update, shard_squares = ends_step(
        device,
        (squares_zero, squares_one),
        (stem_w, stem_m, stem_v),
        (head_w, head_m, head_v),
        stem_parts,
        chains_one[1].result,
    )
    tok_first, tok_second, tok_update = moments(tok_w, token_grad, tok_m, tok_v, weight_decay)
    vec_first, vec_second, vec_update = moments(vec_w, vector_grad, vec_m, vec_v, 0.0)
    hb_first, hb_second, hb_update = moments(hb_w, bias_grad, hb_m, hb_v, 0.0)
    matrix_groups = 2 * LAYERS
    pair_of = lambda array, other, groups: jnp.stack([row_squares(array, groups), row_squares(other, groups)])
    token_squares = pair_of(tok_w, tok_update, matrix_groups)
    token_squares = token_squares + swap(token_squares, "tok", 1)
    at = 1
    while at < count_dp:
        if 4 * at <= count_dp:
            one, two, three = [swap(shard_squares, "dp", k * at) for k in (1, 2, 3)]
            shard_squares = (shard_squares + one) + (two + three)
            at *= 4
        else:
            shard_squares = shard_squares + swap(shard_squares, "dp", at)
            at *= 2
    last = 2 + matrix_groups
    token_squares, shard_squares = fence(token_squares, shard_squares)
    token_squares = token_squares + swap(token_squares, "tok", 2)
    weight_total, update_total = jnp.concatenate(
        [shard_squares[:2, :1], token_squares, shard_squares[:2, 1:last]], 1
    )
    weight_norms = jnp.sqrt(weight_total)
    update_norms = jnp.sqrt(update_total)
    stem_end = 1
    tok_end = 1 + matrix_groups
    chan_end = 1 + 2 * matrix_groups
    stem_new = renew(stem_w, stem_update, weight_norms[0:stem_end], update_norms[0:stem_end], 1)
    tok_new = renew(
        tok_w,
        tok_update,
        weight_norms[stem_end:tok_end],
        update_norms[stem_end:tok_end],
        matrix_groups,
    )
    chan_new, chan_new_low = channel_renew(shard_squares, chan_w, chan_update)
    head_new = renew(head_w, head_update, weight_norms[chan_end:], update_norms[chan_end:], 1)
    vec_weight_norm = jnp.sqrt(row_squares(vec_w, NV))
    vec_update_norm = jnp.sqrt(row_squares(vec_update, NV))
    hb_weight_norm = jnp.sqrt(row_squares(hb_w, 1))
    hb_update_norm = jnp.sqrt(row_squares(hb_update, 1))
    vec_new = renew(vec_w, vec_update, vec_weight_norm, vec_update_norm, NV)
    hb_new = renew(hb_w, hb_update, hb_weight_norm, hb_update_norm, 1)
    stem_new, stem_first, stem_second, tok_new, tok_first, tok_second = [
        turned(a) for a in (stem_new, stem_first, stem_second, tok_new, tok_first, tok_second)
    ]
    norms = jnp.stack(
        [
            jnp.concatenate([weight_norms, vec_weight_norm, hb_weight_norm]),
            jnp.concatenate([update_norms, vec_update_norm, hb_update_norm]),
        ],
        1,
    )
    loss_parts = jnp.stack([loss_total, total])
    return (
        stem_new,
        stem_first,
        stem_second,
        tok_new,
        tok_first,
        tok_second,
        chan_new,
        chan_first,
        chan_second,
        head_new,
        head_first,
        head_second,
        vec_new,
        vec_first,
        vec_second,
        hb_new,
        hb_first,
        hb_second,
        stem_new.astype(jnp.bfloat16),
        tok_new.astype(jnp.bfloat16),
        chan_new_low,
        head_new.astype(jnp.bfloat16),
        norms,
        loss_parts,
    )


def solution(mesh):
    in_specs = (
        P("tok", "dp", None),
        P(),
        P(),
        P(),
        P(),
        P(),
        P(None, "dp"),
        P(None, "dp"),
        P(None, "dp"),
        P(None, None, None, "tok"),
        P(None, None, None, "tok"),
        P(None, None, None, "tok"),
        P(None, None, "dp", None),
        P(None, None, "dp", None),
        P(None, None, "dp", None),
        P("dp", None),
        P("dp", None),
        P("dp", None),
        P(),
        P(),
        P(),
        P(),
        P(),
        P(),
    )
    out_specs = (
        P(None, "dp"),
        P(None, "dp"),
        P(None, "dp"),
        P(None, None, None, "tok"),
        P(None, None, None, "tok"),
        P(None, None, None, "tok"),
        P(None, None, "dp", None),
        P(None, None, "dp", None),
        P(None, None, "dp", None),
        P("dp", None),
        P("dp", None),
        P("dp", None),
        P(),
        P(),
        P(),
        P(),
        P(),
        P(),
        P(None, "dp"),
        P(None, None, None, "tok"),
        P(None, None, "dp", None),
        P("dp", None),
        P(),
        P(),
    )
    return jax.shard_map(body, mesh=mesh, in_specs=in_specs, out_specs=out_specs, check_vma=False)
```
